32 devices in a mesh: wide: 16 (over z, y, core), narrow: 2 (over x).
Axes of the slice: x: 2, y: 2, z: 4, core: 2. Of those that a mesh axis runs over, the one named last changes fastest.
Arguments:
- target_input: bfloat16 [64, 128, 1024], P(('wide', 'narrow')), may hold values from -6 to 6
- memory: bfloat16 [64, 1024, 1024], P(('wide', 'narrow')), may hold values from -6 to 6
- cotangent: bfloat16 [64, 128, 1024], P(('wide', 'narrow')), may hold values from -6 to 6
- mem_lengths: int32 [64], P(('wide', 'narrow')), may hold values from 300 to 1024, as said below
- tgt_lengths: int32 [64], P(('wide', 'narrow')), may hold values from 32 to 128, as said below
- self_qkv: bfloat16 [1024, 3072], P(('wide', 'narrow')), may hold values from -0.1875 to 0.1875
- self_out: bfloat16 [1024, 1024], P(('wide', 'narrow')), may hold values from -0.75 to 0.75
- self_bias: bfloat16 [3, 1024], P(None, ('wide', 'narrow')), may hold values from -3 to 3
- norm1_gain: bfloat16 [1024], P(('wide', 'narrow')), may hold values from 0.5 to 1.5
- norm1_shift: bfloat16 [1024], P(('wide', 'narrow')), may hold values from -3 to 3
- cross_qkv: bfloat16 [1024, 3072], P(('wide', 'narrow')), may hold values from -0.1875 to 0.1875
- cross_out: bfloat16 [1024, 1024], P(('wide', 'narrow')), may hold values from -3 to 3
- cross_bias: bfloat16 [3, 1024], P(None, ('wide', 'narrow')), may hold values from -3 to 3
- norm2_gain: bfloat16 [1024], P(('wide', 'narrow')), may hold values from 0.5 to 1.5
- norm2_shift: bfloat16 [1024], P(('wide', 'narrow')), may hold values from -3 to 3
- ffn_up: bfloat16 [1024, 4096], P(('wide', 'narrow')), may hold values from -0.1875 to 0.1875
- up_bias: bfloat16 [4096], P(('wide', 'narrow')), may hold values from -3 to 3
- ffn_down: bfloat16 [4096, 1024], P(('wide', 'narrow')), may hold values from -0.09375 to 0.09375
- down_bias: bfloat16 [1024], P(('wide', 'narrow')), may hold values from -3 to 3
- norm3_gain: bfloat16 [1024], P(('wide', 'narrow')), may hold values from 0.5 to 1.5
- norm3_shift: bfloat16 [1024], P(('wide', 'narrow')), may hold values from -3 to 3
Outputs:
- block_out: bfloat16 [64, 128, 1024], P(('wide', 'narrow'))
- target_grad: bfloat16 [64, 128, 1024], P(('wide', 'narrow'))
- memory_grad: bfloat16 [64, 1024, 1024], P(('wide', 'narrow'))
- self_qkv_grad: float32 [1024, 3072], P(('wide', 'narrow'))
- self_out_grad: float32 [1024, 1024], P(('wide', 'narrow'))
- self_bias_grad: float32 [3, 1024], P(None, ('wide', 'narrow'))
- norm1_gain_grad: float32 [1024], P(('wide', 'narrow'))
- norm1_shift_grad: float32 [1024], P(('wide', 'narrow'))
- cross_qkv_grad: float32 [1024, 3072], P(('wide', 'narrow'))
- cross_out_grad: float32 [1024, 1024], P(('wide', 'narrow'))
- cross_bias_grad: float32 [3, 1024], P(None, ('wide', 'narrow'))
- norm2_gain_grad: float32 [1024], P(('wide', 'narrow'))
- norm2_shift_grad: float32 [1024], P(('wide', 'narrow'))
- ffn_up_grad: float32 [1024, 4096], P(('wide', 'narrow'))
- up_bias_grad: float32 [4096], P(('wide', 'narrow'))
- ffn_down_grad: float32 [4096, 1024], P(('wide', 'narrow'))
- down_bias_grad: float32 [1024], P(('wide', 'narrow'))
- norm3_gain_grad: float32 [1024], P(('wide', 'narrow'))
- norm3_shift_grad: float32 [1024], P(('wide', 'narrow'))
The draws below stay inside these ranges and needn't reach their ends.
Inputs may be any that keep to these rules, and one draw needn't show every extreme that they name: `mem_lengths`: at least one table has 1024 live positions. `tgt_lengths`: at least one sample has 128 live target positions.
All inputs are finite; a program needn't handle non-finite values.
Results may differ from the reference program's by a relative error of at most 0.02.
Values may be sent and summed in bfloat16 or wider, within the bound.
A program may use at most 256 MiB of HBM per device.

```python
import math
import jax
import jax.numpy as jnp
from jax import lax

D = 1024
H = 16
HD = 64
FF = 4096
TGT_LEN = 128
MEM_LEN = 1024
SAMPLES = 64


def ragged_lengths(key, longest, shortest):
    key_values, key_choice = jax.random.split(key)
    lengths_drawn = jax.random.randint(key_values, (SAMPLES,), shortest, longest + 1)
    chosen = jax.random.randint(key_choice, (), 0, SAMPLES)
    return jnp.where(jnp.arange(SAMPLES) == chosen, longest, lengths_drawn).astype(jnp.int32)


def draw_mem_lengths(key, part):
    key = jax.random.fold_in(key, 7)
    return ragged_lengths(key, MEM_LEN, max(1, MEM_LEN * 300 // 1024))


def draw_tgt_lengths(key, part):
    key = jax.random.fold_in(key, 8)
    return ragged_lengths(key, TGT_LEN, max(1, TGT_LEN // 4))


def spiked(values, key, source, target, shards_of, factor):
    def block_of(axis_at):
        return (jnp.arange(values.shape[axis_at]) // (values.shape[axis_at] // shards_of)).reshape((-1,) + (1,) * (values.ndim - 1 - axis_at))

    first = jax.random.permutation(key, shards_of)[block_of(target)]
    far = (block_of(target) + shards_of // 2) % shards_of
    return jnp.where((block_of(source) == first) | (block_of(source) == far), factor * values, values)


def block_scale(stream_key, shape, cuts, smallest, largest):
    factor_of = 1.0
    for dim, parts in cuts:
        steps = jax.random.uniform(jax.random.fold_in(jax.random.fold_in(stream_key, 6), dim), (parts,), jnp.float32, smallest / len(cuts), largest / len(cuts))
        factor_of = factor_of * jnp.repeat(jnp.exp(steps), shape[dim] // parts).reshape((-1,) + (1,) * (len(shape) - 1 - dim))
    return factor_of


def noise(stream_key, shape, deviation, limit, shards=(), dtype=jnp.bfloat16):
    values = deviation * jax.random.normal(stream_key, shape, jnp.float32)
    if shards:
        values = values * block_scale(stream_key, shape, shards, -0.22, 0.18)
    return jnp.clip(values, -limit, limit).astype(dtype)


def bell_draw_with(stream_key, dims, spread, most, pieces, heavy, kind=jnp.bfloat16):
    values = spread * jax.random.normal(stream_key, dims, jnp.float32)
    if pieces:
        values = values * block_scale(stream_key, dims, pieces, -0.22, 0.18)
    return jnp.clip(spiked(values, jax.random.fold_in(stream_key, 3), *heavy), -most, most).astype(kind)


def setup_inputs(seed: int = 0) -> dict:
    arg_keys = jax.random.split(jax.random.key(seed), 22)
    return {
        "target_input": noise(arg_keys[0], (SAMPLES, TGT_LEN, D), 1.0, 6.0, ((0, 32),)),
        "memory": noise(arg_keys[1], (SAMPLES, MEM_LEN, D), 1.0, 6.0, ((0, 32),)),
        "cotangent": bell_draw_with(arg_keys[2], (SAMPLES, TGT_LEN, D), 1.0, 6.0, ((0, 32),), (0, 2, 32, 2.75)),
        "mem_lengths": draw_mem_lengths(jax.random.fold_in(arg_keys[21], 71), 0),
        "tgt_lengths": draw_tgt_lengths(jax.random.fold_in(arg_keys[21], 71), 0),
        "self_qkv": noise(arg_keys[5], (D, 3 * D), D ** -0.5, 0.1875, ((0, 32),)),
        "self_out": noise(arg_keys[6], (D, D), (max(1, 8 * D // TGT_LEN)) ** -0.5, 0.75, ((0, 32),)),
        "self_bias": noise(arg_keys[7], (3, D), 0.5, 3.0, ((1, 32),)),
        "norm1_gain": jnp.clip(1.0 + 0.1 * jax.random.normal(arg_keys[8], (D,), jnp.float32), 0.5, 1.5).astype(jnp.bfloat16),
        "norm1_shift": noise(arg_keys[9], (D,), 0.5, 3.0, ((0, 32),)),
        "cross_qkv": noise(arg_keys[10], (D, 3 * D), D ** -0.5, 0.1875, ((0, 32),)),
        "cross_out": noise(arg_keys[11], (D, D), (max(1, 4 * D // MEM_LEN)) ** -0.5, 3.0, ((0, 32),)),
        "cross_bias": noise(arg_keys[12], (3, D), 0.5, 3.0, ((1, 32),)),
        "norm2_gain": jnp.clip(1.0 + 0.1 * jax.random.normal(arg_keys[13], (D,), jnp.float32), 0.5, 1.5).astype(jnp.bfloat16),
        "norm2_shift": noise(arg_keys[14], (D,), 0.5, 3.0, ((0, 32),)),
        "ffn_up": noise(arg_keys[15], (D, FF), D ** -0.5, 0.1875, ((0, 32),)),
        "up_bias": noise(arg_keys[16], (FF,), 0.5, 3.0, ((0, 32),)),
        "ffn_down": noise(arg_keys[17], (FF, D), FF ** -0.5, 0.09375, ((0, 32),)),
        "down_bias": noise(arg_keys[18], (D,), 0.5, 3.0, ((0, 32),)),
        "norm3_gain": jnp.clip(1.0 + 0.1 * jax.random.normal(arg_keys[19], (D,), jnp.float32), 0.5, 1.5).astype(jnp.bfloat16),
        "norm3_shift": noise(arg_keys[20], (D,), 0.5, 3.0, ((0, 32),)),
    }


HIGHEST_PRECISION = lax.Precision.HIGHEST
MASK_VALUE = -1e+30

@jax.custom_vjp
def low(v):
    return lax.optimization_barrier(v.astype(jnp.bfloat16)).astype(jnp.float32)

@jax.custom_vjp
def low_back(v):
    return v

def low_keep(v):
    return (low(v), None)

def low_pass(kept, grad):
    return (grad,)

def back_keep(v):
    return (v, None)

def back_low(kept, grad):
    return (low(grad),)
low.defvjp(low_keep, low_pass)
low_back.defvjp(back_keep, back_low)

def project(rows_in, matrix):
    return jnp.einsum('gtd,de->gte', rows_in, matrix, precision=HIGHEST_PRECISION)

def layer_norm(summed, norm_gain, norm_shift):
    average = lax.optimization_barrier(jnp.mean(summed, axis=-1, keepdims=True))
    centred = summed - average
    return centred * lax.rsqrt(lax.optimization_barrier(jnp.mean(centred * centred, axis=-1, keepdims=True)) + 1e-05) * norm_gain + norm_shift

def attention(queries, key_rows, values, usable):
    scores = low_back(jnp.einsum('gqhe,gkhe->ghqk', queries, key_rows, precision=HIGHEST_PRECISION))
    scores = jnp.where(usable[:, None], scores, MASK_VALUE)
    row_peak = lax.optimization_barrier(jnp.max(scores, axis=-1, keepdims=True))
    exponentials = jnp.exp(scores - row_peak)
    attn_probs = low(exponentials / lax.optimization_barrier(jnp.sum(exponentials, axis=-1, keepdims=True)))
    return jnp.einsum('ghqk,gkhe->gqhe', attn_probs, values, precision=HIGHEST_PRECISION)

def forward(weights, inputs, memory_rows, mem_group, tgt_group):
    self_qkv, self_out, self_bias, norm1_gain, norm1_shift, cross_qkv, cross_out, cross_bias, norm2_gain, norm2_shift, ffn_up, up_bias, ffn_down, down_bias, norm3_gain, norm3_shift = weights
    group_size, tgt_len, model_width = inputs.shape
    mem_len = memory_rows.shape[1]
    score_scale = 1.0 / math.sqrt(HD)
    head_shape = (group_size, tgt_len, H, HD)
    mem_head_shape = (group_size, mem_len, H, HD)
    positions = jnp.arange(tgt_len)
    self_usable = (positions[None, None, :] <= positions[None, :, None]) & (positions[None, None, :] < tgt_group[:, None, None])
    cross_usable = jnp.arange(mem_len)[None, None, :] < mem_group[:, None, None]
    projected = project(inputs, self_qkv)
    self_q = low(low_back(projected[..., :model_width] + self_bias[0]) * score_scale).reshape(head_shape)
    self_k = low(low_back(projected[..., model_width:2 * model_width])).reshape(head_shape)
    self_v = low(low_back(projected[..., 2 * model_width:] + self_bias[1])).reshape(head_shape)
    self_mixed = attention(self_q, self_k, self_v, self_usable).reshape(group_size, tgt_len, model_width)
    self_attn = low(low_back(self_mixed))
    self_branch = low_back(project(self_attn, self_out) + self_bias[2])
    hidden_one = layer_norm(inputs + self_branch, norm1_gain, norm1_shift)
    hidden_one_low = low(hidden_one)
    cross_q = low(low_back(project(hidden_one_low, cross_qkv[:, :model_width]) + cross_bias[0]) * score_scale).reshape(head_shape)
    memory_kv = project(memory_rows, cross_qkv[:, model_width:])
    cross_k = low(low_back(memory_kv[..., :model_width])).reshape(mem_head_shape)
    cross_v = low(low_back(memory_kv[..., model_width:] + cross_bias[1])).reshape(mem_head_shape)
    cross_mixed = attention(cross_q, cross_k, cross_v, cross_usable).reshape(group_size, tgt_len, model_width)
    cross_attn = low(low_back(cross_mixed))
    cross_branch = low_back(project(cross_attn, cross_out) + cross_bias[2])
    hidden_two = layer_norm(hidden_one + cross_branch, norm2_gain, norm2_shift)
    hidden_two_low = low(hidden_two)
    pre_act = low_back(project(hidden_two_low, ffn_up) + up_bias)
    act_low = low(jax.nn.gelu(pre_act, approximate=False))
    ffn_branch = low_back(project(act_low, ffn_down) + down_bias)
    return layer_norm(hidden_two + ffn_branch, norm3_gain, norm3_shift)

def reference(target_input, memory, cotangent, mem_lengths, tgt_lengths, self_qkv, self_out, self_bias, norm1_gain, norm1_shift, cross_qkv, cross_out, cross_bias, norm2_gain, norm2_shift, ffn_up, up_bias, ffn_down, down_bias, norm3_gain, norm3_shift):
    params = tuple((weight.astype(jnp.float32) for weight in (self_qkv, self_out, self_bias, norm1_gain, norm1_shift, cross_qkv, cross_out, cross_bias, norm2_gain, norm2_shift, ffn_up, up_bias, ffn_down, down_bias, norm3_gain, norm3_shift)))
    group_size = 4
    group_count = target_input.shape[0] // group_size

    def regroup(array):
        return array.reshape((group_count, group_size) + array.shape[1:])
    stacked = (regroup(target_input.astype(jnp.float32)), regroup(memory.astype(jnp.float32)), regroup(cotangent.astype(jnp.float32)), regroup(mem_lengths), regroup(tgt_lengths))

    def step_group(totals_now, group_item):
        inputs, memory_rows, upstream, mem_group, tgt_group = group_item

        def local_forward(weights, input_rows, memory_part):
            return forward(weights, input_rows, memory_part, mem_group, tgt_group)
        result, pullback = jax.vjp(local_forward, params, inputs, memory_rows)
        weight_grads, input_grad, memory_part_grad = pullback(upstream)
        totals_next = jax.tree.map(jnp.add, totals_now, weight_grads)
        return (totals_next, (result.astype(jnp.bfloat16), input_grad.astype(jnp.bfloat16), memory_part_grad.astype(jnp.bfloat16)))
    zero_totals = jax.tree.map(jnp.zeros_like, params)
    totals, (outputs, input_grads, memory_grads) = lax.scan(step_group, zero_totals, stacked)

    def flatten(array):
        return array.reshape((group_count * group_size,) + array.shape[2:])
    return (flatten(outputs), flatten(input_grads), flatten(memory_grads), totals[0], totals[1], totals[2], totals[3], totals[4], totals[5], totals[6], totals[7], totals[8], totals[9], totals[10], totals[11], totals[12], totals[13], totals[14], totals[15])
```

```python
import functools
import math

import jax
import jax.numpy as jnp
from jax import lax
from jax.experimental import pallas as pl
from jax.experimental.pallas import tpu as pltpu
from jax.sharding import PartitionSpec as P

MESH = pl.DeviceIdType.MESH
AXES = ("wide", "narrow")
LANE_CHUNK = 1024


def places(far_count):
    wide = lax.axis_index("wide")
    x = lax.axis_index("narrow")
    far = wide // 4
    y = (wide // 2) % 2
    core = wide % 2
    near_y = y + core * (1 - 2 * y)
    near_x = x + (1 - core) * (1 - 2 * x)
    other_y = y + (1 - core) * (1 - 2 * y)
    other_x = x + core * (1 - 2 * x)

    def device(f, yy, cc, xx):
        return (f * 4 + yy * 2 + cc, xx)

    return dict(
        far=far,
        y=y,
        core=core,
        x=x,
        near=(near_y, near_x),
        other=(other_y, other_x),
        diagonal=(1 - y, 1 - x),
        near_device=device(far, near_y, core, near_x),
        other_device=device(far, other_y, core, other_x),
        twin_device=device(far, y, 1 - core, x),
        far_devices=[
            (lax.rem(far + d, far_count), device(lax.rem(far + d, far_count), y, core, x))
            for d in range(1, far_count)
        ],
    )


def greet(where):
    barrier = pltpu.get_barrier_semaphore()
    partners = [where["near_device"], where["other_device"], where["twin_device"]]
    partners += [device for _, device in where["far_devices"]]
    for device in partners:
        pl.semaphore_signal(barrier, inc=1, device_id=device, device_id_type=MESH)
    pl.semaphore_wait(barrier, len(partners))


def remote(src, dst, send_sem, recv_sem, device):
    return pltpu.make_async_remote_copy(
        src_ref=src,
        dst_ref=dst,
        send_sem=send_sem,
        recv_sem=recv_sem,
        device_id=device,
        device_id_type=MESH,
    )


def gather_kernel(far_count, chunks, n_arrays, skew, *refs):
    ins, outs = refs[:n_arrays], refs[n_arrays : 2 * n_arrays]
    local_sem, send_sem, recv_sem = refs[2 * n_arrays :]
    me = places(far_count)
    far, y, core, x = me["far"], me["y"], me["core"], me["x"]
    far_all = pl.ds(0, far_count)

    def block(ref, k, *lead):
        _, row, rows, col, cols = chunks[k]
        return ref.at[(*lead, pl.ds(row, rows), pl.ds(col, cols))]

    def own(k):
        return block(ins[chunks[k][0]], k)

    def at(k, *lead):
        return block(outs[chunks[k][0]], k, *lead)

    local = []
    for a in range(n_arrays):
        copy = pltpu.make_async_copy(ins[a], outs[a].at[far, y, core, x], local_sem.at[a])
        copy.start()
        local.append(copy)
    greet(me)

    sent = []

    def go(copy):
        copy.start()
        sent.append(copy)
        return copy

    far_copies, near_copies, other_copies, pass_copies, twin_copies = {}, {}, {}, {}, {}
    lanes = far_count - 1

    def start_far(k):
        far_copies[k] = [
            go(
                remote(
                    own(k),
                    at(k, far, y, core, x),
                    send_sem.at[k, d],
                    recv_sem.at[k, d],
                    device,
                )
            )
            for d, (_, device) in enumerate(me["far_devices"])
        ]

    def start_near(k):
        column = at(k, far_all, y, core, x)
        near_copies[k] = go(
            remote(column, column, send_sem.at[k, lanes], recv_sem.at[k, lanes], me["near_device"])
        )
        other_copies[k] = go(
            remote(
                column, column, send_sem.at[k, lanes + 1], recv_sem.at[k, lanes + 1], me["other_device"]
            )
        )

    def start_pass(k):
        column = at(k, far_all, me["near"][0], core, me["near"][1])
        pass_copies[k] = go(
            remote(
                column, column, send_sem.at[k, lanes + 2], recv_sem.at[k, lanes + 2], me["other_device"]
            )
        )

    def start_twin(k):
        half = at(k, far_all, pl.ds(0, 2), core, pl.ds(0, 2))
        twin_copies[k] = go(
            remote(half, half, send_sem.at[k, lanes + 3], recv_sem.at[k, lanes + 3], me["twin_device"])
        )

    count = len(chunks)
    for t in range(count + 3 * skew):
        k = t - 3 * skew
        if 0 <= k < count:
            other_copies[k].wait_recv()
            pass_copies[k].wait_recv()
            start_twin(k)
        k = t - 2 * skew
        if 0 <= k < count:
            near_copies[k].wait_recv()
            start_pass(k)
        k = t - skew
        if 0 <= k < count:
            if k == 0:
                for copy in local:
                    copy.wait()
            for copy in far_copies[k]:
                copy.wait_recv()
            start_near(k)
        if t < count:
            start_far(t)
    for k in range(count):
        twin_copies[k].wait_recv()
    for copy in sent:
        copy.wait_send()


def gather_all(mesh, shards, chunks, skew, collective_id):
    far_count = mesh.shape["wide"] // 4
    n = len(shards)
    outs = [
        jax.ShapeDtypeStruct((far_count, 2, 2, 2) + s.shape, s.dtype) for s in shards
    ]
    lanes = far_count + 3
    return pl.pallas_call(
        functools.partial(gather_kernel, far_count, chunks, n, skew),
        out_shape=outs,
        in_specs=[pl.BlockSpec(memory_space=pl.ANY)] * n,
        out_specs=[pl.BlockSpec(memory_space=pl.ANY)] * n,
        scratch_shapes=[
            pltpu.SemaphoreType.DMA((n,)),
            pltpu.SemaphoreType.DMA((len(chunks), lanes)),
            pltpu.SemaphoreType.DMA((len(chunks), lanes)),
        ],
        compiler_params=pltpu.CompilerParams(collective_id=collective_id, has_side_effects=True),
        name="gather_params",
    )(*shards)


def scatter_kernel(far_count, chunks, n_arrays, skew, *refs):
    ins, outs = refs[:n_arrays], refs[n_arrays : 2 * n_arrays]
    (mine, from_twin, from_other, from_near, from_far, mine_s, twin_s, other_s, near_s, far_s,
     local_sem, send_sem, recv_sem) = refs[2 * n_arrays :]
    me = places(far_count)
    far, y, core, x = me["far"], me["y"], me["core"], me["x"]
    far_all = pl.ds(0, far_count)
    small = len(chunks) - 1
    slots = mine.shape[0]

    def buffers(k):
        if k == small:
            return mine_s, twin_s, other_s, near_s, far_s
        return mine.at[k % slots], from_twin.at[k], from_other.at[k], from_near.at[k], from_far.at[k]

    def half(k, c):
        a, row, rows, col, cols = chunks[k]
        return ins[a].at[far_all, pl.ds(0, 2), c, pl.ds(0, 2), pl.ds(row, rows), pl.ds(col, cols)]

    sent, loads, twins, others, nears, fars = [], {}, {}, {}, {}, {}

    def go(copy):
        copy.start()
        sent.append(copy)
        return copy

    def start_load(k):
        loads[k] = pltpu.make_async_copy(half(k, core), buffers(k)[0], local_sem.at[k])
        loads[k].start()

    def start_twin(k):
        twins[k] = go(
            remote(half(k, 1 - core), buffers(k)[1], send_sem.at[k, 0], recv_sem.at[k, 0], me["twin_device"])
        )

    def add_mine(k):
        own, total = buffers(k)[:2]

        def body(i, carry):
            f, yy, xx = i // 4, (i // 2) % 2, i % 2
            total[f, yy, xx] = total[f, yy, xx] + own[f, yy, xx]
            return carry

        lax.fori_loop(0, far_count * 4, body, 0)

    def start_other(k):
        total, landing = buffers(k)[1:3]
        others[k] = [
            go(
                remote(
                    total.at[far_all, place[0], place[1]],
                    landing.at[i],
                    send_sem.at[k, 1 + i],
                    recv_sem.at[k, 1 + i],
                    me["other_device"],
                )
            )
            for i, place in enumerate((me["diagonal"], me["other"]))
        ]

    def add_other(k, i):
        total, landing = buffers(k)[1:3]
        place = (me["near"], (y, x))[i]

        def body(f, carry):
            total[f, place[0], place[1]] = total[f, place[0], place[1]] + landing[i, f]
            return carry

        lax.fori_loop(0, far_count, body, 0)

    def start_near(k):
        _, total, _, landing, _ = buffers(k)
        nears[k] = go(
            remote(
                total.at[far_all, me["near"][0], me["near"][1]],
                landing,
                send_sem.at[k, 3],
                recv_sem.at[k, 3],
                me["near_device"],
            )
        )

    def add_near(k):
        _, total, _, landing, _ = buffers(k)

        def body(f, carry):
            total[f, y, x] = total[f, y, x] + landing[f]
            return carry

        lax.fori_loop(0, far_count, body, 0)

    def start_far(k):
        _, total, _, _, landing = buffers(k)
        fars[k] = [
            go(
                remote(
                    total.at[target, y, x],
                    landing.at[d],
                    send_sem.at[k, 4 + d],
                    recv_sem.at[k, 4 + d],
                    device,
                )
            )
            for d, (target, device) in enumerate(me["far_devices"])
        ]

    def finish(k):
        _, total, _, _, landing = buffers(k)
        a, row, rows, col, cols = chunks[k]
        result = total[far, y, x].astype(jnp.float32)
        for d in range(far_count - 1):
            result += landing[d].astype(jnp.float32)
        outs[a][pl.ds(row, rows), pl.ds(col, cols)] = result

    count = len(chunks)
    start_load(0)
    greet(me)
    for t in range(count + 4 * skew):
        k = t - 4 * skew
        if 0 <= k < count:
            for copy in fars[k]:
                copy.wait_recv()
            finish(k)
        k = t - 3 * skew
        if 0 <= k < count:
            nears[k].wait_recv()
            add_near(k)
            start_far(k)
        k = t - 2 * skew
        if 0 <= k < count:
            others[k][0].wait_recv()
            add_other(k, 0)
            start_near(k)
            others[k][1].wait_recv()
            add_other(k, 1)
        k = t - skew
        if 0 <= k < count:
            loads[k].wait()
            twins[k].wait_recv()
            add_mine(k)
            start_other(k)
        if t < count:
            start_twin(t)
            if t + 1 < count:
                start_load(t + 1)
    for copy in sent:
        copy.wait_send()


def scatter_all(mesh, grads, chunks, skew, collective_id):
    far_count = mesh.shape["wide"] // 4
    n = len(grads)
    main = len(chunks) - 1
    rows, cols = chunks[0][2], chunks[0][4]
    small_shape = grads[-1].shape[4:]
    low = grads[0].dtype
    slots = skew + 2
    lanes = far_count + 3
    return pl.pallas_call(
        functools.partial(scatter_kernel, far_count, chunks, n, skew),
        out_shape=[jax.ShapeDtypeStruct(g.shape[4:], jnp.float32) for g in grads],
        in_specs=[pl.BlockSpec(memory_space=pl.ANY)] * n,
        out_specs=[pl.BlockSpec(memory_space=pltpu.VMEM)] * n,
        scratch_shapes=[
            pltpu.VMEM((slots, far_count, 2, 2, rows, cols), low),
            pltpu.VMEM((main, far_count, 2, 2, rows, cols), low),
            pltpu.VMEM((main, 2, far_count, rows, cols), low),
            pltpu.VMEM((main, far_count, rows, cols), low),
            pltpu.VMEM((main, far_count - 1, rows, cols), low),
            pltpu.VMEM((far_count, 2, 2) + small_shape, jnp.float32),
            pltpu.VMEM((far_count, 2, 2) + small_shape, jnp.float32),
            pltpu.VMEM((2, far_count) + small_shape, jnp.float32),
            pltpu.VMEM((far_count,) + small_shape, jnp.float32),
            pltpu.VMEM((far_count - 1,) + small_shape, jnp.float32),
            pltpu.SemaphoreType.DMA((main + 1,)),
            pltpu.SemaphoreType.DMA((main + 1, lanes)),
            pltpu.SemaphoreType.DMA((main + 1, lanes)),
        ],
        compiler_params=pltpu.CompilerParams(
            collective_id=collective_id, has_side_effects=True, vmem_limit_bytes=60 * 2**20
        ),
        name="scatter_grads",
    )(*grads)


def chunk_list(shapes):
    rows = shapes[0][0]
    chunks = []
    for a, (all_rows, all_cols) in enumerate(shapes[:-1]):
        for row in range(0, all_rows, rows):
            for col in range(0, all_cols, LANE_CHUNK):
                chunks.append((a, row, rows, col, LANE_CHUNK))
    last = shapes[-1]
    chunks.append((len(shapes) - 1, 0, last[0], 0, last[1]))
    return chunks

GATHER_SKEW = 1
SCATTER_SKEW = 1


def small_widths(per_device, up_rows):
    return [
        3 * per_device, per_device, per_device, 3 * per_device, per_device, per_device,
        up_rows, per_device, per_device, per_device,
    ]


H = 16
HD = 64


NORM_EPSILON = 1e-05
MASK_VALUE = -1e30


def column_products(left_side, right_side):
    return lax.dot_general(
        left_side, right_side, (((0,), (0,)), ((), ())), preferred_element_type=jnp.float32
    )


def times_transpose(left_side, right_side):
    return lax.dot_general(
        left_side, right_side, (((1,), (1,)), ((), ())), preferred_element_type=jnp.float32
    )


def row_sums(values):
    return jnp.sum(values.astype(jnp.float32), axis=0)


def norm_forward(summed, norm_gain, norm_shift):
    average = jnp.mean(summed, axis=-1, keepdims=True)
    centred = summed - average
    inverse = lax.rsqrt(jnp.mean(centred * centred, axis=-1, keepdims=True) + NORM_EPSILON)
    normed = centred * inverse
    return (normed * norm_gain + norm_shift, normed, inverse)


def norm_backward(incoming, normed, inverse, norm_gain):
    gain_grad = jnp.sum(incoming * normed, axis=0)
    shift_grad = jnp.sum(incoming, axis=0)
    scaled = incoming * norm_gain
    centred_grad = (
        scaled
        - jnp.mean(scaled, axis=-1, keepdims=True)
        - normed * jnp.mean(scaled * normed, axis=-1, keepdims=True)
    )
    return (centred_grad * inverse, gain_grad, shift_grad)


def gelu_parts(pre_act):
    normal_cdf = 0.5 * (1.0 + lax.erf(pre_act * (1.0 / math.sqrt(2.0))))
    density = jnp.exp(-0.5 * pre_act * pre_act) * (1.0 / math.sqrt(2.0 * math.pi))
    return (pre_act * normal_cdf, normal_cdf + pre_act * density)


def masked_scores(queries, key_rows, usable):
    scores = jnp.einsum("sqhe,skhe->shqk", queries, key_rows, preferred_element_type=jnp.float32)
    return jnp.where(usable[:, None], scores, MASK_VALUE)


def attend(queries, key_rows, values, usable):
    scores = masked_scores(queries, key_rows, usable)
    row_peak = jnp.max(scores, axis=-1, keepdims=True)
    exponentials = jnp.exp(scores - row_peak)
    row_total = jnp.sum(exponentials, axis=-1, keepdims=True)
    probs_low = (exponentials / row_total).astype(jnp.bfloat16)
    mixed_heads = jnp.einsum(
        "shqk,skhe->sqhe", probs_low, values, preferred_element_type=jnp.float32
    )
    return (mixed_heads, row_peak + jnp.log(row_total))


def attend_back(queries, key_rows, values, usable, log_totals, upstream):
    attn_probs = jnp.exp(masked_scores(queries, key_rows, usable) - log_totals)
    probs_low = attn_probs.astype(jnp.bfloat16)
    prob_grad = jnp.einsum("sqhe,skhe->shqk", upstream, values, preferred_element_type=jnp.float32)
    row_delta = jnp.sum(attn_probs * prob_grad, axis=-1, keepdims=True)
    score_grad = (attn_probs * (prob_grad - row_delta)).astype(jnp.bfloat16)
    query_grad = jnp.einsum(
        "shqk,skhe->sqhe", score_grad, key_rows, preferred_element_type=jnp.float32
    )
    key_grad = jnp.einsum(
        "shqk,sqhe->skhe", score_grad, queries, preferred_element_type=jnp.float32
    )
    value_grad = jnp.einsum(
        "shqk,sqhe->skhe", probs_low, upstream, preferred_element_type=jnp.float32
    )
    return (query_grad, key_grad, value_grad)


def shards(
    mesh,
    target_input,
    memory,
    cotangent,
    mem_lengths,
    tgt_lengths,
    self_qkv,
    self_out,
    self_bias,
    norm1_gain,
    norm1_shift,
    cross_qkv,
    cross_out,
    cross_bias,
    norm2_gain,
    norm2_shift,
    ffn_up,
    up_bias,
    ffn_down,
    down_bias,
    norm3_gain,
    norm3_shift,
):
    samples_dev, tgt_len, model_width = target_input.shape
    mem_len = memory.shape[1]
    score_scale = 1.0 / math.sqrt(HD)
    tgt_rows = samples_dev * tgt_len
    mem_rows = samples_dev * mem_len
    head_shape = (samples_dev, tgt_len, H, HD)
    mem_head_shape = (samples_dev, mem_len, H, HD)
    inputs_flat = target_input.reshape(tgt_rows, model_width)
    memory_flat = memory.reshape(mem_rows, model_width)
    positions = jnp.arange(tgt_len)
    self_usable = (positions[None, None, :] <= positions[None, :, None]) & (
        positions[None, None, :] < tgt_lengths[:, None, None]
    )
    cross_usable = jnp.arange(mem_len)[None, None, :] < mem_lengths[:, None, None]
    widths = small_widths(model_width // mesh.size, up_bias.shape[0])
    smalls = [
        self_bias, norm1_gain, norm1_shift, cross_bias, norm2_gain, norm2_shift,
        up_bias, down_bias, norm3_gain, norm3_shift,
    ]
    small = jnp.concatenate([v.reshape(-1) for v in smalls])
    small = jnp.pad(small, (0, 2048 - small.shape[0])).reshape(16, 128)
    arrays = [self_qkv, self_out, cross_qkv, cross_out, ffn_up, ffn_down, small]
    chunks = chunk_list([v.shape for v in arrays])
    gathered = gather_all(mesh, arrays, chunks[-1:] + chunks[:-1], GATHER_SKEW, 0)
    qkv_weight, out_weight, cross_in, cross_proj, up_weight, down_weight = [
        v.reshape(-1, v.shape[-1]) for v in gathered[:-1]
    ]
    small_all = gathered[-1].reshape(mesh.size, 2048)
    taken, at = [], 0
    for v, width in zip(smalls, widths):
        part = small_all[:, at : at + width]
        if v.ndim == 2:
            part = part.reshape(mesh.size, 3, width // 3).transpose(1, 0, 2).reshape(3, -1)
        else:
            part = part.reshape(-1)
        taken.append(part)
        at += width
    (self_rows, gain_one, shift_one, cross_rows, gain_two, shift_two,
     up_shift, down_shift, gain_three, shift_three) = taken
    self_shift = self_rows.astype(jnp.float32)
    projected = jnp.dot(inputs_flat, qkv_weight, preferred_element_type=jnp.float32)
    self_q = (
        ((projected[:, :model_width] + self_shift[0]) * score_scale)
        .astype(jnp.bfloat16)
        .reshape(head_shape)
    )
    self_k = projected[:, model_width : 2 * model_width].astype(jnp.bfloat16).reshape(head_shape)
    self_v = (
        (projected[:, 2 * model_width :] + self_shift[1]).astype(jnp.bfloat16).reshape(head_shape)
    )
    self_mixed, self_logsum = attend(self_q, self_k, self_v, self_usable)
    self_attn = self_mixed.reshape(tgt_rows, model_width).astype(jnp.bfloat16)
    self_branch = jnp.dot(self_attn, out_weight, preferred_element_type=jnp.float32) + self_shift[2]
    hidden_one, normed_one, inverse_one = norm_forward(
        inputs_flat.astype(jnp.float32) + self_branch,
        gain_one.astype(jnp.float32),
        shift_one.astype(jnp.float32),
    )
    hidden_one_low = hidden_one.astype(jnp.bfloat16)
    cross_shift = cross_rows.astype(jnp.float32)
    cross_q = (
        (
            (
                jnp.dot(
                    hidden_one_low, cross_in[:, :model_width], preferred_element_type=jnp.float32
                )
                + cross_shift[0]
            )
            * score_scale
        )
        .astype(jnp.bfloat16)
        .reshape(head_shape)
    )
    memory_kv = jnp.dot(memory_flat, cross_in[:, model_width:], preferred_element_type=jnp.float32)
    cross_k = memory_kv[:, :model_width].astype(jnp.bfloat16).reshape(mem_head_shape)
    cross_v = (
        (memory_kv[:, model_width:] + cross_shift[1]).astype(jnp.bfloat16).reshape(mem_head_shape)
    )
    cross_mixed, cross_logsum = attend(cross_q, cross_k, cross_v, cross_usable)
    cross_attn = cross_mixed.reshape(tgt_rows, model_width).astype(jnp.bfloat16)
    cross_branch = (
        jnp.dot(cross_attn, cross_proj, preferred_element_type=jnp.float32) + cross_shift[2]
    )
    hidden_two, normed_two, inverse_two = norm_forward(
        hidden_one + cross_branch, gain_two.astype(jnp.float32), shift_two.astype(jnp.float32)
    )
    hidden_two_low = hidden_two.astype(jnp.bfloat16)
    pre_act = jnp.dot(
        hidden_two_low, up_weight, preferred_element_type=jnp.float32
    ) + up_shift.astype(jnp.float32)
    activated, gelu_slope = gelu_parts(pre_act)
    act_low = activated.astype(jnp.bfloat16)
    ffn_branch = jnp.dot(
        act_low, down_weight, preferred_element_type=jnp.float32
    ) + down_shift.astype(jnp.float32)
    result, normed_three, inverse_three = norm_forward(
        hidden_two + ffn_branch, gain_three.astype(jnp.float32), shift_three.astype(jnp.float32)
    )
    block_out = result.astype(jnp.bfloat16).reshape(samples_dev, tgt_len, model_width)
    upstream = cotangent.reshape(tgt_rows, model_width).astype(jnp.float32)
    d_sum3, gain3_grad, shift3_grad = norm_backward(
        upstream, normed_three, inverse_three, gain_three.astype(jnp.float32)
    )
    d_ffn = d_sum3.astype(jnp.bfloat16)
    down_grad = column_products(act_low, d_ffn)
    down_shift_grad = row_sums(d_ffn)
    d_pre = (times_transpose(d_ffn, down_weight) * gelu_slope).astype(jnp.bfloat16)
    up_grad = column_products(hidden_two_low, d_pre)
    up_shift_grad = row_sums(d_pre)
    d_hidden2 = d_sum3 + times_transpose(d_pre, up_weight)
    d_sum2, gain2_grad, shift2_grad = norm_backward(
        d_hidden2, normed_two, inverse_two, gain_two.astype(jnp.float32)
    )
    d_cross = d_sum2.astype(jnp.bfloat16)
    cross_proj_grad = column_products(cross_attn, d_cross)
    d_cross_attn = times_transpose(d_cross, cross_proj).astype(jnp.bfloat16).reshape(head_shape)
    cross_q_grad, cross_k_grad, cross_v_grad = attend_back(
        cross_q, cross_k, cross_v, cross_usable, cross_logsum, d_cross_attn
    )
    d_cross_q = (cross_q_grad * score_scale).astype(jnp.bfloat16).reshape(tgt_rows, model_width)
    d_cross_kv = jnp.concatenate(
        [cross_k_grad.reshape(mem_rows, model_width), cross_v_grad.reshape(mem_rows, model_width)],
        axis=1,
    ).astype(jnp.bfloat16)
    cross_in_grad = jnp.concatenate(
        [column_products(hidden_one_low, d_cross_q), column_products(memory_flat, d_cross_kv)],
        axis=1,
    )
    cross_shift_grad = jnp.stack(
        [row_sums(d_cross_q), row_sums(d_cross_kv[:, model_width:]), row_sums(d_cross)]
    )
    memory_grad = (
        times_transpose(d_cross_kv, cross_in[:, model_width:])
        .astype(jnp.bfloat16)
        .reshape(samples_dev, mem_len, model_width)
    )
    d_hidden1 = d_sum2 + times_transpose(d_cross_q, cross_in[:, :model_width])
    d_sum1, gain1_grad, shift1_grad = norm_backward(
        d_hidden1, normed_one, inverse_one, gain_one.astype(jnp.float32)
    )
    d_self = d_sum1.astype(jnp.bfloat16)
    self_out_part = column_products(self_attn, d_self)
    d_self_attn = times_transpose(d_self, out_weight).astype(jnp.bfloat16).reshape(head_shape)
    self_q_grad, self_k_grad, self_v_grad = attend_back(
        self_q, self_k, self_v, self_usable, self_logsum, d_self_attn
    )
    d_self_qkv = jnp.concatenate(
        [
            (self_q_grad * score_scale).reshape(tgt_rows, model_width),
            self_k_grad.reshape(tgt_rows, model_width),
            self_v_grad.reshape(tgt_rows, model_width),
        ],
        axis=1,
    ).astype(jnp.bfloat16)
    self_qkv_part = column_products(inputs_flat, d_self_qkv)
    self_shift_grad = jnp.stack(
        [
            row_sums(d_self_qkv[:, :model_width]),
            row_sums(d_self_qkv[:, 2 * model_width :]),
            row_sums(d_self),
        ]
    )
    target_grad = (
        (d_sum1 + times_transpose(d_self_qkv, qkv_weight))
        .astype(jnp.bfloat16)
        .reshape(samples_dev, tgt_len, model_width)
    )
    grads = [self_qkv_part, self_out_part, cross_in_grad, cross_proj_grad, up_grad, down_grad]
    sums = [
        self_shift_grad, gain1_grad, shift1_grad, cross_shift_grad, gain2_grad, shift2_grad,
        up_shift_grad, down_shift_grad, gain3_grad, shift3_grad,
    ]
    parts = []
    for v in sums:
        if v.ndim == 2:
            v = v.reshape(3, mesh.size, -1).transpose(1, 0, 2)
        parts.append(v.reshape(mesh.size, -1))
    packed = jnp.concatenate(parts, axis=1)
    packed = jnp.pad(packed, ((0, 0), (0, 1024 - packed.shape[1])))
    lead = (mesh.shape["wide"] // 4, 2, 2, 2)
    stacked = [
        g.astype(jnp.bfloat16).reshape(lead + (-1, g.shape[-1])) for g in grads
    ] + [packed.reshape(lead + (8, 128))]
    chunks = chunk_list([g.shape[4:] for g in stacked])
    reduced = scatter_all(mesh, stacked, chunks, SCATTER_SKEW, 1)
    small_sums = reduced[-1].reshape(-1)
    outs, at = [], 0
    for v, width in zip(sums, widths):
        part = small_sums[at : at + width]
        outs.append(part.reshape(3, -1) if v.ndim == 2 else part)
        at += width
    return (
        block_out, target_grad, memory_grad,
        reduced[0], reduced[1], outs[0], outs[1], outs[2],
        reduced[2], reduced[3], outs[3], outs[4], outs[5],
        reduced[4], outs[6], reduced[5], outs[7], outs[8], outs[9],
    )


def solution(mesh):
    return jax.shard_map(
        functools.partial(shards, mesh),
        mesh=mesh,
        in_specs=(
            P(("wide", "narrow"), None, None),
            P(("wide", "narrow"), None, None),
            P(("wide", "narrow"), None, None),
            P(("wide", "narrow")),
            P(("wide", "narrow")),
            P(("wide", "narrow"), None),
            P(("wide", "narrow"), None),
            P(None, ("wide", "narrow")),
            P(("wide", "narrow")),
            P(("wide", "narrow")),
            P(("wide", "narrow"), None),
            P(("wide", "narrow"), None),
            P(None, ("wide", "narrow")),
            P(("wide", "narrow")),
            P(("wide", "narrow")),
            P(("wide", "narrow"), None),
            P(("wide", "narrow")),
            P(("wide", "narrow"), None),
            P(("wide", "narrow")),
            P(("wide", "narrow")),
            P(("wide", "narrow")),
        ),
        out_specs=(
            P(("wide", "narrow"), None, None),
            P(("wide", "narrow"), None, None),
            P(("wide", "narrow"), None, None),
            P(("wide", "narrow"), None),
            P(("wide", "narrow"), None),
            P(None, ("wide", "narrow")),
            P(("wide", "narrow")),
            P(("wide", "narrow")),
            P(("wide", "narrow"), None),
            P(("wide", "narrow"), None),
            P(None, ("wide", "narrow")),
            P(("wide", "narrow")),
            P(("wide", "narrow")),
            P(("wide", "narrow"), None),
            P(("wide", "narrow")),
            P(("wide", "narrow"), None),
            P(("wide", "narrow")),
            P(("wide", "narrow")),
            P(("wide", "narrow")),
        ),
        check_vma=False,
    )
```

```python
import functools
import math

import jax
import jax.numpy as jnp
from jax import lax
from jax.experimental import pallas as pl
from jax.experimental.pallas import tpu as pltpu
from jax.sharding import PartitionSpec as P

MESH = pl.DeviceIdType.MESH
HEADS = 16
HEAD_DIM = 64
NORM_EPSILON = 1e-05
MASK_VALUE = -1e30
COLS = 512
GATHER_SKEW = 2
SCATTER_SKEW = 2
STEP_WORK = 2.5
SMALL_ROWS = 16

F32 = jnp.float32
BF16 = jnp.bfloat16

SELF_Q, SELF_V, SELF_O, GAIN1, SHIFT1, CROSS_Q, CROSS_V, CROSS_O, GAIN2, SHIFT2, DOWN, GAIN3, SHIFT3, UP = range(14)
VECTORS = 13


def dot(a, b):
    return lax.dot_general(a, b, (((1,), (0,)), ((), ())), preferred_element_type=F32)


def dot_nt(a, b):
    return lax.dot_general(a, b, (((1,), (1,)), ((), ())), preferred_element_type=F32)


def dot_tn(a, b):
    return lax.dot_general(a, b, (((0,), (0,)), ((), ())), preferred_element_type=F32)


def places(far_count):
    wide = lax.axis_index("wide")
    x = lax.axis_index("narrow")
    far = wide // 4
    y = (wide // 2) % 2
    core = wide % 2
    near_y = y + core * (1 - 2 * y)
    near_x = x + (1 - core) * (1 - 2 * x)
    other_y = y + (1 - core) * (1 - 2 * y)
    other_x = x + core * (1 - 2 * x)

    def device(f, yy, cc, xx):
        return (f * 4 + yy * 2 + cc, xx)

    return dict(
        far=far,
        y=y,
        core=core,
        x=x,
        near=(near_y, near_x),
        other=(other_y, other_x),
        diagonal=(1 - y, 1 - x),
        near_device=device(far, near_y, core, near_x),
        other_device=device(far, other_y, core, other_x),
        twin_device=device(far, y, 1 - core, x),
        far_devices=[
            (lax.rem(far + d, far_count), device(lax.rem(far + d, far_count), y, core, x))
            for d in range(1, far_count)
        ],
    )


def greet(where):
    barrier = pltpu.get_barrier_semaphore()
    partners = [where["near_device"], where["other_device"], where["twin_device"]]
    partners += [device for _, device in where["far_devices"]]
    for device in partners:
        pl.semaphore_signal(barrier, inc=1, device_id=device, device_id_type=MESH)
    pl.semaphore_wait(barrier, len(partners))


def remote(src, dst, send_sem, recv_sem, device):
    return pltpu.make_async_remote_copy(
        src_ref=src,
        dst_ref=dst,
        send_sem=send_sem,
        recv_sem=recv_sem,
        device_id=device,
        device_id_type=MESH,
    )


def matrix(value):
    rows, cols = value.shape[-2:]
    if rows % 16:
        return value.astype(F32).reshape(-1, cols).astype(BF16)
    return value.reshape(-1, cols)


ARRAYS = ("self_qkv", "self_out", "cross_qkv", "cross_out", "ffn_up", "ffn_down")
SQKV, SOUT, CQKV, COUT, FUP, FDOWN, SMALL = range(7)


def gather_chunks(shapes):
    rows = shapes[SQKV][0]
    width = shapes[SOUT][1]
    chunks = [(SMALL, 0, SMALL_ROWS, 0, 128)]
    for a, first, last in (
        (SQKV, 0, 3 * width),
        (SOUT, 0, width),
        (CQKV, width, 3 * width),
        (CQKV, 0, width),
        (COUT, 0, width),
        (FUP, 0, 4 * width),
    ):
        chunks += [(a, 0, rows, col, COLS) for col in range(first, last, COLS)]
    for col in range(0, width, COLS):
        chunks += [(FDOWN, row, rows, col, COLS) for row in range(0, 4 * rows, rows)]
    index = {(a, row, col): k for k, (a, row, _, col, _) in enumerate(chunks)}
    return chunks, index


def scatter_chunks(width):
    chunks = [(FDOWN, 128 * j) for j in range(width // 128)]
    for a, first, last in (
        (FUP, 0, 4 * width),
        (COUT, 0, width),
        (CQKV, 0, 3 * width),
        (SOUT, 0, width),
    ):
        chunks += [(a, col) for col in range(first, last, COLS)]
    chunks += [(SMALL, 0)]
    chunks += [(SQKV, col) for col in range(0, 3 * width, COLS)]
    return chunks


def layer_kernel(cfg, *refs):
    far_count, rows, width, samples, tgt_len, mem_len = cfg
    devices = 8 * far_count
    hidden = 4 * width
    down_rows = 4 * rows
    tokens = samples * tgt_len
    pairs = HEADS // 2
    scale = 1.0 / math.sqrt(HEAD_DIM)
    lanes = far_count + 3
    zs = max(1, far_count // 4)
    zh = max(1, far_count // 2)

    names = (
        "x", "mem_hbm", "cot_hbm", "mem_lengths", "tgt_lengths", "i0", "i1", "i2", "i3", "i4", "i5", "i6",
        "block_out", "target_grad", "memory_grad", "g0", "g1", "g2", "g3", "g4", "g5", "small_out", "w0", "w1",
        "w2", "w3", "w4", "w5", "mem", "cot", "qkv", "self_attn", "n1", "r1", "h1", "h1_low", "cross_q", "cross_k",
        "cross_v", "cross_attn", "n2", "r2", "flow", "h2_low", "act", "slope", "acc", "d_ffn", "d_cross", "d_attn",
        "d_self", "self_lse", "cross_lse", "vecs", "gvecs", "staged", "wbuf", "wquarter", "wgroup", "whalf",
        "small_in", "small_rows", "small_pack", "own", "total", "from_other", "from_near", "from_far", "total_s",
        "from_other_s", "from_near_s", "from_far_s", "load_sem", "in_sem", "local_sem", "gsend", "grecv", "ssend",
        "srecv", "stage_sem",
    )
    r = dict(zip(names, refs, strict=True))
    x_in, mem, cot = r["x"], r["mem"], r["cot"]
    qkv, self_attn, n1, r1, h1, h1_low = (r[n] for n in ("qkv", "self_attn", "n1", "r1", "h1", "h1_low"))
    cross_q, cross_k, cross_v, cross_attn = (r[n] for n in ("cross_q", "cross_k", "cross_v", "cross_attn"))
    n2, r2, flow, h2_low = (r[n] for n in ("n2", "r2", "flow", "h2_low"))
    act, slope, acc = (r[n] for n in ("act", "slope", "acc"))
    d_ffn, d_cross, d_attn, d_self = (r[n] for n in ("d_ffn", "d_cross", "d_attn", "d_self"))
    vecs, gvecs = r["vecs"], r["gvecs"]
    shards = [r["i%d" % i] for i in range(7)]
    whole = [r["w%d" % i] for i in range(6)] + [r["small_in"]]
    sums = [r["g%d" % i] for i in range(6)] + [r["small_out"]]

    me = places(far_count)
    far, y, core, x = me["far"], me["y"], me["core"], me["x"]
    far_all = pl.ds(0, far_count)
    near, other, diagonal = me["near"], me["other"], me["diagonal"]

    def vec(i, col=0, cols=width):
        return vecs[pl.ds(i, 1), pl.ds(col, cols)]


    def group_select(offset, per, first, cols):
        lane = lax.broadcasted_iota(jnp.int32, (128, cols), 0)
        column = lax.broadcasted_iota(jnp.int32, (128, cols), 1) + first
        return lane == (offset % 128) + jnp.bitwise_and(column, per - 1)

    def owner_of(per, first, cols):
        device = lax.broadcasted_iota(jnp.int32, (devices, cols), 0)
        column = lax.broadcasted_iota(jnp.int32, (devices, cols), 1) + first
        return lax.shift_right_logical(column, per.bit_length() - 1) == device

    def vector_places():
        spots = [(i, 128 + i * rows, rows, 0) for i in range(VECTORS)]
        return spots + [(UP + j, 0, down_rows, j * width) for j in range(4)]

    def take_vectors():
        small_in, table = r["small_in"], r["small_rows"]

        def body(b, carry):
            tile = small_in[b // 8, (b // 4) % 2, (b // 2) % 2, b % 2].astype(F32)
            for g in range(5):
                table[g, pl.ds(b, 1), :] = tile[g : g + 1]
            return carry

        lax.fori_loop(0, devices, body, 0)
        for i, offset, per, first in vector_places():
            select = group_select(offset, per, first, width).astype(F32).astype(BF16)
            spread = dot(table[offset // 128].astype(BF16), select)
            vecs[pl.ds(i, 1), :] = jnp.sum(
                jnp.where(owner_of(per, first, width), spread, 0.0), axis=0, keepdims=True
            )

    def pack_vectors():
        pack, table = r["small_pack"], r["small_rows"]
        table[...] = jnp.zeros_like(table)
        for i, offset, per, first in vector_places():
            select = group_select(offset, per, first, width).astype(F32)
            spread = jnp.where(owner_of(per, first, width), gvecs[pl.ds(i, 1), :], 0.0)
            table[offset // 128] += lax.dot_general(
                spread, select, (((1,), (1,)), ((), ())),
                precision=lax.Precision.HIGHEST, preferred_element_type=F32,
            )

        def body(b, carry):
            for g in range(8):
                pack[b // 8, (b // 4) % 2, (b // 2) % 2, b % 2, g : g + 1, :] = table[g, pl.ds(b, 1), :]
            return carry

        lax.fori_loop(0, devices, body, 0)

    def self_project(j):
        def run(w):
            value = dot(x_in[...], matrix(w[...]))
            cols = pl.ds(j * COLS, COLS)
            part, first = j * COLS // width, j * COLS % width
            if part == 0:
                value = (value + vec(SELF_Q, first, COLS)) * scale
            if part == 2:
                value = value + vec(SELF_V, first, COLS)
            qkv[:, cols] = value.astype(BF16)

        return run

    def head_masks():
        lane = lax.broadcasted_iota(jnp.int32, (1, 128), 1)
        low = (lane < HEAD_DIM).astype(F32).astype(BF16)
        return low, (lane >= HEAD_DIM).astype(F32).astype(BF16)

    def both_heads(two):
        low, high = head_masks()
        return jnp.concatenate([two * low, two * high], axis=0)

    def one_row_each(stacked):
        lane = lax.broadcasted_iota(jnp.int32, (tgt_len, 128), 1)
        return jnp.where(lane < HEAD_DIM, stacked[:tgt_len], stacked[tgt_len:])

    def scores_of(keys, queries, length, causal):
        scores = dot_nt(keys, queries)
        key = lax.broadcasted_iota(jnp.int32, scores.shape, 0)
        usable = key < length
        if causal:
            query = jnp.bitwise_and(lax.broadcasted_iota(jnp.int32, scores.shape, 1), tgt_len - 1)
            usable = usable & (key <= query)
        return jnp.where(usable, scores, MASK_VALUE)

    def attend(u, queries, q_at, keys, k_at, values, v_at, key_count, lengths, causal, out, lse):
        s, pair = u // pairs, u % pairs
        lane = pair * 128
        q_rows = pl.ds(pl.multiple_of(s * tgt_len, tgt_len), tgt_len)
        k_rows = pl.ds(pl.multiple_of(s * key_count, key_count), key_count)

        def cols(first):
            return pl.ds(pl.multiple_of(first + lane, 128), 128)

        stacked = both_heads(queries[q_rows, cols(q_at)])
        scores = scores_of(keys[k_rows, cols(k_at)], stacked, lengths[s], causal)
        peak = jnp.max(scores, axis=0, keepdims=True)
        exponentials = jnp.exp(scores - peak)
        total = jnp.sum(exponentials, axis=0, keepdims=True)
        probs = (exponentials * (1.0 / total)).astype(BF16)
        mixed = dot_tn(values[k_rows, cols(v_at)], probs)
        out[q_rows, cols(0)] = one_row_each(mixed.T).astype(BF16)
        lse[pl.ds(u, 1), :] = peak + jnp.log(total)

    def attend_back(u, queries, q_at, keys, k_at, values, v_at, key_count, lengths, causal, lse, value_sum):
        s, pair = u // pairs, u % pairs
        lane = pair * 128
        q_rows = pl.ds(pl.multiple_of(s * tgt_len, tgt_len), tgt_len)
        k_rows = pl.ds(pl.multiple_of(s * key_count, key_count), key_count)

        def cols(first):
            return pl.ds(pl.multiple_of(first + lane, 128), 128)

        stacked = both_heads(queries[q_rows, cols(q_at)])
        upstream = both_heads(d_attn[q_rows, cols(0)])
        key_rows = keys[k_rows, cols(k_at)]
        scores = scores_of(key_rows, stacked, lengths[s], causal)
        probs = jnp.exp(scores - lse[pl.ds(u, 1), :])
        prob_grad = dot_nt(values[k_rows, cols(v_at)], upstream)
        delta = jnp.sum(probs * prob_grad, axis=0, keepdims=True)
        score_grad = (probs * (prob_grad - delta)).astype(BF16)
        query_grad = dot_tn(key_rows, score_grad)
        value_grad = dot(probs.astype(BF16), upstream).astype(BF16)
        values[k_rows, cols(v_at)] = value_grad
        keys[k_rows, cols(k_at)] = dot(score_grad, stacked).astype(BF16)
        queries[q_rows, cols(q_at)] = (one_row_each(query_grad.T) * scale).astype(BF16)
        gvecs[pl.ds(value_sum, 1), cols(0)] += jnp.sum(value_grad.astype(F32), axis=0, keepdims=True)

    def self_attend(first, last):
        def body(u, carry):
            attend(u, qkv, 0, qkv, width, qkv, 2 * width, tgt_len, r["tgt_lengths"], True,
                   self_attn, r["self_lse"])
            return carry

        return lambda: lax.fori_loop(first, last, body, 0)

    def cross_attend(first, last):
        def body(u, carry):
            attend(u, cross_q, 0, cross_k, 0, cross_v, 0, mem_len, r["mem_lengths"], False,
                   cross_attn, r["cross_lse"])
            return carry

        return lambda: lax.fori_loop(first, last, body, 0)

    def self_attend_back(first, last):
        def body(u, carry):
            attend_back(u, qkv, 0, qkv, width, qkv, 2 * width, tgt_len, r["tgt_lengths"], True,
                        r["self_lse"], SELF_V)
            return carry

        return lambda: lax.fori_loop(first, last, body, 0)

    def cross_attend_back(first, last):
        def body(u, carry):
            attend_back(u, cross_q, 0, cross_k, 0, cross_v, 0, mem_len, r["mem_lengths"], False,
                        r["cross_lse"], CROSS_V)
            return carry

        return lambda: lax.fori_loop(first, last, body, 0)

    ROW_TILE = 64

    def over_rows(body):
        def step(i, carry):
            body(pl.ds(pl.multiple_of(i * ROW_TILE, ROW_TILE), ROW_TILE))
            return carry

        lax.fori_loop(0, tokens // ROW_TILE, step, 0)

    def normalise(summed):
        average = jnp.mean(summed, axis=-1, keepdims=True)
        centred = summed - average
        inverse = lax.rsqrt(jnp.mean(centred * centred, axis=-1, keepdims=True) + NORM_EPSILON)
        return centred * inverse, inverse

    def normalise_back(at, incoming, normed, inverse, gain):
        gvecs[pl.ds(at, 1), :] += jnp.sum(incoming * normed, axis=0, keepdims=True)
        gvecs[pl.ds(at + 1, 1), :] += jnp.sum(incoming, axis=0, keepdims=True)
        scaled = incoming * gain
        centred = (
            scaled
            - jnp.mean(scaled, axis=-1, keepdims=True)
            - normed * jnp.mean(scaled * normed, axis=-1, keepdims=True)
        )
        return centred * inverse

    def branch(attn, at, j):
        def run(w):
            cols = pl.ds(j * COLS, COLS)
            acc[:, cols] = dot(attn[...], matrix(w[...])) + vec(at, j * COLS, COLS)

        return run

    def norm_one():
        def body(at):
            normed, inverse = normalise(x_in[at, :].astype(F32) + acc[at, :])
            hidden_one = normed * vec(GAIN1) + vec(SHIFT1)
            n1[at, :] = normed
            r1[at, :] = inverse
            h1[at, :] = hidden_one
            h1_low[at, :] = hidden_one.astype(BF16)

        over_rows(body)

    def cross_query(j):
        def run(w):
            cols = pl.ds(j * COLS, COLS)
            value = (dot(h1_low[...], matrix(w[...])) + vec(CROSS_Q, j * COLS, COLS)) * scale
            cross_q[:, cols] = value.astype(BF16)

        return run

    def cross_project(target, at, j):
        def run(w):
            weight = matrix(w[...])

            def body(i, carry):
                at_rows = pl.ds(pl.multiple_of(i * 256, 256), 256)
                value = dot(mem[at_rows, :], weight)
                if at is not None:
                    value = value + vec(at, j * COLS, COLS)
                target[at_rows, pl.ds(j * COLS, COLS)] = value.astype(BF16)
                return carry

            lax.fori_loop(0, samples * mem_len // 256, body, 0)

        return run

    def norm_two():
        def body(at):
            normed, inverse = normalise(h1[at, :] + acc[at, :])
            hidden_two = normed * vec(GAIN2) + vec(SHIFT2)
            n2[at, :] = normed
            r2[at, :] = inverse
            flow[at, :] = hidden_two
            h2_low[at, :] = hidden_two.astype(BF16)

        over_rows(body)

    def feed_up(j):
        def run(w):
            row, first = UP + j * COLS // width, j * COLS % width
            cols = pl.ds(j * COLS, COLS)
            pre = dot(h2_low[...], matrix(w[...])) + vec(row, first, COLS)
            normal_cdf = 0.5 * (1.0 + lax.erf(pre * (1.0 / math.sqrt(2.0))))
            density = jnp.exp(-0.5 * pre * pre) * (1.0 / math.sqrt(2.0 * math.pi))
            act[:, cols] = (pre * normal_cdf).astype(BF16)
            slope[:, cols] = (normal_cdf + pre * density).astype(BF16)

        return run

    def feed_down(j):
        def run(w):
            acc[:, pl.ds(j * 256, 256)] = dot(act[...], matrix(w[...])) + vec(DOWN, j * 256, 256)

        return run

    def norm_three():
        gvecs[...] = jnp.zeros_like(gvecs)

        def body(at):
            normed, inverse = normalise(flow[at, :] + acc[at, :])
            r["block_out"][at, :] = (normed * vec(GAIN3) + vec(SHIFT3)).astype(BF16)
            grad = normalise_back(GAIN3, cot[at, :].astype(F32), normed, inverse, vec(GAIN3))
            low = grad.astype(BF16)
            flow[at, :] = grad
            d_ffn[at, :] = low
            gvecs[pl.ds(DOWN, 1), :] += jnp.sum(low.astype(F32), axis=0, keepdims=True)

        over_rows(body)

    def pre_back(i):
        def run(w):
            weight = matrix(w[...])
            for part in range(2):
                cols = pl.ds(i * width + part * COLS, COLS)
                value = dot_nt(d_ffn[...], weight[part * COLS : (part + 1) * COLS])
                low = (value * slope[:, cols].astype(F32)).astype(BF16)
                slope[:, cols] = low
                gvecs[pl.ds(UP + i, 1), pl.ds(part * COLS, COLS)] = jnp.sum(
                    low.astype(F32), axis=0, keepdims=True
                )

        return run

    def flow_back(grads, first, j):
        def run(w):
            flow[...] += dot_nt(grads[:, pl.ds(first + j * COLS, COLS)], matrix(w[...]))

        return run

    def norm_two_back():
        def body(at):
            grad = normalise_back(GAIN2, flow[at, :], n2[at, :], r2[at, :], vec(GAIN2))
            low = grad.astype(BF16)
            flow[at, :] = grad
            d_cross[at, :] = low
            gvecs[pl.ds(CROSS_O, 1), :] += jnp.sum(low.astype(F32), axis=0, keepdims=True)

        over_rows(body)

    def norm_one_back():
        gvecs[pl.ds(CROSS_Q, 1), :] = jnp.sum(cross_q[...].astype(F32), axis=0, keepdims=True)

        def body(at):
            grad = normalise_back(GAIN1, flow[at, :], n1[at, :], r1[at, :], vec(GAIN1))
            low = grad.astype(BF16)
            flow[at, :] = grad
            d_self[at, :] = low
            gvecs[pl.ds(SELF_O, 1), :] += jnp.sum(low.astype(F32), axis=0, keepdims=True)

        over_rows(body)

    def attn_back(grads, j):
        def run(w):
            value = dot_nt(grads[:, pl.ds(j * COLS, COLS)], matrix(w[...]))
            if j == 0:
                acc[...] = value
            else:
                d_attn[...] = (acc[...] + value).astype(BF16)

        return run

    def vector_sums():
        gvecs[pl.ds(SELF_Q, 1), :] = jnp.sum(qkv[:, pl.ds(0, width)].astype(F32), axis=0, keepdims=True)
        pack_vectors()

    def target_done():
        r["target_grad"][...] = flow[...].astype(BF16)

    staged, stage_sem = r["staged"], r["stage_sem"]
    stage_copies = []

    def memory_back(half, tiles):
        half_cols = width // 2

        def run(w):
            weight = matrix(w[...])
            for tile in tiles:
                slot = len(stage_copies) % 2
                if len(stage_copies) >= 2:
                    stage_copies[-2].wait()
                at_rows = pl.ds(tile * 256, 256)
                value = dot_nt(cross_k[at_rows, :], weight[:, :width])
                value += dot_nt(cross_v[at_rows, :], weight[:, width:])
                staged[slot] = value.astype(BF16)
                copy = pltpu.make_async_copy(
                    staged.at[slot],
                    r["memory_grad"].at[at_rows, pl.ds(half * half_cols, half_cols)],
                    stage_sem.at[slot],
                )
                copy.start()
                stage_copies.append(copy)

        return run


    every = (far_all, pl.ds(0, 2), pl.ds(0, 2), pl.ds(0, 2))
    loads = []

    def column_load(a, col):
        return (whole[a].at[(*every, pl.ds(0, rows), pl.ds(col, COLS))], "wbuf", 2)

    def quarter_load(j):
        return (whole[FDOWN].at[(*every, pl.ds(0, down_rows), pl.ds(j * 256, 256))], "wquarter", 2)

    def group_load(i):
        return (whole[FDOWN].at[(pl.ds(i * zs, zs), *every[1:])], "wgroup", 1)

    def half_load(i):
        return (
            whole[CQKV].at[(pl.ds(i * zh, zh), *every[1:], pl.ds(0, rows), pl.ds(width, 2 * width))],
            "whalf",
            1,
        )

    chunks, index = gather_chunks([s.shape for s in shards])
    count = len(chunks)
    per_half = width // COLS
    forward = []
    backward = []

    def piece(pieces, cost, run, load=None, dep=0, name=None):
        pieces.append(dict(cost=cost, run=run, load=load, dep=dep, name=name))

    def down_dep(j):
        return index[(FDOWN, down_rows - rows, j * 256 // COLS * COLS)]

    piece(forward, 4.0, take_vectors, None, 0)
    for j in range(3 * width // COLS):
        piece(forward, 0.7, self_project(j), column_load(SQKV, j * COLS), index[(SQKV, 0, j * COLS)])
    for first in range(0, samples * pairs, 8):
        piece(forward, 1.5, self_attend(first, first + 8), None, 0)
    for j in range(per_half):
        piece(forward, 0.7, branch(self_attn, SELF_O, j), column_load(SOUT, j * COLS), index[(SOUT, 0, j * COLS)])
    piece(forward, 1.5, norm_one)
    for target, at, first in ((cross_k, None, width), (cross_v, CROSS_V, 2 * width)):
        for j in range(per_half):
            col = first + j * COLS
            piece(forward, 3.0, cross_project(target, at, j), column_load(CQKV, col), index[(CQKV, 0, col)])
    for j in range(per_half):
        piece(forward, 0.7, cross_query(j), column_load(CQKV, j * COLS), index[(CQKV, 0, j * COLS)])
    for first in range(0, samples * pairs, 4):
        piece(forward, 2.5, cross_attend(first, first + 4))
    for j in range(per_half):
        piece(forward, 0.7, branch(cross_attn, CROSS_O, j), column_load(COUT, j * COLS), index[(COUT, 0, j * COLS)])
    piece(forward, 1.5, norm_two)
    for j in range(hidden // COLS):
        piece(forward, 1.5, feed_up(j), column_load(FUP, j * COLS), index[(FUP, 0, j * COLS)])
    for j in range(width // 256):
        piece(forward, 0.8, feed_down(j), quarter_load(j), down_dep(j))
    piece(forward, 2.0, norm_three)

    for i in range(4):
        piece(backward, 1.5, pre_back(i), group_load(i), name="pre%d" % i)
    for j in range(hidden // COLS):
        piece(backward, 0.8, flow_back(slope, 0, j), column_load(FUP, j * COLS))
    piece(backward, 1.5, norm_two_back, name="norm2")
    for j in range(per_half):
        piece(backward, 0.8, attn_back(d_cross, j), column_load(COUT, j * COLS))
    for first in range(0, samples * pairs, 2):
        piece(backward, 2.5, cross_attend_back(first, first + 2), name="cross")
    for j in range(per_half):
        piece(backward, 0.8, flow_back(cross_q, 0, j), column_load(CQKV, j * COLS))
    piece(backward, 1.5, norm_one_back, name="norm1")
    for j in range(per_half):
        piece(backward, 0.8, attn_back(d_self, j), column_load(SOUT, j * COLS))
    for first in range(0, samples * pairs, 8):
        piece(backward, 2.0, self_attend_back(first, first + 8), name="self")
    piece(backward, 3.0, vector_sums, name="vectors")
    for j in range(3 * width // COLS):
        piece(backward, 0.8, flow_back(qkv, 0, j), column_load(SQKV, j * COLS))
    piece(backward, 0.5, target_done)
    tile_count = samples * mem_len // 256
    for half in range(2):
        for first in range(0, tile_count, 2):
            piece(backward, 2.5, memory_back(half, range(first, first + 2)), ("keep", half_load(half))[first == 0])

    def prepare(pieces):
        uses = {}
        last = None
        for p in pieces:
            if p["load"] == "keep":
                p["copy"], p["buffer"] = None, last
                continue
            p["copy"] = p["buffer"] = None
            if p["load"] is not None:
                src, name, slots = p["load"]
                n = uses.get(name, 0)
                uses[name] = n + 1
                p["buffer"] = r[name].at[n % slots]
                p["slots"] = slots
                sem = r["load_sem"].at[{"wbuf": 0, "wquarter": 2, "wgroup": 4, "whalf": 5}[name] + n % slots]
                p["copy"] = pltpu.make_async_copy(src, p["buffer"], sem)
                last = p["buffer"]
            p["started"] = False

    def start(p):
        if p["copy"] is not None and not p["started"]:
            p["copy"].start()
            p["started"] = True

    def run_piece(pieces, ready):
        p = pieces.pop(0)
        start(p)
        for later in pieces:
            if later["load"] not in (None, "keep"):
                if later["dep"] <= ready and later["slots"] > 1:
                    start(later)
                break
        if p["copy"] is not None:
            p["copy"].wait()
        if p["buffer"] is not None:
            p["run"](p["buffer"])
        else:
            p["run"]()
        return p

    def work(pieces, ready, limit):
        spent = 0.0
        while pieces and pieces[0]["dep"] <= ready and spent < limit:
            spent += run_piece(pieces, ready)["cost"]

    prepare(forward)
    prepare(backward)


    in_copies = [
        pltpu.make_async_copy(r["mem_hbm"], mem, r["in_sem"].at[0]),
        pltpu.make_async_copy(r["cot_hbm"], cot, r["in_sem"].at[1]),
    ]

    def block(ref, k, *lead):
        _, row, row_count, col, cols = chunks[k]
        return ref.at[(*lead, pl.ds(row, row_count), pl.ds(col, cols))]

    def gathered(k, *lead):
        return block(whole[chunks[k][0]], k, *lead)

    local = []
    for a in range(7):
        copy = pltpu.make_async_copy(shards[a], whole[a].at[far, y, core, x], r["local_sem"].at[a])
        copy.start()
        local.append(copy)
    greet(me)
    for copy in in_copies:
        copy.start()

    sent = []

    def go(copy):
        copy.start()
        sent.append(copy)
        return copy

    far_copies, near_copies, other_copies, pass_copies, twin_copies = {}, {}, {}, {}, {}
    last_lane = far_count - 1
    gsend, grecv = r["gsend"], r["grecv"]

    def send(k, lane, ref, device):
        return go(remote(ref, ref, gsend.at[k, lane], grecv.at[k, lane], device))

    def start_far(k):
        far_copies[k] = [
            go(
                remote(
                    block(shards[chunks[k][0]], k),
                    gathered(k, far, y, core, x),
                    gsend.at[k, d],
                    grecv.at[k, d],
                    device,
                )
            )
            for d, (_, device) in enumerate(me["far_devices"])
        ]

    def start_near(k):
        column = gathered(k, far_all, y, core, x)
        near_copies[k] = send(k, last_lane, column, me["near_device"])
        other_copies[k] = send(k, last_lane + 1, column, me["other_device"])

    def start_pass(k):
        pass_copies[k] = send(k, last_lane + 2, gathered(k, far_all, near[0], core, near[1]), me["other_device"])

    def start_twin(k):
        half = gathered(k, far_all, pl.ds(0, 2), core, pl.ds(0, 2))
        twin_copies[k] = send(k, last_lane + 3, half, me["twin_device"])

    skew = GATHER_SKEW
    for t in range(count + 3 * skew + 1):
        k = t - 3 * skew
        if 0 <= k < count:
            other_copies[k].wait_recv()
            pass_copies[k].wait_recv()
            start_twin(k)
        k = t - 2 * skew
        if 0 <= k < count:
            near_copies[k].wait_recv()
            start_pass(k)
        k = t - skew
        if 0 <= k < count:
            if k == 0:
                for copy in local:
                    copy.wait()
            for copy in far_copies[k]:
                copy.wait_recv()
            start_near(k)
        if t < count:
            start_far(t)
        k = t - 3 * skew - 1
        if k >= 0:
            if k == 0:
                for copy in in_copies:
                    copy.wait()
            twin_copies[k].wait_recv()
            work(forward, k, STEP_WORK)
    work(forward, count, 1e9)
    for copy in sent:
        copy.wait_send()


    own, total, from_other, from_near, from_far = (
        r[n] for n in ("own", "total", "from_other", "from_near", "from_far")
    )
    small_buffers = (r["small_pack"], r["total_s"], r["from_other_s"], r["from_near_s"], r["from_far_s"])
    out_chunks = scatter_chunks(width)
    out_count = len(out_chunks)
    skew = SCATTER_SKEW
    own_slots, total_slots, land_slots = own.shape[0], total.shape[0], from_other.shape[0]
    ssend, srecv = r["ssend"], r["srecv"]

    def buffers(k):
        if out_chunks[k][0] == SMALL:
            return small_buffers
        return (
            own.at[k % own_slots],
            total.at[k % total_slots],
            from_other.at[k % land_slots],
            from_near.at[k % land_slots],
            from_far.at[k % land_slots],
        )

    def compute(k):
        a, col = out_chunks[k]
        if a == SMALL:
            return
        target = buffers(k)[0]
        if a == FDOWN:
            right = d_ffn[:, pl.ds(col, 128)]

            def body(i, carry):
                left = act[:, pl.ds(pl.multiple_of(i * 256, 256), 256)]
                value = dot_tn(left, right).astype(BF16)
                for piece_at in range(0, 256, rows):
                    b = i * (256 // down_rows) + piece_at // down_rows
                    q = piece_at % down_rows // rows
                    target[b // 8, (b // 4) % 2, (b // 2) % 2, b % 2, :, q * 128 : (q + 1) * 128] = value[
                        piece_at : piece_at + rows
                    ]
                return carry

            lax.fori_loop(0, hidden // 256, body, 0)
            return
        left, right = {
            FUP: (h2_low, slope),
            COUT: (cross_attn, d_cross),
            SOUT: (self_attn, d_self),
            SQKV: (x_in, qkv),
            CQKV: (
                (h1_low, cross_q),
                (mem, cross_k),
                (mem, cross_v),
            )[col // width if a == CQKV else 0],
        }[a]
        first = col % width if a == CQKV else col
        right = right[:, pl.ds(first, COLS)]

        def body(i, carry):
            value = dot_tn(left[:, pl.ds(pl.multiple_of(i * 256, 256), 256)], right).astype(BF16)
            for j in range(256 // rows):
                target[i * (256 // rows) // 8 + j // 8, (j // 4) % 2, (j // 2) % 2, j % 2] = value[
                    j * rows : (j + 1) * rows
                ]
            return carry

        lax.fori_loop(0, width // 256, body, 0)

    twins, others, nears, fars = {}, {}, {}, {}

    def start_twin_sum(k):
        target, landing = buffers(k)[:2]
        twins[k] = remote(
            target.at[far_all, pl.ds(0, 2), 1 - core, pl.ds(0, 2)],
            landing,
            ssend.at[k, 0],
            srecv.at[k, 0],
            me["twin_device"],
        )
        twins[k].start()

    def add_own(k):
        mine, running = buffers(k)[:2]

        def body(i, carry):
            f, yy, xx = i // 4, (i // 2) % 2, i % 2
            running[f, yy, xx] = running[f, yy, xx] + mine[f, yy, core, xx]
            return carry

        lax.fori_loop(0, far_count * 4, body, 0)

    def start_others(k):
        running, landing = buffers(k)[1:3]
        others[k] = []
        for i, place in enumerate((diagonal, other)):
            copy = remote(
                running.at[far_all, place[0], place[1]],
                landing.at[i],
                ssend.at[k, 1 + i],
                srecv.at[k, 1 + i],
                me["other_device"],
            )
            copy.start()
            others[k].append(copy)

    def add_other(k, i):
        running, landing = buffers(k)[1:3]
        place = (near, (y, x))[i]

        def body(f, carry):
            running[f, place[0], place[1]] = running[f, place[0], place[1]] + landing[i, f]
            return carry

        lax.fori_loop(0, far_count, body, 0)

    def start_near_sum(k):
        _, running, _, landing, _ = buffers(k)
        nears[k] = remote(
            running.at[far_all, near[0], near[1]],
            landing,
            ssend.at[k, 3],
            srecv.at[k, 3],
            me["near_device"],
        )
        nears[k].start()

    def add_near(k):
        _, running, _, landing, _ = buffers(k)

        def body(f, carry):
            running[f, y, x] = running[f, y, x] + landing[f]
            return carry

        lax.fori_loop(0, far_count, body, 0)

    def start_fars(k):
        _, running, _, _, landing = buffers(k)
        fars[k] = []
        for d, (target, device) in enumerate(me["far_devices"]):
            copy = remote(running.at[target, y, x], landing.at[d], ssend.at[k, 4 + d], srecv.at[k, 4 + d], device)
            copy.start()
            fars[k].append(copy)

    def finish(k):
        _, running, _, _, landing = buffers(k)
        a, col = out_chunks[k]
        result = running[far, y, x].astype(F32)
        for d in range(far_count - 1):
            result += landing[d].astype(F32)
        if a == SMALL:
            sums[a][...] = result
        elif a == FDOWN:
            for q in range(4):
                sums[a][q * rows : (q + 1) * rows, pl.ds(col, 128)] = result[:, q * 128 : (q + 1) * 128]
        else:
            sums[a][:, pl.ds(col, COLS)] = result
        for copy in (*others[k], nears[k], *fars[k]):
            copy.wait_send()

    needs = {FUP: "pre3", COUT: "norm2", CQKV: "cross", SOUT: "norm1", SQKV: "self", SMALL: "vectors"}

    for t in range(out_count + 4 * skew):
        k = t - 4 * skew
        if 0 <= k < out_count:
            for copy in fars[k]:
                copy.wait_recv()
            finish(k)
        k = t - 3 * skew
        if 0 <= k < out_count:
            nears[k].wait_recv()
            add_near(k)
            start_fars(k)
        k = t - 2 * skew
        if 0 <= k < out_count:
            others[k][0].wait_recv()
            add_other(k, 0)
            start_near_sum(k)
            others[k][1].wait_recv()
            add_other(k, 1)
        k = t - skew
        if 0 <= k < out_count:
            twins[k].wait()
            add_own(k)
            start_others(k)
        if t < out_count:
            need = needs.get(out_chunks[t][0])
            while any(p["name"] == need for p in backward if need):
                run_piece(backward, count)
            compute(t)
            start_twin_sum(t)
        work(backward, count, STEP_WORK)
    work(backward, count, 1e9)
    for copy in stage_copies[-2:]:
        copy.wait()


def layer(mesh, target_input, memory, cotangent, mem_lengths, tgt_lengths, shards, small):
    samples, tgt_len, width = target_input.shape
    mem_len = memory.shape[1]
    far_count = mesh.shape["wide"] // 4
    rows = shards[SQKV].shape[0]
    tokens, keys, hidden = samples * tgt_len, samples * mem_len, 4 * width
    zs, zh = max(1, far_count // 4), max(1, far_count // 2)
    lanes = far_count + 3
    count = len(gather_chunks([s.shape for s in shards])[0])
    out_count = len(scatter_chunks(width))
    lead = (far_count, 2, 2, 2)
    shrink = 1 if rows >= 16 else 2
    total_slots, land_slots, own_slots = 5 * SCATTER_SKEW + 1, 2 * SCATTER_SKEW + 1, SCATTER_SKEW + 1

    def vmem(shape, dtype=BF16):
        return pltpu.VMEM(shape, dtype)

    small_sum = (8, 128)
    scratch = [
        vmem((keys, width)),
        vmem((tokens, width)),
        vmem((tokens, 3 * width)),
        vmem((tokens, width)),
        vmem((tokens, width), F32),
        vmem((tokens, 1), F32),
        vmem((tokens, width), F32),
        vmem((tokens, width)),
        vmem((tokens, width)),
        vmem((keys, width)),
        vmem((keys, width)),
        vmem((tokens, width)),
        vmem((tokens, width), F32),
        vmem((tokens, 1), F32),
        vmem((tokens, width), F32),
        vmem((tokens, width)),
        vmem((tokens, hidden)),
        vmem((tokens, hidden)),
        vmem((tokens, width), F32),
        vmem((tokens, width)),
        vmem((tokens, width)),
        vmem((tokens, width)),
        vmem((tokens, width)),
        vmem((samples * HEADS // 2, 2 * tgt_len), F32),
        vmem((samples * HEADS // 2, 2 * tgt_len), F32),
        vmem((24, width), F32),
        vmem((24, width), F32),
        vmem((2, 256, width // 2)),
        vmem((2,) + lead + (rows, COLS)),
        vmem((2,) + lead + (4 * rows, 256)),
        vmem((1, zs, 2, 2, 2, 4 * rows, width)),
        vmem((1, zh, 2, 2, 2, rows, 2 * width)),
        vmem(lead + (SMALL_ROWS, 128)),
        vmem((8, mesh.size, 128), F32),
        vmem(lead + small_sum, F32),
        vmem((own_slots,) + lead + (rows, COLS)),
        vmem((total_slots, far_count, 2, 2, rows, COLS)),
        vmem((land_slots, 2, far_count, rows, COLS)),
        vmem((land_slots, far_count, rows, COLS)),
        vmem((land_slots, far_count - 1, rows, COLS)),
        vmem((far_count, 2, 2) + small_sum, F32),
        vmem((2, far_count) + small_sum, F32),
        vmem((far_count,) + small_sum, F32),
        vmem((far_count - 1,) + small_sum, F32),
        pltpu.SemaphoreType.DMA((6,)),
        pltpu.SemaphoreType.DMA((2,)),
        pltpu.SemaphoreType.DMA((7,)),
        pltpu.SemaphoreType.DMA((count, lanes)),
        pltpu.SemaphoreType.DMA((count, lanes)),
        pltpu.SemaphoreType.DMA((out_count, lanes)),
        pltpu.SemaphoreType.DMA((out_count, lanes)),
        pltpu.SemaphoreType.DMA((2,)),
    ]
    in_vmem, anywhere = pl.BlockSpec(memory_space=pltpu.VMEM), pl.BlockSpec(memory_space=pl.ANY)
    in_smem = pl.BlockSpec(memory_space=pltpu.SMEM)
    out_shape = [
        jax.ShapeDtypeStruct((tokens, width), BF16),
        jax.ShapeDtypeStruct((tokens, width), BF16),
        jax.ShapeDtypeStruct((keys, width), BF16),
    ]
    out_shape += [jax.ShapeDtypeStruct(s.shape, F32) for s in shards]
    out_shape += [jax.ShapeDtypeStruct(small_sum, F32)]
    out_shape += [jax.ShapeDtypeStruct(lead + s.shape, BF16) for s in shards]
    outs = pl.pallas_call(
        functools.partial(layer_kernel, (far_count, rows, width, samples, tgt_len, mem_len)),
        out_shape=out_shape,
        in_specs=[in_vmem, anywhere, anywhere, in_smem, in_smem] + [in_vmem] * 7,
        out_specs=[in_vmem, in_vmem, anywhere] + [in_vmem] * 7 + [anywhere] * 6,
        scratch_shapes=scratch,
        compiler_params=pltpu.CompilerParams(
            collective_id=0, has_side_effects=True, vmem_limit_bytes=63 * 2**20
        ),
        cost_estimate=pl.CostEstimate(flops=52 * 10**9, bytes_accessed=10**8, transcendentals=10**7),
        name="decoder_layer",
    )(
        target_input.reshape(tokens, width),
        memory.reshape(keys, width),
        cotangent.reshape(tokens, width),
        mem_lengths,
        tgt_lengths,
        *shards,
        small,
    )
    return outs[:10]


def step(
    mesh,
    target_input,
    memory,
    cotangent,
    mem_lengths,
    tgt_lengths,
    self_qkv,
    self_out,
    self_bias,
    norm1_gain,
    norm1_shift,
    cross_qkv,
    cross_out,
    cross_bias,
    norm2_gain,
    norm2_shift,
    ffn_up,
    up_bias,
    ffn_down,
    down_bias,
    norm3_gain,
    norm3_shift,
):
    per, up_per = norm1_gain.shape[0], up_bias.shape[0]
    pieces = [jnp.pad(up_bias, (0, 128 - up_per))] + [
        v.reshape(-1)
        for v in (
            self_bias, norm1_gain, norm1_shift, cross_bias, norm2_gain, norm2_shift,
            down_bias, norm3_gain, norm3_shift,
        )
    ]
    small = jnp.concatenate(pieces)
    small = jnp.pad(small, (0, SMALL_ROWS * 128 - small.shape[0])).reshape(SMALL_ROWS, 128)
    block_out, target_grad, memory_grad, *grads, sums = layer(
        mesh, target_input, memory, cotangent, mem_lengths, tgt_lengths,
        [self_qkv, self_out, cross_qkv, cross_out, ffn_up, ffn_down], small,
    )
    sums = sums.reshape(-1)

    def vector(i, n=1):
        return sums[128 + i * per : 128 + (i + n) * per]

    return (
        block_out.reshape(target_input.shape),
        target_grad.reshape(target_input.shape),
        memory_grad.reshape(memory.shape),
        grads[SQKV],
        grads[SOUT],
        vector(SELF_Q, 3).reshape(3, per),
        vector(GAIN1),
        vector(SHIFT1),
        grads[CQKV],
        grads[COUT],
        vector(CROSS_Q, 3).reshape(3, per),
        vector(GAIN2),
        vector(SHIFT2),
        grads[FUP],
        sums[:up_per],
        grads[FDOWN],
        vector(DOWN),
        vector(GAIN3),
        vector(SHIFT3),
    )


def solution(mesh):
    both = ("wide", "narrow")
    stream, matrix_spec, vector_spec, bias_spec = P(both, None, None), P(both, None), P(both), P(None, both)
    weights = (
        matrix_spec, matrix_spec, bias_spec, vector_spec, vector_spec,
        matrix_spec, matrix_spec, bias_spec, vector_spec, vector_spec,
        matrix_spec, vector_spec, matrix_spec, vector_spec, vector_spec, vector_spec,
    )
    return jax.shard_map(
        functools.partial(step, mesh),
        mesh=mesh,
        in_specs=(stream, stream, stream, vector_spec, vector_spec) + weights,
        out_specs=(stream, stream, stream) + weights,
        check_vma=False,
    )
```

```python
import functools
import math

import jax
import jax.numpy as jnp
from jax import lax
from jax.experimental import pallas as pl
from jax.experimental.pallas import tpu as pltpu
from jax.sharding import PartitionSpec as P

MESH = pl.DeviceIdType.MESH
HEADS = 16
HEAD_DIM = 64
NORM_EPSILON = 1e-05
MASK_VALUE = -1e30
COLS = 512
GATHER_SKEW = 2
SCATTER_SKEW = 2
STEP_WORK = 2.5
AHEAD = 8
SMALL_ROWS = 16

F32 = jnp.float32
BF16 = jnp.bfloat16

SELF_Q, SELF_V, SELF_O, GAIN1, SHIFT1, CROSS_Q, CROSS_V, CROSS_O, GAIN2, SHIFT2, DOWN, GAIN3, SHIFT3, UP = range(14)
VECTORS = 13


def dot(a, b):
    return lax.dot_general(a, b, (((1,), (0,)), ((), ())), preferred_element_type=F32)


def dot_nt(a, b):
    return lax.dot_general(a, b, (((1,), (1,)), ((), ())), preferred_element_type=F32)


def dot_tn(a, b):
    return lax.dot_general(a, b, (((0,), (0,)), ((), ())), preferred_element_type=F32)


def places(far_count):
    wide = lax.axis_index("wide")
    x = lax.axis_index("narrow")
    far = wide // 4
    y = (wide // 2) % 2
    core = wide % 2
    near_y = y + core * (1 - 2 * y)
    near_x = x + (1 - core) * (1 - 2 * x)
    other_y = y + (1 - core) * (1 - 2 * y)
    other_x = x + core * (1 - 2 * x)

    def device(f, yy, cc, xx):
        return (f * 4 + yy * 2 + cc, xx)

    return dict(
        far=far,
        y=y,
        core=core,
        x=x,
        near=(near_y, near_x),
        other=(other_y, other_x),
        diagonal=(1 - y, 1 - x),
        near_device=device(far, near_y, core, near_x),
        other_device=device(far, other_y, core, other_x),
        twin_device=device(far, y, 1 - core, x),
        far_devices=[
            (lax.rem(far + d, far_count), device(lax.rem(far + d, far_count), y, core, x))
            for d in range(1, far_count)
        ],
    )


def greet(where):
    barrier = pltpu.get_barrier_semaphore()
    partners = [where["near_device"], where["other_device"], where["twin_device"]]
    partners += [device for _, device in where["far_devices"]]
    for device in partners:
        pl.semaphore_signal(barrier, inc=1, device_id=device, device_id_type=MESH)
    pl.semaphore_wait(barrier, len(partners))


def remote(src, dst, send_sem, recv_sem, device):
    return pltpu.make_async_remote_copy(
        src_ref=src,
        dst_ref=dst,
        send_sem=send_sem,
        recv_sem=recv_sem,
        device_id=device,
        device_id_type=MESH,
    )


def matrix(value):
    rows, cols = value.shape[-2:]
    if rows % 16:
        return value.astype(F32).reshape(-1, cols).astype(BF16)
    return value.reshape(-1, cols)


ARRAYS = ("self_qkv", "self_out", "cross_qkv", "cross_out", "ffn_up", "ffn_down")
SQKV, SOUT, CQKV, COUT, FUP, FDOWN, SMALL = range(7)


def gather_chunks(shapes):
    rows = shapes[SQKV][0]
    width = shapes[SOUT][1]
    chunks = [(SMALL, 0, SMALL_ROWS, 0, 128)]
    for a, first, last in (
        (SQKV, 0, 3 * width),
        (SOUT, 0, width),
        (CQKV, width, 3 * width),
        (CQKV, 0, width),
        (COUT, 0, width),
        (FUP, 0, 4 * width),
    ):
        chunks += [(a, 0, rows, col, COLS) for col in range(first, last, COLS)]
    for col in range(0, width, COLS):
        chunks += [(FDOWN, row, rows, col, COLS) for row in range(0, 4 * rows, rows)]
    index = {(a, row, col): k for k, (a, row, _, col, _) in enumerate(chunks)}
    return chunks, index


def scatter_chunks(width):
    chunks = [(FDOWN, 128 * j) for j in range(width // 128)]
    for a, first, last in (
        (FUP, 0, 4 * width),
        (COUT, 0, width),
        (CQKV, 0, 3 * width),
        (SOUT, 0, width),
    ):
        chunks += [(a, col) for col in range(first, last, COLS)]
    chunks += [(SMALL, 0)]
    chunks += [(SQKV, col) for col in range(0, 3 * width, COLS)]
    return chunks


def layer_kernel(cfg, *refs):
    far_count, rows, width, samples, tgt_len, mem_len = cfg
    devices = 8 * far_count
    hidden = 4 * width
    down_rows = 4 * rows
    tokens = samples * tgt_len
    pairs = HEADS // 2
    scale = 1.0 / math.sqrt(HEAD_DIM)
    lanes = far_count + 3
    zs = max(1, far_count // 4)
    zh = max(1, far_count // 2)

    names = (
        "x_hbm", "mem_hbm", "cot_hbm", "mem_lengths", "tgt_lengths", "i0", "i1", "i2", "i3", "i4", "i5", "i6",
        "block_out", "target_grad", "memory_grad", "g0", "g1", "g2", "g3", "g4", "g5", "small_out", "w0", "w1",
        "w2", "w3", "w4", "w5", "x", "mem", "cot", "qkv", "self_attn", "n1", "r1", "h1", "h1_low", "cross_q",
        "cross_k", "cross_v", "cross_attn", "n2", "r2", "flow", "h2_low", "act", "act_t", "slope", "acc", "d_ffn",
        "d_cross", "d_attn", "d_self", "self_lse", "cross_lse", "vecs", "gvecs", "staged", "wbuf", "wquarter",
        "small_in", "small_rows", "small_pack", "own", "total", "from_other", "from_near", "from_far", "total_s",
        "from_other_s", "from_near_s", "from_far_s", "load_sem", "in_sem", "local_sem", "gsend", "grecv", "ssend",
        "srecv", "stage_sem",
    )
    r = dict(zip(names, refs, strict=True))
    x_in, mem, cot = r["x"], r["mem"], r["cot"]
    qkv, self_attn, n1, r1, h1, h1_low = (r[n] for n in ("qkv", "self_attn", "n1", "r1", "h1", "h1_low"))
    cross_q, cross_k, cross_v, cross_attn = (r[n] for n in ("cross_q", "cross_k", "cross_v", "cross_attn"))
    n2, r2, flow, h2_low = (r[n] for n in ("n2", "r2", "flow", "h2_low"))
    act, act_t, slope, acc = (r[n] for n in ("act", "act_t", "slope", "acc"))
    d_ffn, d_cross, d_attn, d_self = (r[n] for n in ("d_ffn", "d_cross", "d_attn", "d_self"))
    vecs, gvecs = r["vecs"], r["gvecs"]
    shards = [r["i%d" % i] for i in range(7)]
    whole = [r["w%d" % i] for i in range(6)] + [r["small_in"]]
    sums = [r["g%d" % i] for i in range(6)] + [r["small_out"]]

    me = places(far_count)
    far, y, core, x = me["far"], me["y"], me["core"], me["x"]
    far_all = pl.ds(0, far_count)
    near, other, diagonal = me["near"], me["other"], me["diagonal"]

    def vec(i, col=0, cols=width):
        return vecs[pl.ds(i, 1), pl.ds(col, cols)]


    def owner_of(per, first):
        device = lax.broadcasted_iota(jnp.int32, (devices, width), 0)
        column = lax.broadcasted_iota(jnp.int32, (devices, width), 1) + first
        return lax.shift_right_logical(column, per.bit_length() - 1) == device

    def spread_of(per):
        lane = lax.broadcasted_iota(jnp.int32, (128, width), 0)
        column = lax.broadcasted_iota(jnp.int32, (128, width), 1)
        return (lane == jnp.bitwise_and(column, per - 1)).astype(F32).astype(BF16)

    def take_vectors():
        small_in, table = r["small_in"], r["small_rows"]

        def body(b, carry):
            tile = small_in[b // 8, (b // 4) % 2, (b // 2) % 2, b % 2].astype(F32)
            for i in range(VECTORS + 1):
                table[i, pl.ds(b, 1), :] = tile[i : i + 1]
            return carry

        lax.fori_loop(0, devices, body, 0)
        spread, owner = spread_of(rows), owner_of(rows, 0)
        for i in range(VECTORS):
            values = dot(table[i].astype(BF16), spread)
            vecs[pl.ds(i, 1), :] = jnp.sum(jnp.where(owner, values, 0.0), axis=0, keepdims=True)
        values = dot(table[VECTORS].astype(BF16), spread_of(down_rows))
        for j in range(4):
            owner = owner_of(down_rows, j * width)
            vecs[pl.ds(UP + j, 1), :] = jnp.sum(jnp.where(owner, values, 0.0), axis=0, keepdims=True)

    def pack_vectors():
        pack = r["small_pack"]

        pack[...] = jnp.zeros_like(pack)
        for b in range(devices):
            lead = (b // 8, (b // 4) % 2, (b // 2) % 2, b % 2)
            lane, up_lane = b * rows // 128 * 128, b * down_rows % width // 128 * 128
            up_row = UP + b * down_rows // width
            pack[(*lead, slice(0, VECTORS))] = gvecs[0:VECTORS, lane : lane + 128]
            pack[(*lead, slice(VECTORS, VECTORS + 1))] = gvecs[up_row : up_row + 1, up_lane : up_lane + 128]

    def turn(ref, first=0, cols=width):
        def run():
            def body(i, carry):
                cols_at = pl.ds(pl.multiple_of(first + i * 256, 256), 256)
                ref[:, cols_at] = ref[:, cols_at].T
                return carry

            lax.fori_loop(0, cols // 256, body, 0)

        return run

    def turn_memory(s):
        def run():
            blocks = width // 256

            def at(i, j):
                return (
                    pl.ds(pl.multiple_of(s * mem_len + i * 256, 256), 256),
                    pl.ds(pl.multiple_of(j * 256, 256), 256),
                )

            for i in range(blocks):
                mem[at(i, i)] = mem[at(i, i)].T
                for j in range(i + 1, blocks):
                    upper, lower = mem[at(i, j)].T, mem[at(j, i)].T
                    mem[at(i, j)] = lower
                    mem[at(j, i)] = upper

        return run

    def self_project(j):
        def run(w):
            value = dot(x_in[...], matrix(w[...]))
            cols = pl.ds(j * COLS, COLS)
            part, first = j * COLS // width, j * COLS % width
            if part == 0:
                value = (value + vec(SELF_Q, first, COLS)) * scale
            if part == 2:
                value = value + vec(SELF_V, first, COLS)
            qkv[:, cols] = value.astype(BF16)

        return run

    def head_masks():
        lane = lax.broadcasted_iota(jnp.int32, (1, 128), 1)
        low = (lane < HEAD_DIM).astype(F32).astype(BF16)
        return low, (lane >= HEAD_DIM).astype(F32).astype(BF16)

    def both_heads(two):
        low, high = head_masks()
        return jnp.concatenate([two * low, two * high], axis=0)

    def one_row_each(stacked):
        lane = lax.broadcasted_iota(jnp.int32, (tgt_len, 128), 1)
        return jnp.where(lane < HEAD_DIM, stacked[:tgt_len], stacked[tgt_len:])

    def scores_of(keys, queries, length, causal):
        scores = dot_nt(keys, queries)
        key = lax.broadcasted_iota(jnp.int32, scores.shape, 0)
        usable = key < length
        if causal:
            query = jnp.bitwise_and(lax.broadcasted_iota(jnp.int32, scores.shape, 1), tgt_len - 1)
            usable = usable & (key <= query)
        return jnp.where(usable, scores, MASK_VALUE)

    def attend(u, queries, q_at, keys, k_at, values, v_at, key_count, lengths, causal, out, lse):
        s, pair = u // pairs, u % pairs
        lane = pair * 128
        q_rows = pl.ds(pl.multiple_of(s * tgt_len, tgt_len), tgt_len)
        k_rows = pl.ds(pl.multiple_of(s * key_count, key_count), key_count)

        def cols(first):
            return pl.ds(pl.multiple_of(first + lane, 128), 128)

        stacked = both_heads(queries[q_rows, cols(q_at)])
        scores = scores_of(keys[k_rows, cols(k_at)], stacked, lengths[s], causal)
        peak = jnp.max(scores, axis=0, keepdims=True)
        exponentials = jnp.exp(scores - peak)
        total = jnp.sum(exponentials, axis=0, keepdims=True)
        probs = (exponentials * (1.0 / total)).astype(BF16)
        mixed = dot_tn(values[k_rows, cols(v_at)], probs)
        out[q_rows, cols(0)] = one_row_each(mixed.T).astype(BF16)
        lse[pl.ds(u, 1), :] = peak + jnp.log(total)

    def attend_back(u, queries, q_at, keys, k_at, values, v_at, key_count, lengths, causal, lse, value_sum):
        s, pair = u // pairs, u % pairs
        lane = pair * 128
        q_rows = pl.ds(pl.multiple_of(s * tgt_len, tgt_len), tgt_len)
        k_rows = pl.ds(pl.multiple_of(s * key_count, key_count), key_count)

        def cols(first):
            return pl.ds(pl.multiple_of(first + lane, 128), 128)

        stacked = both_heads(queries[q_rows, cols(q_at)])
        upstream = both_heads(d_attn[q_rows, cols(0)])
        key_rows = keys[k_rows, cols(k_at)]
        scores = scores_of(key_rows, stacked, lengths[s], causal)
        probs = jnp.exp(scores - lse[pl.ds(u, 1), :])
        prob_grad = dot_nt(values[k_rows, cols(v_at)], upstream)
        delta = jnp.sum(probs * prob_grad, axis=0, keepdims=True)
        score_grad = (probs * (prob_grad - delta)).astype(BF16)
        query_grad = dot_tn(key_rows, score_grad)
        value_grad = dot(probs.astype(BF16), upstream).astype(BF16)
        values[k_rows, cols(v_at)] = value_grad
        keys[k_rows, cols(k_at)] = dot(score_grad, stacked).astype(BF16)
        queries[q_rows, cols(q_at)] = (one_row_each(query_grad.T) * scale).astype(BF16)
        gvecs[pl.ds(value_sum, 1), cols(0)] += jnp.sum(value_grad.astype(F32), axis=0, keepdims=True)

    def self_attend(first, last):
        def body(u, carry):
            attend(u, qkv, 0, qkv, width, qkv, 2 * width, tgt_len, r["tgt_lengths"], True,
                   self_attn, r["self_lse"])
            return carry

        return lambda: lax.fori_loop(first, last, body, 0)

    def cross_attend(first, last):
        def body(u, carry):
            attend(u, cross_q, 0, cross_k, 0, cross_v, 0, mem_len, r["mem_lengths"], False,
                   cross_attn, r["cross_lse"])
            return carry

        return lambda: lax.fori_loop(first, last, body, 0)

    def self_attend_back(first, last):
        def body(u, carry):
            attend_back(u, qkv, 0, qkv, width, qkv, 2 * width, tgt_len, r["tgt_lengths"], True,
                        r["self_lse"], SELF_V)
            return carry

        return lambda: lax.fori_loop(first, last, body, 0)

    def cross_attend_back(first, last):
        def body(u, carry):
            attend_back(u, cross_q, 0, cross_k, 0, cross_v, 0, mem_len, r["mem_lengths"], False,
                        r["cross_lse"], CROSS_V)
            return carry

        return lambda: lax.fori_loop(first, last, body, 0)

    ROW_TILE = 64

    def over_rows(body):
        def step(i, carry):
            body(pl.ds(pl.multiple_of(i * ROW_TILE, ROW_TILE), ROW_TILE))
            return carry

        lax.fori_loop(0, tokens // ROW_TILE, step, 0)

    def normalise(summed):
        average = jnp.mean(summed, axis=-1, keepdims=True)
        centred = summed - average
        inverse = lax.rsqrt(jnp.mean(centred * centred, axis=-1, keepdims=True) + NORM_EPSILON)
        return centred * inverse, inverse

    def normalise_back(at, incoming, normed, inverse, gain):
        gvecs[pl.ds(at, 1), :] += jnp.sum(incoming * normed, axis=0, keepdims=True)
        gvecs[pl.ds(at + 1, 1), :] += jnp.sum(incoming, axis=0, keepdims=True)
        scaled = incoming * gain
        centred = (
            scaled
            - jnp.mean(scaled, axis=-1, keepdims=True)
            - normed * jnp.mean(scaled * normed, axis=-1, keepdims=True)
        )
        return centred * inverse

    def branch(attn, at, j):
        def run(w):
            cols = pl.ds(j * COLS, COLS)
            acc[:, cols] = dot(attn[...], matrix(w[...])) + vec(at, j * COLS, COLS)

        return run

    def norm_one():
        def body(at):
            normed, inverse = normalise(x_in[at, :].astype(F32) + acc[at, :])
            hidden_one = normed * vec(GAIN1) + vec(SHIFT1)
            n1[at, :] = normed
            r1[at, :] = inverse
            h1[at, :] = hidden_one
            h1_low[at, :] = hidden_one.astype(BF16)

        over_rows(body)

    def cross_query(j):
        def run(w):
            cols = pl.ds(j * COLS, COLS)
            value = (dot(h1_low[...], matrix(w[...])) + vec(CROSS_Q, j * COLS, COLS)) * scale
            cross_q[:, cols] = value.astype(BF16)

        return run

    def cross_project(target, at, j):
        def run(w):
            weight = matrix(w[...])

            def body(i, carry):
                at_rows = pl.ds(pl.multiple_of(i * 256, 256), 256)
                value = dot(mem[at_rows, :], weight)
                if at is not None:
                    value = value + vec(at, j * COLS, COLS)
                target[at_rows, pl.ds(j * COLS, COLS)] = value.astype(BF16)
                return carry

            lax.fori_loop(0, samples * mem_len // 256, body, 0)

        return run

    def norm_two():
        def body(at):
            normed, inverse = normalise(h1[at, :] + acc[at, :])
            hidden_two = normed * vec(GAIN2) + vec(SHIFT2)
            n2[at, :] = normed
            r2[at, :] = inverse
            flow[at, :] = hidden_two
            h2_low[at, :] = hidden_two.astype(BF16)

        over_rows(body)

    def feed_up(j):
        def run(w):
            row, first = UP + j * COLS // width, j * COLS % width
            cols = pl.ds(j * COLS, COLS)
            pre = dot(h2_low[...], matrix(w[...])) + vec(row, first, COLS)
            normal_cdf = 0.5 * (1.0 + lax.erf(pre * (1.0 / math.sqrt(2.0))))
            density = jnp.exp(-0.5 * pre * pre) * (1.0 / math.sqrt(2.0 * math.pi))
            low = (pre * normal_cdf).astype(BF16)
            act[:, cols] = low
            act_t[pl.ds(j * COLS, COLS), :] = low.T
            slope[:, cols] = (normal_cdf + pre * density).astype(BF16)

        return run

    def feed_down(j):
        def run(w):
            acc[:, pl.ds(j * 256, 256)] = dot(act[...], matrix(w[...])) + vec(DOWN, j * 256, 256)

        return run

    def norm_three():
        gvecs[...] = jnp.zeros_like(gvecs)

        def body(at):
            normed, inverse = normalise(flow[at, :] + acc[at, :])
            r["block_out"][at, :] = (normed * vec(GAIN3) + vec(SHIFT3)).astype(BF16)
            grad = normalise_back(GAIN3, cot[at, :].astype(F32), normed, inverse, vec(GAIN3))
            low = grad.astype(BF16)
            flow[at, :] = grad
            d_ffn[at, :] = low
            gvecs[pl.ds(DOWN, 1), :] += jnp.sum(low.astype(F32), axis=0, keepdims=True)

        over_rows(body)

    def pre_back(i):
        def run(w):
            cols = pl.ds(i * width, width)
            value = None
            for q in range(4):
                part = dot_nt(d_ffn[:, pl.ds(q * 256, 256)], matrix(w[q * zs : (q + 1) * zs]))
                value = part if value is None else value + part
            low = (value * slope[:, cols].astype(F32)).astype(BF16)
            slope[:, cols] = low
            gvecs[pl.ds(UP + i, 1), :] = jnp.sum(low.astype(F32), axis=0, keepdims=True)

        return run

    def flow_back(grads, first, j):
        def run(w):
            flow[...] += dot_nt(grads[:, pl.ds(first + j * COLS, COLS)], matrix(w[...]))

        return run

    def norm_two_back():
        def body(at):
            grad = normalise_back(GAIN2, flow[at, :], n2[at, :], r2[at, :], vec(GAIN2))
            low = grad.astype(BF16)
            flow[at, :] = grad
            d_cross[at, :] = low
            gvecs[pl.ds(CROSS_O, 1), :] += jnp.sum(low.astype(F32), axis=0, keepdims=True)

        over_rows(body)

    def norm_one_back():
        gvecs[pl.ds(CROSS_Q, 1), :] = jnp.sum(cross_q[...].astype(F32), axis=0, keepdims=True)

        def body(at):
            grad = normalise_back(GAIN1, flow[at, :], n1[at, :], r1[at, :], vec(GAIN1))
            low = grad.astype(BF16)
            flow[at, :] = grad
            d_self[at, :] = low
            gvecs[pl.ds(SELF_O, 1), :] += jnp.sum(low.astype(F32), axis=0, keepdims=True)

        over_rows(body)

    def attn_back(grads, j):
        def run(w):
            value = dot_nt(grads[:, pl.ds(j * COLS, COLS)], matrix(w[...]))
            if j == 0:
                acc[...] = value
            else:
                d_attn[...] = (acc[...] + value).astype(BF16)

        return run

    def vector_sums():
        gvecs[pl.ds(SELF_Q, 1), :] = jnp.sum(qkv[:, pl.ds(0, width)].astype(F32), axis=0, keepdims=True)
        pack_vectors()

    def target_done():
        r["target_grad"][...] = flow[...].astype(BF16)

    staged, stage_sem = r["staged"], r["stage_sem"]
    stage_copies = []

    def memory_back(half, tiles):
        half_cols = width // 2

        def run(w):
            weights = [matrix(w[c // 2, c % 2 * zh : (c % 2 + 1) * zh]) for c in range(4)]
            for tile in tiles:
                slot = len(stage_copies) % 2
                if len(stage_copies) >= 2:
                    stage_copies[-2].wait()
                at_rows = pl.ds(tile * 256, 256)
                value = dot_nt(cross_k[at_rows, :half_cols], weights[0])
                value += dot_nt(cross_k[at_rows, half_cols:], weights[1])
                value += dot_nt(cross_v[at_rows, :half_cols], weights[2])
                value += dot_nt(cross_v[at_rows, half_cols:], weights[3])
                staged[slot] = value.astype(BF16)
                copy = pltpu.make_async_copy(
                    staged.at[slot],
                    r["memory_grad"].at[at_rows, pl.ds(half * half_cols, half_cols)],
                    stage_sem.at[slot],
                )
                copy.start()
                stage_copies.append(copy)

        return run


    every = (far_all, pl.ds(0, 2), pl.ds(0, 2), pl.ds(0, 2))
    wbuf, wquarter = r["wbuf"], r["wquarter"]
    wslots = wbuf.shape[0]
    uses = {"column": 0, "quarter": 0}

    def next_slot(kind, slots):
        uses[kind] += 1
        return (uses[kind] - 1) % slots

    def column_load(a, col):
        slot = next_slot("column", wslots)
        src = whole[a].at[(*every, pl.ds(0, rows), pl.ds(col, COLS))]
        return dict(buffer=wbuf.at[slot], takes=[slot], copies=[(src, wbuf.at[slot])])

    def quarter_load(j):
        slot = next_slot("quarter", 2)
        src = whole[FDOWN].at[(*every, pl.ds(0, down_rows), pl.ds(j * 256, 256))]
        return dict(buffer=wquarter.at[slot], takes=[wslots + slot], copies=[(src, wquarter.at[slot])])

    def group_load(i):
        slot = next_slot("quarter", 2)
        copies = [
            (
                whole[FDOWN].at[(pl.ds(i * zs, zs), *every[1:], pl.ds(0, down_rows), pl.ds(q * 256, 256))],
                wquarter.at[slot, pl.ds(q * zs, zs)],
            )
            for q in range(4)
        ]
        return dict(buffer=wquarter.at[slot], takes=[wslots + slot], copies=copies)

    def half_load(i):
        copies = [
            (
                whole[CQKV].at[
                    (pl.ds(i * zh, zh), *every[1:], pl.ds(0, rows), pl.ds(width + c * COLS, COLS))
                ],
                wbuf.at[2 * i + c // 2, pl.ds(c % 2 * zh, zh)],
            )
            for c in range(4)
        ]
        return dict(buffer=wbuf.at[pl.ds(2 * i, 2)], takes=[2 * i, 2 * i + 1], copies=copies)

    chunks, index = gather_chunks([s.shape for s in shards])
    count = len(chunks)
    per_half = width // COLS
    forward = []
    backward = []

    def piece(pieces, cost, run, load=None, dep=0, name=None):
        pieces.append(dict(cost=cost, run=run, load=load, dep=dep, name=name))

    def down_dep(j):
        return index[(FDOWN, down_rows - rows, j * 256 // COLS * COLS)]

    piece(forward, 4.0, take_vectors, None, 0)
    for j in range(3 * width // COLS):
        piece(forward, 0.7, self_project(j), column_load(SQKV, j * COLS), index[(SQKV, 0, j * COLS)])
    for first in range(0, samples * pairs, 8):
        piece(forward, 1.5, self_attend(first, first + 8), None, 0)
    for j in range(per_half):
        piece(forward, 0.7, branch(self_attn, SELF_O, j), column_load(SOUT, j * COLS), index[(SOUT, 0, j * COLS)])
    piece(forward, 1.5, norm_one)
    piece(forward, 1.0, turn(x_in))
    piece(forward, 1.0, turn(self_attn))
    for target, at, first in ((cross_k, None, width), (cross_v, CROSS_V, 2 * width)):
        for j in range(per_half):
            col = first + j * COLS
            piece(forward, 3.0, cross_project(target, at, j), column_load(CQKV, col), index[(CQKV, 0, col)])
    for j in range(per_half):
        piece(forward, 0.7, cross_query(j), column_load(CQKV, j * COLS), index[(CQKV, 0, j * COLS)])
    piece(forward, 1.0, turn(h1_low))
    for s in range(samples):
        piece(forward, 2.5, turn_memory(s))
    for first in range(0, samples * pairs, 4):
        piece(forward, 2.5, cross_attend(first, first + 4))
    for j in range(per_half):
        piece(forward, 0.7, branch(cross_attn, CROSS_O, j), column_load(COUT, j * COLS), index[(COUT, 0, j * COLS)])
    piece(forward, 1.5, norm_two)
    piece(forward, 1.0, turn(cross_attn))
    for j in range(hidden // COLS):
        piece(forward, 1.5, feed_up(j), column_load(FUP, j * COLS), index[(FUP, 0, j * COLS)])
    piece(forward, 1.0, turn(h2_low))
    for j in range(width // 256):
        piece(forward, 0.8, feed_down(j), quarter_load(j), down_dep(j))
    piece(forward, 2.0, norm_three)

    for i in range(4):
        piece(backward, 1.5, pre_back(i), group_load(i), name="pre%d" % i)
    for j in range(hidden // COLS):
        piece(backward, 0.8, flow_back(slope, 0, j), column_load(FUP, j * COLS))
    piece(backward, 1.5, norm_two_back, name="norm2")
    for j in range(per_half):
        piece(backward, 0.8, attn_back(d_cross, j), column_load(COUT, j * COLS))
    for first in range(0, samples * pairs, 2):
        piece(backward, 2.5, cross_attend_back(first, first + 2), name="cross")
    for j in range(per_half):
        piece(backward, 0.8, flow_back(cross_q, 0, j), column_load(CQKV, j * COLS))
    piece(backward, 1.5, norm_one_back, name="norm1")
    for j in range(per_half):
        piece(backward, 0.8, attn_back(d_self, j), column_load(SOUT, j * COLS))
    for first in range(0, samples * pairs, 8):
        piece(backward, 2.0, self_attend_back(first, first + 8), name="self")
    piece(backward, 3.0, vector_sums, name="vectors")
    for j in range(3 * width // COLS):
        piece(backward, 0.8, flow_back(qkv, 0, j), column_load(SQKV, j * COLS))
    piece(backward, 0.5, target_done)
    tile_count = samples * mem_len // 256
    for half in range(2):
        for first in range(0, tile_count, 2):
            piece(backward, 2.5, memory_back(half, range(first, first + 2)), ("keep", half_load(half))[first == 0])

    def prepare(pieces, holders):
        last = None
        for p in pieces:
            p["done"] = p["started"] = False
            p["copies"], p["after"], p["buffer"] = [], [], None
            if p["load"] == "keep":
                p["buffer"] = last["buffer"]
                for slot in last["load"]["takes"]:
                    holders[slot] = p
            elif p["load"] is not None:
                p["buffer"] = p["load"]["buffer"]
                for slot in p["load"]["takes"]:
                    if slot in holders:
                        p["after"].append(holders[slot])
                    holders[slot] = p
                for n, (src, dst) in enumerate(p["load"]["copies"]):
                    sem = r["load_sem"].at[p["load"]["takes"][0], n]
                    p["copies"].append(pltpu.make_async_copy(src, dst, sem))
                last = p

    def start(p):
        for copy in p["copies"]:
            if not p["started"]:
                copy.start()
        p["started"] = True

    def look_ahead(pieces, ready):
        for later in pieces[:AHEAD]:
            if later["dep"] > ready:
                break
            if not later["started"] and all(p["done"] for p in later["after"]):
                start(later)

    def run_piece(pieces, ready):
        p = pieces.pop(0)
        start(p)
        look_ahead(pieces, ready)
        for copy in p["copies"]:
            copy.wait()
        if p["buffer"] is not None:
            p["run"](p["buffer"])
        else:
            p["run"]()
        p["done"] = True
        return p

    def work(pieces, ready, limit):
        spent = 0.0
        look_ahead(pieces, ready)
        while pieces and pieces[0]["dep"] <= ready and spent < limit:
            spent += run_piece(pieces, ready)["cost"]

    holders = {}
    prepare(forward, holders)
    prepare(backward, holders)


    in_copies = [
        pltpu.make_async_copy(r["mem_hbm"], mem, r["in_sem"].at[0]),
        pltpu.make_async_copy(r["cot_hbm"], cot, r["in_sem"].at[1]),
        pltpu.make_async_copy(r["x_hbm"], x_in, r["in_sem"].at[2]),
    ]

    def block(ref, k, *lead):
        _, row, row_count, col, cols = chunks[k]
        return ref.at[(*lead, pl.ds(row, row_count), pl.ds(col, cols))]

    def gathered(k, *lead):
        return block(whole[chunks[k][0]], k, *lead)

    local = []
    for a in range(7):
        copy = pltpu.make_async_copy(shards[a], whole[a].at[far, y, core, x], r["local_sem"].at[a])
        copy.start()
        local.append(copy)
    greet(me)
    for copy in in_copies:
        copy.start()

    sent = []

    def go(copy):
        copy.start()
        sent.append(copy)
        return copy

    far_copies, near_copies, other_copies, pass_copies, twin_copies = {}, {}, {}, {}, {}
    last_lane = far_count - 1
    gsend, grecv = r["gsend"], r["grecv"]

    def send(k, lane, ref, device):
        return go(remote(ref, ref, gsend.at[k, lane], grecv.at[k, lane], device))

    def start_far(k):
        far_copies[k] = [
            go(
                remote(
                    block(shards[chunks[k][0]], k),
                    gathered(k, far, y, core, x),
                    gsend.at[k, d],
                    grecv.at[k, d],
                    device,
                )
            )
            for d, (_, device) in enumerate(me["far_devices"])
        ]

    def start_near(k):
        column = gathered(k, far_all, y, core, x)
        near_copies[k] = send(k, last_lane, column, me["near_device"])
        other_copies[k] = send(k, last_lane + 1, column, me["other_device"])

    def start_pass(k):
        pass_copies[k] = send(k, last_lane + 2, gathered(k, far_all, near[0], core, near[1]), me["other_device"])

    def start_twin(k):
        half = gathered(k, far_all, pl.ds(0, 2), core, pl.ds(0, 2))
        twin_copies[k] = send(k, last_lane + 3, half, me["twin_device"])

    skew = GATHER_SKEW
    for t in range(count + 3 * skew + 1):
        k = t - 3 * skew
        if 0 <= k < count:
            other_copies[k].wait_recv()
            pass_copies[k].wait_recv()
            start_twin(k)
        k = t - 2 * skew
        if 0 <= k < count:
            near_copies[k].wait_recv()
            start_pass(k)
        k = t - skew
        if 0 <= k < count:
            if k == 0:
                for copy in local:
                    copy.wait()
            for copy in far_copies[k]:
                copy.wait_recv()
            start_near(k)
        if t < count:
            start_far(t)
        k = t - 3 * skew - 1
        if k >= 0:
            if k == 0:
                for copy in in_copies:
                    copy.wait()
            twin_copies[k].wait_recv()
            work(forward, k, STEP_WORK)
    work(forward, count, 1e9)
    for copy in sent:
        copy.wait_send()


    own, total, from_other, from_near, from_far = (
        r[n] for n in ("own", "total", "from_other", "from_near", "from_far")
    )
    small_buffers = (r["small_pack"], r["total_s"], r["from_other_s"], r["from_near_s"], r["from_far_s"])
    out_chunks = scatter_chunks(width)
    out_count = len(out_chunks)
    skew = SCATTER_SKEW
    own_slots, total_slots, land_slots = own.shape[0], total.shape[0], from_other.shape[0]
    ssend, srecv = r["ssend"], r["srecv"]

    def buffers(k):
        if out_chunks[k][0] == SMALL:
            return small_buffers
        return (
            own.at[k % own_slots],
            total.at[k % total_slots],
            from_other.at[k % land_slots],
            from_near.at[k % land_slots],
            from_far.at[k % land_slots],
        )

    def compute(k):
        a, col = out_chunks[k]
        if a == SMALL:
            return
        target = buffers(k)[0]
        if a == FDOWN:
            right = d_ffn[:, pl.ds(col, 128)]

            def body(i, carry):
                left = act_t[pl.ds(pl.multiple_of(i * 256, 256), 256), :]
                value = dot(left, right).astype(BF16)
                for piece_at in range(0, 256, rows):
                    b = i * (256 // down_rows) + piece_at // down_rows
                    q = piece_at % down_rows // rows
                    target[b // 8, (b // 4) % 2, (b // 2) % 2, b % 2, :, q * 128 : (q + 1) * 128] = value[
                        piece_at : piece_at + rows
                    ]
                return carry

            lax.fori_loop(0, hidden // 256, body, 0)
            return
        left, right = {
            FUP: (h2_low, slope),
            COUT: (cross_attn, d_cross),
            SOUT: (self_attn, d_self),
            SQKV: (x_in, qkv),
            CQKV: (
                (h1_low, cross_q),
                (mem, cross_k),
                (mem, cross_v),
            )[col // width if a == CQKV else 0],
        }[a]
        first = col % width if a == CQKV else col
        cols_at = pl.ds(first, COLS)

        def body(i, carry):
            at = pl.ds(pl.multiple_of(i * 256, 256), 256)
            if left is mem:
                value = None
                for s in range(samples):
                    keys_at = pl.ds(s * mem_len, mem_len)
                    feature_rows = pl.ds(pl.multiple_of(s * mem_len + i * 256, 256), 256)
                    part = dot(mem[feature_rows, :], right[keys_at, cols_at])
                    value = part if value is None else value + part
            else:
                value = dot(left[:, at], right[:, cols_at])
            value = value.astype(BF16)
            for j in range(256 // rows):
                target[i * (256 // rows) // 8 + j // 8, (j // 4) % 2, (j // 2) % 2, j % 2] = value[
                    j * rows : (j + 1) * rows
                ]
            return carry

        lax.fori_loop(0, width // 256, body, 0)

    twins, others, nears, fars = {}, {}, {}, {}

    def start_twin_sum(k):
        target, landing = buffers(k)[:2]
        twins[k] = remote(
            target.at[far_all, pl.ds(0, 2), 1 - core, pl.ds(0, 2)],
            landing,
            ssend.at[k, 0],
            srecv.at[k, 0],
            me["twin_device"],
        )
        twins[k].start()

    def add_own(k):
        mine, running = buffers(k)[:2]

        def body(i, carry):
            f, yy, xx = i // 4, (i // 2) % 2, i % 2
            running[f, yy, xx] = running[f, yy, xx] + mine[f, yy, core, xx]
            return carry

        lax.fori_loop(0, far_count * 4, body, 0)

    def start_others(k):
        running, landing = buffers(k)[1:3]
        others[k] = []
        for i, place in enumerate((diagonal, other)):
            copy = remote(
                running.at[far_all, place[0], place[1]],
                landing.at[i],
                ssend.at[k, 1 + i],
                srecv.at[k, 1 + i],
                me["other_device"],
            )
            copy.start()
            others[k].append(copy)

    def add_other(k, i):
        running, landing = buffers(k)[1:3]
        place = (near, (y, x))[i]

        def body(f, carry):
            running[f, place[0], place[1]] = running[f, place[0], place[1]] + landing[i, f]
            return carry

        lax.fori_loop(0, far_count, body, 0)

    def start_near_sum(k):
        _, running, _, landing, _ = buffers(k)
        nears[k] = remote(
            running.at[far_all, near[0], near[1]],
            landing,
            ssend.at[k, 3],
            srecv.at[k, 3],
            me["near_device"],
        )
        nears[k].start()

    def add_near(k):
        _, running, _, landing, _ = buffers(k)

        def body(f, carry):
            running[f, y, x] = running[f, y, x] + landing[f]
            return carry

        lax.fori_loop(0, far_count, body, 0)

    def start_fars(k):
        _, running, _, _, landing = buffers(k)
        fars[k] = []
        for d, (target, device) in enumerate(me["far_devices"]):
            copy = remote(running.at[target, y, x], landing.at[d], ssend.at[k, 4 + d], srecv.at[k, 4 + d], device)
            copy.start()
            fars[k].append(copy)

    def finish(k):
        _, running, _, _, landing = buffers(k)
        a, col = out_chunks[k]
        result = running[far, y, x].astype(F32)
        for d in range(far_count - 1):
            result += landing[d].astype(F32)
        if a == SMALL:
            lane = (far * 8 + y * 4 + core * 2 + x) * rows % 128
            up_lane = (far * 8 + y * 4 + core * 2 + x) * down_rows % 128
            vectors = pltpu.roll(result, (128 - lane) % 128, 1)
            ups = pltpu.roll(result, (128 - up_lane) % 128, 1)
            row = lax.broadcasted_iota(jnp.int32, result.shape, 0)
            sums[a][...] = jnp.where(row == VECTORS, ups, vectors)
        elif a == FDOWN:
            for q in range(4):
                sums[a][q * rows : (q + 1) * rows, pl.ds(col, 128)] = result[:, q * 128 : (q + 1) * 128]
        else:
            sums[a][:, pl.ds(col, COLS)] = result
        for copy in (*others[k], nears[k], *fars[k]):
            copy.wait_send()

    needs = {FUP: "pre3", COUT: "norm2", CQKV: "cross", SOUT: "norm1", SQKV: "self", SMALL: "vectors"}

    for t in range(out_count + 4 * skew):
        k = t - 4 * skew
        if 0 <= k < out_count:
            for copy in fars[k]:
                copy.wait_recv()
            finish(k)
        k = t - 3 * skew
        if 0 <= k < out_count:
            nears[k].wait_recv()
            add_near(k)
            start_fars(k)
        k = t - 2 * skew
        if 0 <= k < out_count:
            others[k][0].wait_recv()
            add_other(k, 0)
            start_near_sum(k)
            others[k][1].wait_recv()
            add_other(k, 1)
        k = t - skew
        if 0 <= k < out_count:
            twins[k].wait()
            add_own(k)
            start_others(k)
        if t < out_count:
            need = needs.get(out_chunks[t][0])
            while any(p["name"] == need for p in backward if need):
                run_piece(backward, count)
            compute(t)
            start_twin_sum(t)
        work(backward, count, STEP_WORK)
    work(backward, count, 1e9)
    for copy in stage_copies[-2:]:
        copy.wait()


def layer(mesh, target_input, memory, cotangent, mem_lengths, tgt_lengths, shards, small):
    samples, tgt_len, width = target_input.shape
    mem_len = memory.shape[1]
    far_count = mesh.shape["wide"] // 4
    rows = shards[SQKV].shape[0]
    tokens, keys, hidden = samples * tgt_len, samples * mem_len, 4 * width
    lanes = far_count + 3
    count = len(gather_chunks([s.shape for s in shards])[0])
    out_count = len(scatter_chunks(width))
    lead = (far_count, 2, 2, 2)
    shrink = 1 if rows >= 16 else 2
    total_slots, land_slots, own_slots = 5 * SCATTER_SKEW + 1, 2 * SCATTER_SKEW + 1, SCATTER_SKEW + 1

    def vmem(shape, dtype=BF16):
        return pltpu.VMEM(shape, dtype)

    small_sum = (SMALL_ROWS, 128)
    scratch = [
        vmem((tokens, width)),
        vmem((keys, width)),
        vmem((tokens, width)),
        vmem((tokens, 3 * width)),
        vmem((tokens, width)),
        vmem((tokens, width), F32),
        vmem((tokens, 1), F32),
        vmem((tokens, width), F32),
        vmem((tokens, width)),
        vmem((tokens, width)),
        vmem((keys, width)),
        vmem((keys, width)),
        vmem((tokens, width)),
        vmem((tokens, width), F32),
        vmem((tokens, 1), F32),
        vmem((tokens, width), F32),
        vmem((tokens, width)),
        vmem((tokens, hidden)),
        vmem((hidden, tokens)),
        vmem((tokens, hidden)),
        vmem((tokens, width), F32),
        vmem((tokens, width)),
        vmem((tokens, width)),
        vmem((tokens, width)),
        vmem((tokens, width)),
        vmem((samples * HEADS // 2, 2 * tgt_len), F32),
        vmem((samples * HEADS // 2, 2 * tgt_len), F32),
        vmem((24, width), F32),
        vmem((24, width), F32),
        vmem((2, 256, width // 2)),
        vmem((4,) + lead + (rows, COLS)),
        vmem((2,) + lead + (4 * rows, 256)),
        vmem(lead + (SMALL_ROWS, 128)),
        vmem((SMALL_ROWS, mesh.size, 128), F32),
        vmem(lead + small_sum, F32),
        vmem((own_slots,) + lead + (rows, COLS)),
        vmem((total_slots, far_count, 2, 2, rows, COLS)),
        vmem((land_slots, 2, far_count, rows, COLS)),
        vmem((land_slots, far_count, rows, COLS)),
        vmem((land_slots, far_count - 1, rows, COLS)),
        vmem((far_count, 2, 2) + small_sum, F32),
        vmem((2, far_count) + small_sum, F32),
        vmem((far_count,) + small_sum, F32),
        vmem((far_count - 1,) + small_sum, F32),
        pltpu.SemaphoreType.DMA((6, 4)),
        pltpu.SemaphoreType.DMA((3,)),
        pltpu.SemaphoreType.DMA((7,)),
        pltpu.SemaphoreType.DMA((count, lanes)),
        pltpu.SemaphoreType.DMA((count, lanes)),
        pltpu.SemaphoreType.DMA((out_count, lanes)),
        pltpu.SemaphoreType.DMA((out_count, lanes)),
        pltpu.SemaphoreType.DMA((2,)),
    ]
    in_vmem, anywhere = pl.BlockSpec(memory_space=pltpu.VMEM), pl.BlockSpec(memory_space=pl.ANY)
    in_smem = pl.BlockSpec(memory_space=pltpu.SMEM)
    out_shape = [
        jax.ShapeDtypeStruct((tokens, width), BF16),
        jax.ShapeDtypeStruct((tokens, width), BF16),
        jax.ShapeDtypeStruct((keys, width), BF16),
    ]
    out_shape += [jax.ShapeDtypeStruct(s.shape, F32) for s in shards]
    out_shape += [jax.ShapeDtypeStruct(small_sum, F32)]
    out_shape += [jax.ShapeDtypeStruct(lead + s.shape, BF16) for s in shards]
    outs = pl.pallas_call(
        functools.partial(layer_kernel, (far_count, rows, width, samples, tgt_len, mem_len)),
        out_shape=out_shape,
        in_specs=[anywhere, anywhere, anywhere, in_smem, in_smem] + [in_vmem] * 7,
        out_specs=[in_vmem, in_vmem, anywhere] + [in_vmem] * 7 + [anywhere] * 6,
        scratch_shapes=scratch,
        compiler_params=pltpu.CompilerParams(
            collective_id=0, has_side_effects=True, vmem_limit_bytes=63 * 2**20
        ),
        cost_estimate=pl.CostEstimate(flops=52 * 10**9, bytes_accessed=10**8, transcendentals=10**7),
        name="decoder_layer",
    )(
        target_input.reshape(tokens, width),
        memory.reshape(keys, width),
        cotangent.reshape(tokens, width),
        mem_lengths,
        tgt_lengths,
        *shards,
        small,
    )
    return outs[:10]


def step(
    mesh,
    target_input,
    memory,
    cotangent,
    mem_lengths,
    tgt_lengths,
    self_qkv,
    self_out,
    self_bias,
    norm1_gain,
    norm1_shift,
    cross_qkv,
    cross_out,
    cross_bias,
    norm2_gain,
    norm2_shift,
    ffn_up,
    up_bias,
    ffn_down,
    down_bias,
    norm3_gain,
    norm3_shift,
):
    per, up_per = norm1_gain.shape[0], up_bias.shape[0]
    small = jnp.zeros((SMALL_ROWS, 128), BF16)
    row = 0
    for v in (
        self_bias, norm1_gain, norm1_shift, cross_bias, norm2_gain, norm2_shift,
        down_bias, norm3_gain, norm3_shift, up_bias,
    ):
        v = v.reshape(-1, v.shape[-1])
        small += jnp.pad(v, ((row, SMALL_ROWS - row - v.shape[0]), (0, 128 - v.shape[1])))
        row += v.shape[0]
    block_out, target_grad, memory_grad, *grads, sums = layer(
        mesh, target_input, memory, cotangent, mem_lengths, tgt_lengths,
        [self_qkv, self_out, cross_qkv, cross_out, ffn_up, ffn_down], small,
    )
    return (
        block_out.reshape(target_input.shape),
        target_grad.reshape(target_input.shape),
        memory_grad.reshape(memory.shape),
        grads[SQKV],
        grads[SOUT],
        sums[SELF_Q : SELF_Q + 3, :per],
        sums[GAIN1, :per],
        sums[SHIFT1, :per],
        grads[CQKV],
        grads[COUT],
        sums[CROSS_Q : CROSS_Q + 3, :per],
        sums[GAIN2, :per],
        sums[SHIFT2, :per],
        grads[FUP],
        sums[VECTORS, :up_per],
        grads[FDOWN],
        sums[DOWN, :per],
        sums[GAIN3, :per],
        sums[SHIFT3, :per],
    )


def solution(mesh):
    both = ("wide", "narrow")
    stream, matrix_spec, vector_spec, bias_spec = P(both, None, None), P(both, None), P(both), P(None, both)
    weights = (
        matrix_spec, matrix_spec, bias_spec, vector_spec, vector_spec,
        matrix_spec, matrix_spec, bias_spec, vector_spec, vector_spec,
        matrix_spec, vector_spec, matrix_spec, vector_spec, vector_spec, vector_spec,
    )
    return jax.shard_map(
        functools.partial(step, mesh),
        mesh=mesh,
        in_specs=(stream, stream, stream, vector_spec, vector_spec) + weights,
        out_specs=(stream, stream, stream) + weights,
        check_vma=False,
    )
```

```python
import functools
import math

import jax
import jax.numpy as jnp
from jax import lax
from jax.experimental import pallas as pl
from jax.experimental.pallas import tpu as pltpu
from jax.sharding import PartitionSpec as P

MESH = pl.DeviceIdType.MESH
HEADS = 16
HEAD_DIM = 64
NORM_EPSILON = 1e-05
MASK_VALUE = -1e30
COLS = 512
GATHER_SKEW = 2
SCATTER_SKEW = 2
FORWARD_WORK = 1.5
BACKWARD_WORK = 1.5
GATHER_CROSSED = (0, 0, 1)
SCATTER_CROSSED = (0, 0, 1)
AHEAD = 8
SMALL_ROWS = 16

F32 = jnp.float32
BF16 = jnp.bfloat16

SELF_Q, SELF_V, SELF_O, GAIN1, SHIFT1, CROSS_Q, CROSS_V, CROSS_O, GAIN2, SHIFT2, DOWN, GAIN3, SHIFT3, UP = range(14)
VECTORS = 13


def dot(a, b):
    return lax.dot_general(a, b, (((1,), (0,)), ((), ())), preferred_element_type=F32)


def dot_nt(a, b):
    return lax.dot_general(a, b, (((1,), (1,)), ((), ())), preferred_element_type=F32)


def dot_tn(a, b):
    return lax.dot_general(a, b, (((0,), (0,)), ((), ())), preferred_element_type=F32)


def places(far_count):
    wide = lax.axis_index("wide")
    x = lax.axis_index("narrow")
    far = wide // 4
    y = (wide // 2) % 2
    core = wide % 2
    near_y = y + core * (1 - 2 * y)
    near_x = x + (1 - core) * (1 - 2 * x)
    other_y = y + (1 - core) * (1 - 2 * y)
    other_x = x + core * (1 - 2 * x)

    def device(f, yy, cc, xx):
        return (f * 4 + yy * 2 + cc, xx)

    return dict(
        far=far,
        y=y,
        core=core,
        x=x,
        near=(near_y, near_x),
        other=(other_y, other_x),
        diagonal=(1 - y, 1 - x),
        near_device=device(far, near_y, core, near_x),
        other_device=device(far, other_y, core, other_x),
        twin_device=device(far, y, 1 - core, x),
        far_devices=[
            (lax.rem(far + d, far_count), device(lax.rem(far + d, far_count), y, core, x))
            for d in range(1, far_count)
        ],
    )


def greet(where):
    barrier = pltpu.get_barrier_semaphore()
    partners = [where["near_device"], where["other_device"], where["twin_device"]]
    partners += [device for _, device in where["far_devices"]]
    for device in partners:
        pl.semaphore_signal(barrier, inc=1, device_id=device, device_id_type=MESH)
    pl.semaphore_wait(barrier, len(partners))


def remote(src, dst, send_sem, recv_sem, device):
    return pltpu.make_async_remote_copy(
        src_ref=src,
        dst_ref=dst,
        send_sem=send_sem,
        recv_sem=recv_sem,
        device_id=device,
        device_id_type=MESH,
    )


def matrix(value):
    rows, cols = value.shape[-2:]
    if rows % 16:
        return value.astype(F32).reshape(-1, cols).astype(BF16)
    return value.reshape(-1, cols)


ARRAYS = ("self_qkv", "self_out", "cross_qkv", "cross_out", "ffn_up", "ffn_down")
SQKV, SOUT, CQKV, COUT, FUP, FDOWN, SMALL = range(7)


def crossed(far_count, pattern, array, k):
    return far_count == 4 and array != SMALL and pattern[k % len(pattern)] == 1


def gather_chunks(shapes):
    rows = shapes[SQKV][0]
    width = shapes[SOUT][1]
    chunks = [(SMALL, 0, SMALL_ROWS, 0, 128)]
    for a, first, last in (
        (SQKV, 0, 3 * width),
        (SOUT, 0, width),
        (CQKV, width, 3 * width),
        (CQKV, 0, width),
        (COUT, 0, width),
        (FUP, 0, 4 * width),
    ):
        chunks += [(a, 0, rows, col, COLS) for col in range(first, last, COLS)]
    for col in range(0, width, COLS):
        chunks += [(FDOWN, row, rows, col, COLS) for row in range(0, 4 * rows, rows)]
    index = {(a, row, col): k for k, (a, row, _, col, _) in enumerate(chunks)}
    return chunks, index


def scatter_chunks(width):
    chunks = [(FDOWN, 128 * j) for j in range(width // 128)]
    for a, first, last in (
        (FUP, 0, 4 * width),
        (COUT, 0, width),
        (CQKV, 0, 3 * width),
        (SOUT, 0, width),
    ):
        chunks += [(a, col) for col in range(first, last, COLS)]
    chunks += [(SMALL, 0)]
    chunks += [(SQKV, col) for col in range(0, 3 * width, COLS)]
    return chunks


def layer_kernel(cfg, *refs):
    far_count, rows, width, samples, tgt_len, mem_len = cfg
    devices = 8 * far_count
    hidden = 4 * width
    down_rows = 4 * rows
    tokens = samples * tgt_len
    pairs = HEADS // 2
    scale = 1.0 / math.sqrt(HEAD_DIM)
    zs = max(1, far_count // 4)
    zh = max(1, far_count // 2)

    names = (
        "x_hbm", "mem_hbm", "cot_hbm", "mem_lengths", "tgt_lengths", "i0", "i1", "i2", "i3", "i4", "i5", "i6",
        "block_out", "target_grad", "memory_grad", "g0", "g1", "g2", "g3", "g4", "g5", "small_out", "w0", "w1",
        "w2", "w3", "w4", "w5", "x", "mem", "cot", "qkv", "self_attn", "n1", "r1", "h1", "h1_low", "cross_q",
        "cross_k", "cross_v", "cross_attn", "n2", "r2", "flow", "h2_low", "act", "act_t", "slope", "acc", "d_ffn",
        "d_cross", "d_attn", "d_self", "self_lse", "cross_lse", "vecs", "gvecs", "staged", "wbuf", "wquarter",
        "small_in", "small_rows", "small_pack", "own", "total", "from_other", "from_near", "from_far",
        "from_near_far", "total_s", "from_other_s", "from_near_s", "from_far_s", "load_sem", "in_sem", "local_sem",
        "gsend", "grecv", "ssend", "srecv", "stage_sem",
    )
    r = dict(zip(names, refs, strict=True))
    x_in, mem, cot = r["x"], r["mem"], r["cot"]
    qkv, self_attn, n1, r1, h1, h1_low = (r[n] for n in ("qkv", "self_attn", "n1", "r1", "h1", "h1_low"))
    cross_q, cross_k, cross_v, cross_attn = (r[n] for n in ("cross_q", "cross_k", "cross_v", "cross_attn"))
    n2, r2, flow, h2_low = (r[n] for n in ("n2", "r2", "flow", "h2_low"))
    act, act_t, slope, acc = (r[n] for n in ("act", "act_t", "slope", "acc"))
    d_ffn, d_cross, d_attn, d_self = (r[n] for n in ("d_ffn", "d_cross", "d_attn", "d_self"))
    vecs, gvecs = r["vecs"], r["gvecs"]
    shards = [r["i%d" % i] for i in range(7)]
    whole = [r["w%d" % i] for i in range(6)] + [r["small_in"]]
    sums = [r["g%d" % i] for i in range(6)] + [r["small_out"]]

    me = places(far_count)
    far, y, core, x = me["far"], me["y"], me["core"], me["x"]
    far_all = pl.ds(0, far_count)
    near, other, diagonal = me["near"], me["other"], me["diagonal"]

    def vec(i, col=0, cols=width):
        return vecs[pl.ds(i, 1), pl.ds(col, cols)]


    def owner_of(per, first):
        device = lax.broadcasted_iota(jnp.int32, (devices, width), 0)
        column = lax.broadcasted_iota(jnp.int32, (devices, width), 1) + first
        return lax.shift_right_logical(column, per.bit_length() - 1) == device

    def spread_of(per):
        lane = lax.broadcasted_iota(jnp.int32, (128, width), 0)
        column = lax.broadcasted_iota(jnp.int32, (128, width), 1)
        return (lane == jnp.bitwise_and(column, per - 1)).astype(F32).astype(BF16)

    def take_vectors():
        small_in, table = r["small_in"], r["small_rows"]

        def body(b, carry):
            tile = small_in[b // 8, (b // 4) % 2, (b // 2) % 2, b % 2].astype(F32)
            for i in range(VECTORS + 1):
                table[i, pl.ds(b, 1), :] = tile[i : i + 1]
            return carry

        lax.fori_loop(0, devices, body, 0)
        spread, owner = spread_of(rows), owner_of(rows, 0)
        for i in range(VECTORS):
            values = dot(table[i].astype(BF16), spread)
            vecs[pl.ds(i, 1), :] = jnp.sum(jnp.where(owner, values, 0.0), axis=0, keepdims=True)
        values = dot(table[VECTORS].astype(BF16), spread_of(down_rows))
        for j in range(4):
            owner = owner_of(down_rows, j * width)
            vecs[pl.ds(UP + j, 1), :] = jnp.sum(jnp.where(owner, values, 0.0), axis=0, keepdims=True)

    def pack_vectors():
        pack = r["small_pack"]

        pack[...] = jnp.zeros_like(pack)
        for b in range(devices):
            lead = (b // 8, (b // 4) % 2, (b // 2) % 2, b % 2)
            lane, up_lane = b * rows // 128 * 128, b * down_rows % width // 128 * 128
            up_row = UP + b * down_rows // width
            pack[(*lead, slice(0, VECTORS))] = gvecs[0:VECTORS, lane : lane + 128]
            pack[(*lead, slice(VECTORS, VECTORS + 1))] = gvecs[up_row : up_row + 1, up_lane : up_lane + 128]

    def turn(ref, first=0, cols=width):
        def run():
            def body(i, carry):
                cols_at = pl.ds(pl.multiple_of(first + i * 256, 256), 256)
                ref[:, cols_at] = ref[:, cols_at].T
                return carry

            lax.fori_loop(0, cols // 256, body, 0)

        return run

    def turn_memory(s, i):
        def run():
            blocks = width // 256

            def at(i, j):
                return (
                    pl.ds(pl.multiple_of(s * mem_len + i * 256, 256), 256),
                    pl.ds(pl.multiple_of(j * 256, 256), 256),
                )

            mem[at(i, i)] = mem[at(i, i)].T
            for j in range(i + 1, blocks):
                upper, lower = mem[at(i, j)].T, mem[at(j, i)].T
                mem[at(i, j)] = lower
                mem[at(j, i)] = upper

        return run

    def self_project(j):
        def run(w):
            value = dot(x_in[...], matrix(w[...]))
            cols = pl.ds(j * COLS, COLS)
            part, first = j * COLS // width, j * COLS % width
            if part == 0:
                value = (value + vec(SELF_Q, first, COLS)) * scale
            if part == 2:
                value = value + vec(SELF_V, first, COLS)
            qkv[:, cols] = value.astype(BF16)

        return run

    def head_masks():
        lane = lax.broadcasted_iota(jnp.int32, (1, 128), 1)
        low = (lane < HEAD_DIM).astype(F32).astype(BF16)
        return low, (lane >= HEAD_DIM).astype(F32).astype(BF16)

    def both_heads(two):
        low, high = head_masks()
        return jnp.concatenate([two * low, two * high], axis=0)

    def one_row_each(stacked):
        lane = lax.broadcasted_iota(jnp.int32, (tgt_len, 128), 1)
        return jnp.where(lane < HEAD_DIM, stacked[:tgt_len], stacked[tgt_len:])

    def scores_of(keys, queries, length, causal):
        scores = dot_nt(keys, queries)
        key = lax.broadcasted_iota(jnp.int32, scores.shape, 0)
        usable = key < length
        if causal:
            query = jnp.bitwise_and(lax.broadcasted_iota(jnp.int32, scores.shape, 1), tgt_len - 1)
            usable = usable & (key <= query)
        return jnp.where(usable, scores, MASK_VALUE)

    def attend(u, queries, q_at, keys, k_at, values, v_at, key_count, lengths, causal, out, lse):
        s, pair = u // pairs, u % pairs
        lane = pair * 128
        q_rows = pl.ds(pl.multiple_of(s * tgt_len, tgt_len), tgt_len)
        k_rows = pl.ds(pl.multiple_of(s * key_count, key_count), key_count)

        def cols(first):
            return pl.ds(pl.multiple_of(first + lane, 128), 128)

        stacked = both_heads(queries[q_rows, cols(q_at)])
        scores = scores_of(keys[k_rows, cols(k_at)], stacked, lengths[s], causal)
        peak = jnp.max(scores, axis=0, keepdims=True)
        exponentials = jnp.exp(scores - peak)
        total = jnp.sum(exponentials, axis=0, keepdims=True)
        probs = (exponentials * (1.0 / total)).astype(BF16)
        mixed = dot_tn(values[k_rows, cols(v_at)], probs)
        out[q_rows, cols(0)] = one_row_each(mixed.T).astype(BF16)
        lse[pl.ds(u, 1), :] = peak + jnp.log(total)

    def attend_back(u, queries, q_at, keys, k_at, values, v_at, key_count, lengths, causal, lse, value_sum):
        s, pair = u // pairs, u % pairs
        lane = pair * 128
        q_rows = pl.ds(pl.multiple_of(s * tgt_len, tgt_len), tgt_len)
        k_rows = pl.ds(pl.multiple_of(s * key_count, key_count), key_count)

        def cols(first):
            return pl.ds(pl.multiple_of(first + lane, 128), 128)

        stacked = both_heads(queries[q_rows, cols(q_at)])
        upstream = both_heads(d_attn[q_rows, cols(0)])
        key_rows = keys[k_rows, cols(k_at)]
        scores = scores_of(key_rows, stacked, lengths[s], causal)
        probs = jnp.exp(scores - lse[pl.ds(u, 1), :])
        prob_grad = dot_nt(values[k_rows, cols(v_at)], upstream)
        delta = jnp.sum(probs * prob_grad, axis=0, keepdims=True)
        score_grad = (probs * (prob_grad - delta)).astype(BF16)
        query_grad = dot_tn(key_rows, score_grad)
        value_grad = dot(probs.astype(BF16), upstream).astype(BF16)
        values[k_rows, cols(v_at)] = value_grad
        keys[k_rows, cols(k_at)] = dot(score_grad, stacked).astype(BF16)
        queries[q_rows, cols(q_at)] = (one_row_each(query_grad.T) * scale).astype(BF16)
        gvecs[pl.ds(value_sum, 1), cols(0)] += jnp.sum(value_grad.astype(F32), axis=0, keepdims=True)

    def self_attend(first, last):
        def body(u, carry):
            attend(u, qkv, 0, qkv, width, qkv, 2 * width, tgt_len, r["tgt_lengths"], True,
                   self_attn, r["self_lse"])
            return carry

        return lambda: lax.fori_loop(first, last, body, 0)

    def cross_attend(first, last):
        def body(u, carry):
            attend(u, cross_q, 0, cross_k, 0, cross_v, 0, mem_len, r["mem_lengths"], False,
                   cross_attn, r["cross_lse"])
            return carry

        return lambda: lax.fori_loop(first, last, body, 0)

    def self_attend_back(first, last):
        def body(u, carry):
            attend_back(u, qkv, 0, qkv, width, qkv, 2 * width, tgt_len, r["tgt_lengths"], True,
                        r["self_lse"], SELF_V)
            return carry

        return lambda: lax.fori_loop(first, last, body, 0)

    def cross_attend_back(first, last):
        def body(u, carry):
            attend_back(u, cross_q, 0, cross_k, 0, cross_v, 0, mem_len, r["mem_lengths"], False,
                        r["cross_lse"], CROSS_V)
            return carry

        return lambda: lax.fori_loop(first, last, body, 0)

    ROW_TILE = 64

    def over_rows(body):
        def step(i, carry):
            body(pl.ds(pl.multiple_of(i * ROW_TILE, ROW_TILE), ROW_TILE))
            return carry

        lax.fori_loop(0, tokens // ROW_TILE, step, 0)

    def normalise(summed):
        average = jnp.mean(summed, axis=-1, keepdims=True)
        centred = summed - average
        inverse = lax.rsqrt(jnp.mean(centred * centred, axis=-1, keepdims=True) + NORM_EPSILON)
        return centred * inverse, inverse

    def normalise_back(at, incoming, normed, inverse, gain):
        gvecs[pl.ds(at, 1), :] += jnp.sum(incoming * normed, axis=0, keepdims=True)
        gvecs[pl.ds(at + 1, 1), :] += jnp.sum(incoming, axis=0, keepdims=True)
        scaled = incoming * gain
        centred = (
            scaled
            - jnp.mean(scaled, axis=-1, keepdims=True)
            - normed * jnp.mean(scaled * normed, axis=-1, keepdims=True)
        )
        return centred * inverse

    def branch(attn, at, j):
        def run(w):
            cols = pl.ds(j * COLS, COLS)
            acc[:, cols] = dot(attn[...], matrix(w[...])) + vec(at, j * COLS, COLS)

        return run

    def norm_one():
        def body(at):
            normed, inverse = normalise(x_in[at, :].astype(F32) + acc[at, :])
            hidden_one = normed * vec(GAIN1) + vec(SHIFT1)
            n1[at, :] = normed
            r1[at, :] = inverse
            h1[at, :] = hidden_one
            h1_low[at, :] = hidden_one.astype(BF16)

        over_rows(body)

    def cross_query(j):
        def run(w):
            cols = pl.ds(j * COLS, COLS)
            value = (dot(h1_low[...], matrix(w[...])) + vec(CROSS_Q, j * COLS, COLS)) * scale
            cross_q[:, cols] = value.astype(BF16)

        return run

    def cross_project(target, at, j, first):
        def run(w):
            weight = matrix(w[...])

            def body(i, carry):
                at_rows = pl.ds(pl.multiple_of(i * 256, 256), 256)
                value = dot(mem[at_rows, :], weight)
                if at is not None:
                    value = value + vec(at, j * COLS, COLS)
                target[at_rows, pl.ds(j * COLS, COLS)] = value.astype(BF16)
                return carry

            lax.fori_loop(first, first + samples * mem_len // 512, body, 0)

        return run

    def norm_two():
        def body(at):
            normed, inverse = normalise(h1[at, :] + acc[at, :])
            hidden_two = normed * vec(GAIN2) + vec(SHIFT2)
            n2[at, :] = normed
            r2[at, :] = inverse
            flow[at, :] = hidden_two
            h2_low[at, :] = hidden_two.astype(BF16)

        over_rows(body)

    def feed_up(j):
        def run(w):
            row, first = UP + j * COLS // width, j * COLS % width
            cols = pl.ds(j * COLS, COLS)
            pre = dot(h2_low[...], matrix(w[...])) + vec(row, first, COLS)
            normal_cdf = 0.5 * (1.0 + lax.erf(pre * (1.0 / math.sqrt(2.0))))
            density = jnp.exp(-0.5 * pre * pre) * (1.0 / math.sqrt(2.0 * math.pi))
            low = (pre * normal_cdf).astype(BF16)
            act[:, cols] = low
            act_t[pl.ds(j * COLS, COLS), :] = low.T
            slope[:, cols] = (normal_cdf + pre * density).astype(BF16)

        return run

    def feed_down(j):
        def run(w):
            acc[:, pl.ds(j * 256, 256)] = dot(act[...], matrix(w[...])) + vec(DOWN, j * 256, 256)

        return run

    def norm_three():
        gvecs[...] = jnp.zeros_like(gvecs)

        def body(at):
            normed, inverse = normalise(flow[at, :] + acc[at, :])
            r["block_out"][at, :] = (normed * vec(GAIN3) + vec(SHIFT3)).astype(BF16)
            grad = normalise_back(GAIN3, cot[at, :].astype(F32), normed, inverse, vec(GAIN3))
            low = grad.astype(BF16)
            flow[at, :] = grad
            d_ffn[at, :] = low
            gvecs[pl.ds(DOWN, 1), :] += jnp.sum(low.astype(F32), axis=0, keepdims=True)

        over_rows(body)

    def pre_back(i):
        def run(w):
            cols = pl.ds(i * width, width)
            value = None
            for q in range(4):
                part = dot_nt(d_ffn[:, pl.ds(q * 256, 256)], matrix(w[q * zs : (q + 1) * zs]))
                value = part if value is None else value + part
            low = (value * slope[:, cols].astype(F32)).astype(BF16)
            slope[:, cols] = low
            gvecs[pl.ds(UP + i, 1), :] = jnp.sum(low.astype(F32), axis=0, keepdims=True)

        return run

    def flow_back(grads, first, j):
        def run(w):
            flow[...] += dot_nt(grads[:, pl.ds(first + j * COLS, COLS)], matrix(w[...]))

        return run

    def norm_two_back():
        def body(at):
            grad = normalise_back(GAIN2, flow[at, :], n2[at, :], r2[at, :], vec(GAIN2))
            low = grad.astype(BF16)
            flow[at, :] = grad
            d_cross[at, :] = low
            gvecs[pl.ds(CROSS_O, 1), :] += jnp.sum(low.astype(F32), axis=0, keepdims=True)

        over_rows(body)

    def norm_one_back():
        gvecs[pl.ds(CROSS_Q, 1), :] = jnp.sum(cross_q[...].astype(F32), axis=0, keepdims=True)

        def body(at):
            grad = normalise_back(GAIN1, flow[at, :], n1[at, :], r1[at, :], vec(GAIN1))
            low = grad.astype(BF16)
            flow[at, :] = grad
            d_self[at, :] = low
            gvecs[pl.ds(SELF_O, 1), :] += jnp.sum(low.astype(F32), axis=0, keepdims=True)

        over_rows(body)

    def attn_back(grads, j):
        def run(w):
            value = dot_nt(grads[:, pl.ds(j * COLS, COLS)], matrix(w[...]))
            if j == 0:
                acc[...] = value
            else:
                d_attn[...] = (acc[...] + value).astype(BF16)

        return run

    def vector_sums():
        gvecs[pl.ds(SELF_Q, 1), :] = jnp.sum(qkv[:, pl.ds(0, width)].astype(F32), axis=0, keepdims=True)
        pack_vectors()

    def target_done():
        r["target_grad"][...] = flow[...].astype(BF16)

    staged, stage_sem = r["staged"], r["stage_sem"]
    stage_copies = []

    def memory_back(half, tiles):
        half_cols = width // 2

        def run(w):
            weights = [matrix(w[c // 2, c % 2 * zh : (c % 2 + 1) * zh]) for c in range(4)]
            for tile in tiles:
                slot = len(stage_copies) % 2
                if len(stage_copies) >= 2:
                    stage_copies[-2].wait()
                at_rows = pl.ds(tile * 512, 512)
                value = dot_nt(cross_k[at_rows, :half_cols], weights[0])
                value += dot_nt(cross_k[at_rows, half_cols:], weights[1])
                value += dot_nt(cross_v[at_rows, :half_cols], weights[2])
                value += dot_nt(cross_v[at_rows, half_cols:], weights[3])
                staged[slot] = value.astype(BF16)
                copy = pltpu.make_async_copy(
                    staged.at[slot],
                    r["memory_grad"].at[at_rows, pl.ds(half * half_cols, half_cols)],
                    stage_sem.at[slot],
                )
                copy.start()
                stage_copies.append(copy)

        return run


    every = (far_all, pl.ds(0, 2), pl.ds(0, 2), pl.ds(0, 2))
    wbuf, wquarter = r["wbuf"], r["wquarter"]
    wslots = wbuf.shape[0]
    uses = {"column": 0, "quarter": 0}

    def next_slot(kind, slots):
        uses[kind] += 1
        return (uses[kind] - 1) % slots

    def column_load(a, col):
        slot = next_slot("column", wslots)
        src = whole[a].at[(*every, pl.ds(0, rows), pl.ds(col, COLS))]
        return dict(buffer=wbuf.at[slot], takes=[slot], copies=[(src, wbuf.at[slot])])

    def quarter_load(j):
        slot = next_slot("quarter", 2)
        src = whole[FDOWN].at[(*every, pl.ds(0, down_rows), pl.ds(j * 256, 256))]
        return dict(buffer=wquarter.at[slot], takes=[wslots + slot], copies=[(src, wquarter.at[slot])])

    def group_load(i):
        slot = next_slot("quarter", 2)
        copies = [
            (
                whole[FDOWN].at[(pl.ds(i * zs, zs), *every[1:], pl.ds(0, down_rows), pl.ds(q * 256, 256))],
                wquarter.at[slot, pl.ds(q * zs, zs)],
            )
            for q in range(4)
        ]
        return dict(buffer=wquarter.at[slot], takes=[wslots + slot], copies=copies)

    def half_load(i):
        copies = [
            (
                whole[CQKV].at[
                    (pl.ds(i * zh, zh), *every[1:], pl.ds(0, rows), pl.ds(width + c * COLS, COLS))
                ],
                wbuf.at[2 * i + c // 2, pl.ds(c % 2 * zh, zh)],
            )
            for c in range(4)
        ]
        return dict(buffer=wbuf.at[pl.ds(2 * i, 2)], takes=[2 * i, 2 * i + 1], copies=copies)

    chunks, index = gather_chunks([s.shape for s in shards])
    count = len(chunks)
    per_half = width // COLS
    forward = []
    backward = []

    def piece(pieces, cost, run, load=None, dep=0, name=None):
        pieces.append(dict(cost=cost, run=run, load=load, dep=dep, name=name))

    def down_dep(j):
        return index[(FDOWN, down_rows - rows, j * 256 // COLS * COLS)]

    piece(forward, 4.0, take_vectors, None, 0)
    for j in range(3 * width // COLS):
        piece(forward, 0.5, self_project(j), column_load(SQKV, j * COLS), index[(SQKV, 0, j * COLS)])
    for first in range(0, samples * pairs, 4):
        piece(forward, 1.2, self_attend(first, first + 4), None, 0)
    for j in range(per_half):
        piece(forward, 0.5, branch(self_attn, SELF_O, j), column_load(SOUT, j * COLS), index[(SOUT, 0, j * COLS)])
    piece(forward, 0.9, norm_one)
    piece(forward, 0.5, turn(x_in))
    piece(forward, 0.5, turn(self_attn))
    for target, at, first in ((cross_k, None, width), (cross_v, CROSS_V, 2 * width)):
        for j in range(per_half):
            col = first + j * COLS
            dep = index[(CQKV, 0, col)]
            piece(forward, 1.2, cross_project(target, at, j, 0), column_load(CQKV, col), dep)
            piece(forward, 1.2, cross_project(target, at, j, samples * mem_len // 512), "keep", dep)
    for j in range(per_half):
        piece(forward, 0.5, cross_query(j), column_load(CQKV, j * COLS), index[(CQKV, 0, j * COLS)])
    piece(forward, 0.5, turn(h1_low))
    for s in range(samples):
        for i in range(width // 256):
            piece(forward, 0.3 * (2 * (width // 256 - i) - 1) / 2, turn_memory(s, i))
    for first in range(0, samples * pairs, 2):
        piece(forward, 1.6, cross_attend(first, first + 2))
    for j in range(per_half):
        piece(forward, 0.5, branch(cross_attn, CROSS_O, j), column_load(COUT, j * COLS), index[(COUT, 0, j * COLS)])
    piece(forward, 0.9, norm_two)
    piece(forward, 0.5, turn(cross_attn))
    for j in range(hidden // COLS):
        piece(forward, 1.2, feed_up(j), column_load(FUP, j * COLS), index[(FUP, 0, j * COLS)])
    piece(forward, 0.5, turn(h2_low))
    for j in range(width // 256):
        piece(forward, 0.8, feed_down(j), quarter_load(j), down_dep(j))
    piece(forward, 2.0, norm_three)

    for i in range(4):
        piece(backward, 0.7, pre_back(i), group_load(i), name="pre%d" % i)
    for j in range(hidden // COLS):
        piece(backward, 0.3, flow_back(slope, 0, j), column_load(FUP, j * COLS))
    piece(backward, 0.9, norm_two_back, name="norm2")
    for j in range(per_half):
        piece(backward, 0.3, attn_back(d_cross, j), column_load(COUT, j * COLS))
    for first in range(0, samples * pairs):
        piece(backward, 1.2, cross_attend_back(first, first + 1), name="cross")
    for j in range(per_half):
        piece(backward, 0.3, flow_back(cross_q, 0, j), column_load(CQKV, j * COLS))
    piece(backward, 0.9, norm_one_back, name="norm1")
    for j in range(per_half):
        piece(backward, 0.3, attn_back(d_self, j), column_load(SOUT, j * COLS))
    for first in range(0, samples * pairs, 2):
        piece(backward, 1.0, self_attend_back(first, first + 2), name="self")
    piece(backward, 1.0, vector_sums, name="vectors")
    for j in range(3 * width // COLS):
        piece(backward, 0.3, flow_back(qkv, 0, j), column_load(SQKV, j * COLS))
    piece(backward, 0.5, target_done)
    tile_count = samples * mem_len // 512
    for half in range(2):
        for first in range(tile_count):
            piece(backward, 1.6, memory_back(half, range(first, first + 1)), half_load(half) if first == 0 else "keep")

    def prepare(pieces, holders):
        last = None
        for p in pieces:
            p["done"] = p["started"] = False
            p["copies"], p["after"], p["buffer"] = [], [], None
            if p["load"] == "keep":
                p["buffer"] = last["buffer"]
                for slot in last["load"]["takes"]:
                    holders[slot] = p
            elif p["load"] is not None:
                p["buffer"] = p["load"]["buffer"]
                for slot in p["load"]["takes"]:
                    if slot in holders:
                        p["after"].append(holders[slot])
                    holders[slot] = p
                for n, (src, dst) in enumerate(p["load"]["copies"]):
                    sem = r["load_sem"].at[p["load"]["takes"][0], n]
                    p["copies"].append(pltpu.make_async_copy(src, dst, sem))
                last = p

    def start(p):
        for copy in p["copies"]:
            if not p["started"]:
                copy.start()
        p["started"] = True

    def look_ahead(pieces, ready):
        for later in pieces[:AHEAD]:
            if later["dep"] > ready:
                break
            if not later["started"] and all(p["done"] for p in later["after"]):
                start(later)

    def run_piece(pieces, ready):
        p = pieces.pop(0)
        start(p)
        look_ahead(pieces, ready)
        for copy in p["copies"]:
            copy.wait()
        if p["buffer"] is not None:
            p["run"](p["buffer"])
        else:
            p["run"]()
        p["done"] = True
        return p

    def work(pieces, ready, limit):
        spent = 0.0
        look_ahead(pieces, ready)
        while pieces and pieces[0]["dep"] <= ready and spent < limit:
            spent += run_piece(pieces, ready)["cost"]

    holders = {}
    prepare(forward, holders)
    prepare(backward, holders)


    in_copies = [
        pltpu.make_async_copy(r["mem_hbm"], mem, r["in_sem"].at[0]),
        pltpu.make_async_copy(r["cot_hbm"], cot, r["in_sem"].at[1]),
        pltpu.make_async_copy(r["x_hbm"], x_in, r["in_sem"].at[2]),
    ]

    def block(ref, k, *lead):
        _, row, row_count, col, cols = chunks[k]
        return ref.at[(*lead, pl.ds(row, row_count), pl.ds(col, cols))]

    def gathered(k, *lead):
        return block(whole[chunks[k][0]], k, *lead)

    local = []
    for a in range(7):
        copy = pltpu.make_async_copy(shards[a], whole[a].at[far, y, core, x], r["local_sem"].at[a])
        copy.start()
        local.append(copy)
    greet(me)
    for copy in in_copies:
        copy.start()

    sent = []

    def go(copy):
        copy.start()
        sent.append(copy)
        return copy

    far_copies, near_copies, other_copies, pass_copies, twin_copies = {}, {}, {}, {}, {}
    last_lane = far_count - 1
    gsend, grecv = r["gsend"], r["grecv"]

    def send(k, lane, ref, device):
        return go(remote(ref, ref, gsend.at[k, lane], grecv.at[k, lane], device))

    def start_far(k):
        far_copies[k] = [
            go(
                remote(
                    block(shards[chunks[k][0]], k),
                    gathered(k, far, y, core, x),
                    gsend.at[k, d],
                    grecv.at[k, d],
                    device,
                )
            )
            for d, (_, device) in enumerate(me["far_devices"])
        ]
        if cross_way[k]:
            near_copies[k] = go(
                remote(
                    block(shards[chunks[k][0]], k),
                    gathered(k, far, y, core, x),
                    gsend.at[k, last_lane],
                    grecv.at[k, last_lane],
                    me["near_device"],
                )
            )

    def start_near(k):
        column = gathered(k, far_all, y, core, x)
        other_copies[k] = send(k, last_lane + 1, column, me["other_device"])
        if cross_way[k]:
            near_copies[k].wait_recv()
            landed = gathered(k, far, near[0], core, near[1])
            near_copies[k] = [
                send(k, last_lane + 4 + d, landed, device) for d, (_, device) in enumerate(me["far_devices"])
            ]
        else:
            near_copies[k] = [send(k, last_lane, column, me["near_device"])]

    def start_pass(k):
        pass_copies[k] = send(k, last_lane + 2, gathered(k, far_all, near[0], core, near[1]), me["other_device"])

    def start_twin(k):
        half = gathered(k, far_all, pl.ds(0, 2), core, pl.ds(0, 2))
        twin_copies[k] = send(k, last_lane + 3, half, me["twin_device"])

    cross_way = [crossed(far_count, GATHER_CROSSED, chunk[0], k) for k, chunk in enumerate(chunks)]
    skew = GATHER_SKEW
    for t in range(count + 3 * skew + 1):
        k = t - 3 * skew
        if 0 <= k < count:
            other_copies[k].wait_recv()
            pass_copies[k].wait_recv()
            start_twin(k)
        k = t - 2 * skew
        if 0 <= k < count:
            for copy in near_copies[k]:
                copy.wait_recv()
            start_pass(k)
        k = t - skew
        if 0 <= k < count:
            if k == 0:
                for copy in local:
                    copy.wait()
            for copy in far_copies[k]:
                copy.wait_recv()
            start_near(k)
        if t < count:
            start_far(t)
        k = t - 3 * skew - 1
        if k >= 0:
            if k == 0:
                for copy in in_copies:
                    copy.wait()
            twin_copies[k].wait_recv()
            work(forward, k, FORWARD_WORK)
    work(forward, count, 1e9)
    for copy in sent:
        copy.wait_send()


    own, total, from_other, from_near, from_far = (
        r[n] for n in ("own", "total", "from_other", "from_near", "from_far")
    )
    small_buffers = (r["small_pack"], r["total_s"], r["from_other_s"], r["from_near_s"], r["from_far_s"])
    out_chunks = scatter_chunks(width)
    out_count = len(out_chunks)
    skew = SCATTER_SKEW
    own_slots, total_slots = own.shape[0], total.shape[0]
    other_slots, land_slots = from_other.shape[0], from_near.shape[0]
    from_near_far = r["from_near_far"]
    ssend, srecv = r["ssend"], r["srecv"]

    def buffers(k):
        if out_chunks[k][0] == SMALL:
            return small_buffers
        return (
            own.at[k % own_slots],
            total.at[k % total_slots],
            from_other.at[k % other_slots],
            from_near.at[k % land_slots],
            from_far.at[k % land_slots],
        )

    def compute(k):
        a, col = out_chunks[k]
        if a == SMALL:
            return
        target = buffers(k)[0]
        if a == FDOWN:
            right = d_ffn[:, pl.ds(col, 128)]
            for i in range(hidden // width):
                value = dot(act_t[i * width : (i + 1) * width], right).astype(BF16)
                for piece_at in range(0, width, rows):
                    b = (i * width + piece_at) // down_rows
                    q = piece_at % down_rows // rows
                    target[b // 8, (b // 4) % 2, (b // 2) % 2, b % 2, :, q * 128 : (q + 1) * 128] = value[
                        piece_at : piece_at + rows
                    ]
            return
        left, right = {
            FUP: (h2_low, slope),
            COUT: (cross_attn, d_cross),
            SOUT: (self_attn, d_self),
            SQKV: (x_in, qkv),
            CQKV: (
                (h1_low, cross_q),
                (mem, cross_k),
                (mem, cross_v),
            )[col // width if a == CQKV else 0],
        }[a]
        first = col % width if a == CQKV else col
        cols_at = pl.ds(first, COLS)
        if left is mem:
            part_rows = 512
            for i in range(0, width, part_rows):
                value = None
                for s in range(samples):
                    part = dot(
                        mem[s * mem_len + i : s * mem_len + i + part_rows],
                        right[pl.ds(s * mem_len, mem_len), cols_at],
                    )
                    value = part if value is None else value + part
                store_blocks(target, i, value.astype(BF16))
        else:
            turned = [left[:, i : i + 256] for i in range(0, width, 256)]
            value = dot(jnp.concatenate(turned, axis=0), right[:, cols_at])
            store_blocks(target, 0, value.astype(BF16))

    def store_blocks(target, first, value):
        for at in range(0, value.shape[0], rows):
            b = (first + at) // rows
            target[b // 8, (b // 4) % 2, (b // 2) % 2, b % 2] = value[at : at + rows]

    twins, others, nears, fars, near_fars = {}, {}, {}, {}, {}
    cross_out = [crossed(far_count, SCATTER_CROSSED, chunk[0], k) for k, chunk in enumerate(out_chunks)]

    def start_twin_sum(k):
        target, landing = buffers(k)[:2]
        twins[k] = remote(
            target.at[far_all, pl.ds(0, 2), 1 - core, pl.ds(0, 2)],
            landing,
            ssend.at[k, 0],
            srecv.at[k, 0],
            me["twin_device"],
        )
        twins[k].start()

    def add_own(k):
        mine, running = buffers(k)[:2]

        def body(i, carry):
            f, yy, xx = i // 4, (i // 2) % 2, i % 2
            running[f, yy, xx] = running[f, yy, xx] + mine[f, yy, core, xx]
            return carry

        lax.fori_loop(0, far_count * 4, body, 0)

    def start_others(k):
        running, landing = buffers(k)[1:3]
        others[k] = []
        for i, place in enumerate((diagonal, other)):
            copy = remote(
                running.at[far_all, place[0], place[1]],
                landing.at[i],
                ssend.at[k, 1 + i],
                srecv.at[k, 1 + i],
                me["other_device"],
            )
            copy.start()
            others[k].append(copy)

    def add_other(k, i):
        running, landing = buffers(k)[1:3]
        place = (near, (y, x))[i]

        def body(f, carry):
            running[f, place[0], place[1]] = running[f, place[0], place[1]] + landing[i, f]
            return carry

        lax.fori_loop(0, far_count, body, 0)

    def start_near_sum(k):
        _, running, _, landing, _ = buffers(k)
        source, target = running.at[far_all, near[0], near[1]], landing
        if cross_out[k]:
            source, target = running.at[far, near[0], near[1]], landing.at[0]
        nears[k] = remote(source, target, ssend.at[k, 3], srecv.at[k, 3], me["near_device"])
        nears[k].start()

    def start_near_fars(k):
        running, landing = buffers(k)[1], from_near_far.at[k % land_slots]
        near_fars[k] = []
        for d, (target, device) in enumerate(me["far_devices"]):
            lane = far_count + 3 + d
            copy = remote(
                running.at[target, near[0], near[1]], landing.at[d], ssend.at[k, lane], srecv.at[k, lane], device
            )
            copy.start()
            near_fars[k].append(copy)

    def add_near_fars(k):
        running, landing = buffers(k)[1], from_near_far.at[k % land_slots]
        result = running[far, near[0], near[1]].astype(F32)
        for d in range(far_count - 1):
            result += landing[d].astype(F32)
        running[far, near[0], near[1]] = result.astype(BF16)

    def add_near(k):
        _, running, _, landing, _ = buffers(k)

        def body(f, carry):
            running[f, y, x] = running[f, y, x] + landing[f]
            return carry

        lax.fori_loop(0, far_count, body, 0)

    def start_fars(k):
        _, running, _, _, landing = buffers(k)
        fars[k] = []
        for d, (target, device) in enumerate(me["far_devices"]):
            copy = remote(running.at[target, y, x], landing.at[d], ssend.at[k, 4 + d], srecv.at[k, 4 + d], device)
            copy.start()
            fars[k].append(copy)

    def finish(k):
        _, running, _, _, landing = buffers(k)
        a, col = out_chunks[k]
        result = running[far, y, x].astype(F32)
        for d in range(far_count - 1):
            result += landing[d].astype(F32)
        if cross_out[k]:
            result += buffers(k)[3][0].astype(F32)
        if a == SMALL:
            lane = (far * 8 + y * 4 + core * 2 + x) * rows % 128
            up_lane = (far * 8 + y * 4 + core * 2 + x) * down_rows % 128
            vectors = pltpu.roll(result, (128 - lane) % 128, 1)
            ups = pltpu.roll(result, (128 - up_lane) % 128, 1)
            row = lax.broadcasted_iota(jnp.int32, result.shape, 0)
            sums[a][...] = jnp.where(row == VECTORS, ups, vectors)
        elif a == FDOWN:
            for q in range(4):
                sums[a][q * rows : (q + 1) * rows, pl.ds(col, 128)] = result[:, q * 128 : (q + 1) * 128]
        else:
            sums[a][:, pl.ds(col, COLS)] = result
        for copy in (*others[k], nears[k], *fars[k], *near_fars.get(k, ())):
            copy.wait_send()

    needs = {FUP: "pre3", COUT: "norm2", CQKV: "cross", SOUT: "norm1", SQKV: "self", SMALL: "vectors"}

    def make_chunk(k):
        need = needs.get(out_chunks[k][0])
        while any(p["name"] == need for p in backward if need):
            run_piece(backward, count)
        compute(k)

    make_chunk(0)
    for t in range(out_count + 4 * skew):
        k = t - 4 * skew
        if 0 <= k < out_count:
            for copy in fars[k]:
                copy.wait_recv()
            if cross_out[k]:
                nears[k].wait_recv()
            finish(k)
        k = t - 3 * skew
        if 0 <= k < out_count:
            if cross_out[k]:
                for copy in near_fars[k]:
                    copy.wait_recv()
                add_near_fars(k)
                start_near_sum(k)
            else:
                nears[k].wait_recv()
                add_near(k)
                start_fars(k)
        k = t - 2 * skew
        if 0 <= k < out_count:
            others[k][0].wait_recv()
            add_other(k, 0)
            if cross_out[k]:
                start_near_fars(k)
            else:
                start_near_sum(k)
            others[k][1].wait_recv()
            add_other(k, 1)
            if cross_out[k]:
                start_fars(k)
        k = t - skew
        if 0 <= k < out_count:
            twins[k].wait()
            add_own(k)
            start_others(k)
        if t < out_count:
            start_twin_sum(t)
        if t + 1 < out_count:
            make_chunk(t + 1)
        work(backward, count, BACKWARD_WORK)
    work(backward, count, 1e9)
    for copy in stage_copies[-2:]:
        copy.wait()


def layer(mesh, target_input, memory, cotangent, mem_lengths, tgt_lengths, shards, small):
    samples, tgt_len, width = target_input.shape
    mem_len = memory.shape[1]
    far_count = mesh.shape["wide"] // 4
    rows = shards[SQKV].shape[0]
    tokens, keys, hidden = samples * tgt_len, samples * mem_len, 4 * width
    lanes = far_count + 3 + (3 if far_count == 4 else 0)
    count = len(gather_chunks([s.shape for s in shards])[0])
    out_count = len(scatter_chunks(width))
    lead = (far_count, 2, 2, 2)
    total_slots, own_slots = 5 * SCATTER_SKEW + 1, SCATTER_SKEW + 1
    other_slots, land_slots = 2 * SCATTER_SKEW + 1, (4 if far_count == 4 else 3) * SCATTER_SKEW

    def vmem(shape, dtype=BF16):
        return pltpu.VMEM(shape, dtype)

    small_sum = (SMALL_ROWS, 128)
    scratch = [
        vmem((tokens, width)),
        vmem((keys, width)),
        vmem((tokens, width)),
        vmem((tokens, 3 * width)),
        vmem((tokens, width)),
        vmem((tokens, width), F32),
        vmem((tokens, 1), F32),
        vmem((tokens, width), F32),
        vmem((tokens, width)),
        vmem((tokens, width)),
        vmem((keys, width)),
        vmem((keys, width)),
        vmem((tokens, width)),
        vmem((tokens, width), F32),
        vmem((tokens, 1), F32),
        vmem((tokens, width), F32),
        vmem((tokens, width)),
        vmem((tokens, hidden)),
        vmem((hidden, tokens)),
        vmem((tokens, hidden)),
        vmem((tokens, width), F32),
        vmem((tokens, width)),
        vmem((tokens, width)),
        vmem((tokens, width)),
        vmem((tokens, width)),
        vmem((samples * HEADS // 2, 2 * tgt_len), F32),
        vmem((samples * HEADS // 2, 2 * tgt_len), F32),
        vmem((24, width), F32),
        vmem((24, width), F32),
        vmem((2, 512, width // 2)),
        vmem((4,) + lead + (rows, COLS)),
        vmem((2,) + lead + (4 * rows, 256)),
        vmem(lead + (SMALL_ROWS, 128)),
        vmem((SMALL_ROWS, mesh.size, 128), F32),
        vmem(lead + small_sum, F32),
        vmem((own_slots,) + lead + (rows, COLS)),
        vmem((total_slots, far_count, 2, 2, rows, COLS)),
        vmem((other_slots, 2, far_count, rows, COLS)),
        vmem((land_slots, far_count, rows, COLS)),
        vmem((land_slots, far_count - 1, rows, COLS)),
        vmem((land_slots if far_count == 4 else 1, 3, rows, COLS)),
        vmem((far_count, 2, 2) + small_sum, F32),
        vmem((2, far_count) + small_sum, F32),
        vmem((far_count,) + small_sum, F32),
        vmem((far_count - 1,) + small_sum, F32),
        pltpu.SemaphoreType.DMA((6, 4)),
        pltpu.SemaphoreType.DMA((3,)),
        pltpu.SemaphoreType.DMA((7,)),
        pltpu.SemaphoreType.DMA((count, lanes)),
        pltpu.SemaphoreType.DMA((count, lanes)),
        pltpu.SemaphoreType.DMA((out_count, lanes)),
        pltpu.SemaphoreType.DMA((out_count, lanes)),
        pltpu.SemaphoreType.DMA((2,)),
    ]
    in_vmem, anywhere = pl.BlockSpec(memory_space=pltpu.VMEM), pl.BlockSpec(memory_space=pl.ANY)
    in_smem = pl.BlockSpec(memory_space=pltpu.SMEM)
    out_shape = [
        jax.ShapeDtypeStruct((tokens, width), BF16),
        jax.ShapeDtypeStruct((tokens, width), BF16),
        jax.ShapeDtypeStruct((keys, width), BF16),
    ]
    out_shape += [jax.ShapeDtypeStruct(s.shape, F32) for s in shards]
    out_shape += [jax.ShapeDtypeStruct(small_sum, F32)]
    out_shape += [jax.ShapeDtypeStruct(lead + s.shape, BF16) for s in shards]
    outs = pl.pallas_call(
        functools.partial(layer_kernel, (far_count, rows, width, samples, tgt_len, mem_len)),
        out_shape=out_shape,
        in_specs=[anywhere, anywhere, anywhere, in_smem, in_smem] + [in_vmem] * 7,
        out_specs=[in_vmem, in_vmem, anywhere] + [in_vmem] * 7 + [anywhere] * 6,
        scratch_shapes=scratch,
        compiler_params=pltpu.CompilerParams(
            collective_id=0, has_side_effects=True, vmem_limit_bytes=63 * 2**20
        ),
        cost_estimate=pl.CostEstimate(flops=52 * 10**9, bytes_accessed=10**8, transcendentals=10**7),
        name="decoder_layer",
    )(
        target_input.reshape(tokens, width),
        memory.reshape(keys, width),
        cotangent.reshape(tokens, width),
        mem_lengths,
        tgt_lengths,
        *shards,
        small,
    )
    return outs[:10]


def step(
    mesh,
    target_input,
    memory,
    cotangent,
    mem_lengths,
    tgt_lengths,
    self_qkv,
    self_out,
    self_bias,
    norm1_gain,
    norm1_shift,
    cross_qkv,
    cross_out,
    cross_bias,
    norm2_gain,
    norm2_shift,
    ffn_up,
    up_bias,
    ffn_down,
    down_bias,
    norm3_gain,
    norm3_shift,
):
    per, up_per = norm1_gain.shape[0], up_bias.shape[0]
    small = jnp.zeros((SMALL_ROWS, 128), BF16)
    row = 0
    for v in (
        self_bias, norm1_gain, norm1_shift, cross_bias, norm2_gain, norm2_shift,
        down_bias, norm3_gain, norm3_shift, up_bias,
    ):
        v = v.reshape(-1, v.shape[-1])
        small += jnp.pad(v, ((row, SMALL_ROWS - row - v.shape[0]), (0, 128 - v.shape[1])))
        row += v.shape[0]
    block_out, target_grad, memory_grad, *grads, sums = layer(
        mesh, target_input, memory, cotangent, mem_lengths, tgt_lengths,
        [self_qkv, self_out, cross_qkv, cross_out, ffn_up, ffn_down], small,
    )
    return (
        block_out.reshape(target_input.shape),
        target_grad.reshape(target_input.shape),
        memory_grad.reshape(memory.shape),
        grads[SQKV],
        grads[SOUT],
        sums[SELF_Q : SELF_Q + 3, :per],
        sums[GAIN1, :per],
        sums[SHIFT1, :per],
        grads[CQKV],
        grads[COUT],
        sums[CROSS_Q : CROSS_Q + 3, :per],
        sums[GAIN2, :per],
        sums[SHIFT2, :per],
        grads[FUP],
        sums[VECTORS, :up_per],
        grads[FDOWN],
        sums[DOWN, :per],
        sums[GAIN3, :per],
        sums[SHIFT3, :per],
    )


def solution(mesh):
    both = ("wide", "narrow")
    stream, matrix_spec, vector_spec, bias_spec = P(both, None, None), P(both, None), P(both), P(None, both)
    weights = (
        matrix_spec, matrix_spec, bias_spec, vector_spec, vector_spec,
        matrix_spec, matrix_spec, bias_spec, vector_spec, vector_spec,
        matrix_spec, vector_spec, matrix_spec, vector_spec, vector_spec, vector_spec,
    )
    return jax.shard_map(
        functools.partial(step, mesh),
        mesh=mesh,
        in_specs=(stream, stream, stream, vector_spec, vector_spec) + weights,
        out_specs=(stream, stream, stream) + weights,
        check_vma=False,
    )
```

```python
import functools
import math

import jax
import jax.numpy as jnp
from jax import lax
from jax.experimental import pallas as pl
from jax.experimental.pallas import tpu as pltpu
from jax.sharding import PartitionSpec as P

MESH = pl.DeviceIdType.MESH
HEADS = 16
HEAD_DIM = 64
NORM_EPSILON = 1e-05
MASK_VALUE = -1e30
COLS = 512
GATHER_SKEW = 2
SCATTER_SKEW = 2
FORWARD_WORK = 1.5
BACKWARD_WORK = 1.5
GATHER_CROSSED = (0, 0, 1)
SCATTER_CROSSED = (0, 0, 1)
AHEAD = 8
SMALL_ROWS = 16

F32 = jnp.float32
BF16 = jnp.bfloat16

SELF_Q, SELF_V, SELF_O, GAIN1, SHIFT1, CROSS_Q, CROSS_V, CROSS_O, GAIN2, SHIFT2, DOWN, GAIN3, SHIFT3, UP = range(14)
VECTORS = 13


def dot(a, b):
    return lax.dot_general(a, b, (((1,), (0,)), ((), ())), preferred_element_type=F32)


def dot_nt(a, b):
    return lax.dot_general(a, b, (((1,), (1,)), ((), ())), preferred_element_type=F32)


def dot_tn(a, b):
    return lax.dot_general(a, b, (((0,), (0,)), ((), ())), preferred_element_type=F32)


def places(far_count):
    wide = lax.axis_index("wide")
    x = lax.axis_index("narrow")
    far = wide // 4
    y = (wide // 2) % 2
    core = wide % 2
    near_y = y + core * (1 - 2 * y)
    near_x = x + (1 - core) * (1 - 2 * x)
    other_y = y + (1 - core) * (1 - 2 * y)
    other_x = x + core * (1 - 2 * x)

    def device(f, yy, cc, xx):
        return (f * 4 + yy * 2 + cc, xx)

    return dict(
        far=far,
        y=y,
        core=core,
        x=x,
        near=(near_y, near_x),
        other=(other_y, other_x),
        diagonal=(1 - y, 1 - x),
        near_device=device(far, near_y, core, near_x),
        other_device=device(far, other_y, core, other_x),
        twin_device=device(far, y, 1 - core, x),
        far_devices=[
            (lax.rem(far + d, far_count), device(lax.rem(far + d, far_count), y, core, x))
            for d in range(1, far_count)
        ],
    )


def greet(where):
    barrier = pltpu.get_barrier_semaphore()
    partners = [where["near_device"], where["other_device"], where["twin_device"]]
    partners += [device for _, device in where["far_devices"]]
    for device in partners:
        pl.semaphore_signal(barrier, inc=1, device_id=device, device_id_type=MESH)
    pl.semaphore_wait(barrier, len(partners))


def remote(src, dst, send_sem, recv_sem, device):
    return pltpu.make_async_remote_copy(
        src_ref=src,
        dst_ref=dst,
        send_sem=send_sem,
        recv_sem=recv_sem,
        device_id=device,
        device_id_type=MESH,
    )


def matrix(value):
    rows, cols = value.shape[-2:]
    if rows % 16:
        return value.astype(F32).reshape(-1, cols).astype(BF16)
    return value.reshape(-1, cols)


ARRAYS = ("self_qkv", "self_out", "cross_qkv", "cross_out", "ffn_up", "ffn_down")
SQKV, SOUT, CQKV, COUT, FUP, FDOWN, SMALL = range(7)


def crossed(far_count, pattern, array, k):
    return far_count == 4 and array != SMALL and pattern[k % len(pattern)] == 1


def gather_chunks(shapes):
    rows = shapes[SQKV][0]
    width = shapes[SOUT][1]
    chunks = [(SMALL, 0, SMALL_ROWS, 0, 128)]
    for a, first, last in (
        (SQKV, 0, 3 * width),
        (SOUT, 0, width),
        (CQKV, width, 3 * width),
        (CQKV, 0, width),
        (COUT, 0, width),
        (FUP, 0, 4 * width),
    ):
        chunks += [(a, 0, rows, col, COLS) for col in range(first, last, COLS)]
    for col in range(0, width, COLS):
        chunks += [(FDOWN, row, rows, col, COLS) for row in range(0, 4 * rows, rows)]
    index = {(a, row, col): k for k, (a, row, _, col, _) in enumerate(chunks)}
    return chunks, index


def scatter_chunks(width):
    chunks = [(FDOWN, 128 * j) for j in range(width // 128)]
    for a, first, last in (
        (FUP, 0, 4 * width),
        (COUT, 0, width),
        (CQKV, 0, 3 * width),
        (SOUT, 0, width),
    ):
        chunks += [(a, col) for col in range(first, last, COLS)]
    chunks += [(SMALL, 0)]
    chunks += [(SQKV, col) for col in range(0, 3 * width, COLS)]
    return chunks


def layer_kernel(cfg, *refs):
    far_count, rows, width, samples, tgt_len, mem_len = cfg
    devices = 8 * far_count
    hidden = 4 * width
    down_rows = 4 * rows
    tokens = samples * tgt_len
    pairs = HEADS // 2
    scale = 1.0 / math.sqrt(HEAD_DIM)
    zs = max(1, far_count // 4)
    zh = max(1, far_count // 2)

    names = (
        "x_hbm", "mem_hbm", "cot_hbm", "mem_lengths", "tgt_lengths", "i0", "i1", "i2", "i3", "i4", "i5", "i6",
        "block_out", "target_grad", "memory_grad", "o0", "o1", "o2", "o3", "o4", "o5", "o6", "w0", "w1", "w2", "w3",
        "w4", "w5", "g0", "g1", "g2", "g3", "g4", "g5", "small_out", "x", "mem", "cot", "qkv", "self_attn", "n1",
        "r1", "h1", "h1_low", "cross_q", "cross_k", "cross_v", "cross_attn", "n2", "r2", "flow", "h2_low", "act",
        "act_t", "slope", "acc", "d_ffn", "d_cross", "d_attn", "d_self", "self_lse", "cross_lse", "vecs", "gvecs",
        "staged", "wbuf", "wquarter", "small_in", "small_rows", "small_pack", "own", "total", "from_other",
        "from_near", "from_far", "from_near_far", "total_s", "from_other_s", "from_near_s", "from_far_s",
        "load_sem", "in_sem", "local_sem", "gsend", "grecv", "ssend", "srecv", "stage_sem", "out_sem",
    )
    r = dict(zip(names, refs, strict=True))
    x_in, mem, cot = r["x"], r["mem"], r["cot"]
    qkv, self_attn, n1, r1, h1, h1_low = (r[n] for n in ("qkv", "self_attn", "n1", "r1", "h1", "h1_low"))
    cross_q, cross_k, cross_v, cross_attn = (r[n] for n in ("cross_q", "cross_k", "cross_v", "cross_attn"))
    n2, r2, flow, h2_low = (r[n] for n in ("n2", "r2", "flow", "h2_low"))
    act, act_t, slope, acc = (r[n] for n in ("act", "act_t", "slope", "acc"))
    d_ffn, d_cross, d_attn, d_self = (r[n] for n in ("d_ffn", "d_cross", "d_attn", "d_self"))
    vecs, gvecs = r["vecs"], r["gvecs"]
    shards = [r["i%d" % i] for i in range(7)]
    whole = [r["w%d" % i] for i in range(6)] + [r["small_in"]]
    sums = [r["g%d" % i] for i in range(6)] + [r["small_out"]]

    me = places(far_count)
    far, y, core, x = me["far"], me["y"], me["core"], me["x"]
    far_all = pl.ds(0, far_count)
    near, other, diagonal = me["near"], me["other"], me["diagonal"]

    def vec(i, col=0, cols=width):
        return vecs[pl.ds(i, 1), pl.ds(col, cols)]


    def owner_of(per, first):
        device = lax.broadcasted_iota(jnp.int32, (devices, width), 0)
        column = lax.broadcasted_iota(jnp.int32, (devices, width), 1) + first
        return lax.shift_right_logical(column, per.bit_length() - 1) == device

    def spread_of(per):
        lane = lax.broadcasted_iota(jnp.int32, (128, width), 0)
        column = lax.broadcasted_iota(jnp.int32, (128, width), 1)
        return (lane == jnp.bitwise_and(column, per - 1)).astype(F32).astype(BF16)

    def take_vectors():
        small_in, table = r["small_in"], r["small_rows"]

        def body(b, carry):
            tile = small_in[b // 8, (b // 4) % 2, (b // 2) % 2, b % 2].astype(F32)
            for i in range(VECTORS + 1):
                table[i, pl.ds(b, 1), :] = tile[i : i + 1]
            return carry

        lax.fori_loop(0, devices, body, 0)
        spread, owner = spread_of(rows), owner_of(rows, 0)
        for i in range(VECTORS):
            values = dot(table[i].astype(BF16), spread)
            vecs[pl.ds(i, 1), :] = jnp.sum(jnp.where(owner, values, 0.0), axis=0, keepdims=True)
        values = dot(table[VECTORS].astype(BF16), spread_of(down_rows))
        for j in range(4):
            owner = owner_of(down_rows, j * width)
            vecs[pl.ds(UP + j, 1), :] = jnp.sum(jnp.where(owner, values, 0.0), axis=0, keepdims=True)

    def pack_vectors():
        pack = r["small_pack"]

        pack[...] = jnp.zeros_like(pack)
        for b in range(devices):
            lead = (b // 8, (b // 4) % 2, (b // 2) % 2, b % 2)
            lane, up_lane = b * rows // 128 * 128, b * down_rows % width // 128 * 128
            up_row = UP + b * down_rows // width
            pack[(*lead, slice(0, VECTORS))] = gvecs[0:VECTORS, lane : lane + 128]
            pack[(*lead, slice(VECTORS, VECTORS + 1))] = gvecs[up_row : up_row + 1, up_lane : up_lane + 128]

    def turn(ref, first=0, cols=width):
        def run():
            def body(i, carry):
                cols_at = pl.ds(pl.multiple_of(first + i * 256, 256), 256)
                ref[:, cols_at] = ref[:, cols_at].T
                return carry

            lax.fori_loop(0, cols // 256, body, 0)

        return run

    def turn_memory(s, i):
        def run():
            blocks = width // 256

            def at(i, j):
                return (
                    pl.ds(pl.multiple_of(s * mem_len + i * 256, 256), 256),
                    pl.ds(pl.multiple_of(j * 256, 256), 256),
                )

            mem[at(i, i)] = mem[at(i, i)].T
            for j in range(i + 1, blocks):
                upper, lower = mem[at(i, j)].T, mem[at(j, i)].T
                mem[at(i, j)] = lower
                mem[at(j, i)] = upper

        return run

    def self_project(j):
        def run(w):
            value = dot(x_in[...], matrix(w[...]))
            cols = pl.ds(j * COLS, COLS)
            part, first = j * COLS // width, j * COLS % width
            if part == 0:
                value = (value + vec(SELF_Q, first, COLS)) * scale
            if part == 2:
                value = value + vec(SELF_V, first, COLS)
            qkv[:, cols] = value.astype(BF16)

        return run

    def head_masks():
        lane = lax.broadcasted_iota(jnp.int32, (1, 128), 1)
        low = (lane < HEAD_DIM).astype(F32).astype(BF16)
        return low, (lane >= HEAD_DIM).astype(F32).astype(BF16)

    def both_heads(two):
        low, high = head_masks()
        return jnp.concatenate([two * low, two * high], axis=0)

    def one_row_each(stacked):
        lane = lax.broadcasted_iota(jnp.int32, (tgt_len, 128), 1)
        return jnp.where(lane < HEAD_DIM, stacked[:tgt_len], stacked[tgt_len:])

    def scores_of(keys, queries, length, causal):
        scores = dot_nt(keys, queries)
        key = lax.broadcasted_iota(jnp.int32, scores.shape, 0)
        usable = key < length
        if causal:
            query = jnp.bitwise_and(lax.broadcasted_iota(jnp.int32, scores.shape, 1), tgt_len - 1)
            usable = usable & (key <= query)
        return jnp.where(usable, scores, MASK_VALUE)

    def attend(u, queries, q_at, keys, k_at, values, v_at, key_count, lengths, causal, out, lse):
        s, pair = u // pairs, u % pairs
        lane = pair * 128
        q_rows = pl.ds(pl.multiple_of(s * tgt_len, tgt_len), tgt_len)
        k_rows = pl.ds(pl.multiple_of(s * key_count, key_count), key_count)

        def cols(first):
            return pl.ds(pl.multiple_of(first + lane, 128), 128)

        stacked = both_heads(queries[q_rows, cols(q_at)])
        scores = scores_of(keys[k_rows, cols(k_at)], stacked, lengths[s], causal)
        peak = jnp.max(scores, axis=0, keepdims=True)
        exponentials = jnp.exp(scores - peak)
        total = jnp.sum(exponentials, axis=0, keepdims=True)
        probs = (exponentials * (1.0 / total)).astype(BF16)
        mixed = dot_tn(values[k_rows, cols(v_at)], probs)
        out[q_rows, cols(0)] = one_row_each(mixed.T).astype(BF16)
        lse[pl.ds(u, 1), :] = peak + jnp.log(total)

    def attend_back(u, queries, q_at, keys, k_at, values, v_at, key_count, lengths, causal, lse, value_sum):
        s, pair = u // pairs, u % pairs
        lane = pair * 128
        q_rows = pl.ds(pl.multiple_of(s * tgt_len, tgt_len), tgt_len)
        k_rows = pl.ds(pl.multiple_of(s * key_count, key_count), key_count)

        def cols(first):
            return pl.ds(pl.multiple_of(first + lane, 128), 128)

        stacked = both_heads(queries[q_rows, cols(q_at)])
        upstream = both_heads(d_attn[q_rows, cols(0)])
        key_rows = keys[k_rows, cols(k_at)]
        scores = scores_of(key_rows, stacked, lengths[s], causal)
        probs = jnp.exp(scores - lse[pl.ds(u, 1), :])
        prob_grad = dot_nt(values[k_rows, cols(v_at)], upstream)
        delta = jnp.sum(probs * prob_grad, axis=0, keepdims=True)
        score_grad = (probs * (prob_grad - delta)).astype(BF16)
        query_grad = dot_tn(key_rows, score_grad)
        value_grad = dot(probs.astype(BF16), upstream).astype(BF16)
        values[k_rows, cols(v_at)] = value_grad
        keys[k_rows, cols(k_at)] = dot(score_grad, stacked).astype(BF16)
        queries[q_rows, cols(q_at)] = (one_row_each(query_grad.T) * scale).astype(BF16)
        gvecs[pl.ds(value_sum, 1), cols(0)] += jnp.sum(value_grad.astype(F32), axis=0, keepdims=True)

    def self_attend(first, last):
        def body(u, carry):
            attend(u, qkv, 0, qkv, width, qkv, 2 * width, tgt_len, r["tgt_lengths"], True,
                   self_attn, r["self_lse"])
            return carry

        return lambda: lax.fori_loop(first, last, body, 0)

    def cross_attend(first, last):
        def body(u, carry):
            attend(u, cross_q, 0, cross_k, 0, cross_v, 0, mem_len, r["mem_lengths"], False,
                   cross_attn, r["cross_lse"])
            return carry

        return lambda: lax.fori_loop(first, last, body, 0)

    def self_attend_back(first, last):
        def body(u, carry):
            attend_back(u, qkv, 0, qkv, width, qkv, 2 * width, tgt_len, r["tgt_lengths"], True,
                        r["self_lse"], SELF_V)
            return carry

        return lambda: lax.fori_loop(first, last, body, 0)

    def cross_attend_back(first, last):
        def body(u, carry):
            attend_back(u, cross_q, 0, cross_k, 0, cross_v, 0, mem_len, r["mem_lengths"], False,
                        r["cross_lse"], CROSS_V)
            return carry

        return lambda: lax.fori_loop(first, last, body, 0)

    ROW_TILE = 64

    def over_rows(body):
        def step(i, carry):
            body(pl.ds(pl.multiple_of(i * ROW_TILE, ROW_TILE), ROW_TILE))
            return carry

        lax.fori_loop(0, tokens // ROW_TILE, step, 0)

    def normalise(summed):
        average = jnp.mean(summed, axis=-1, keepdims=True)
        centred = summed - average
        inverse = lax.rsqrt(jnp.mean(centred * centred, axis=-1, keepdims=True) + NORM_EPSILON)
        return centred * inverse, inverse

    def normalise_back(at, incoming, normed, inverse, gain):
        gvecs[pl.ds(at, 1), :] += jnp.sum(incoming * normed, axis=0, keepdims=True)
        gvecs[pl.ds(at + 1, 1), :] += jnp.sum(incoming, axis=0, keepdims=True)
        scaled = incoming * gain
        centred = (
            scaled
            - jnp.mean(scaled, axis=-1, keepdims=True)
            - normed * jnp.mean(scaled * normed, axis=-1, keepdims=True)
        )
        return centred * inverse

    def branch(attn, at, j):
        def run(w):
            cols = pl.ds(j * COLS, COLS)
            acc[:, cols] = dot(attn[...], matrix(w[...])) + vec(at, j * COLS, COLS)

        return run

    def norm_one():
        def body(at):
            normed, inverse = normalise(x_in[at, :].astype(F32) + acc[at, :])
            hidden_one = normed * vec(GAIN1) + vec(SHIFT1)
            n1[at, :] = normed
            r1[at, :] = inverse
            h1[at, :] = hidden_one
            h1_low[at, :] = hidden_one.astype(BF16)

        over_rows(body)

    def cross_query(j):
        def run(w):
            cols = pl.ds(j * COLS, COLS)
            value = (dot(h1_low[...], matrix(w[...])) + vec(CROSS_Q, j * COLS, COLS)) * scale
            cross_q[:, cols] = value.astype(BF16)

        return run

    def cross_project(target, at, j, first):
        def run(w):
            weight = matrix(w[...])

            def body(i, carry):
                at_rows = pl.ds(pl.multiple_of(i * 256, 256), 256)
                value = dot(mem[at_rows, :], weight)
                if at is not None:
                    value = value + vec(at, j * COLS, COLS)
                target[at_rows, pl.ds(j * COLS, COLS)] = value.astype(BF16)
                return carry

            lax.fori_loop(first, first + samples * mem_len // 512, body, 0)

        return run

    def norm_two():
        def body(at):
            normed, inverse = normalise(h1[at, :] + acc[at, :])
            hidden_two = normed * vec(GAIN2) + vec(SHIFT2)
            n2[at, :] = normed
            r2[at, :] = inverse
            flow[at, :] = hidden_two
            h2_low[at, :] = hidden_two.astype(BF16)

        over_rows(body)

    def feed_up(j):
        def run(w):
            row, first = UP + j * COLS // width, j * COLS % width
            cols = pl.ds(j * COLS, COLS)
            pre = dot(h2_low[...], matrix(w[...])) + vec(row, first, COLS)
            normal_cdf = 0.5 * (1.0 + lax.erf(pre * (1.0 / math.sqrt(2.0))))
            density = jnp.exp(-0.5 * pre * pre) * (1.0 / math.sqrt(2.0 * math.pi))
            low = (pre * normal_cdf).astype(BF16)
            act[:, cols] = low
            act_t[pl.ds(j * COLS, COLS), :] = low.T
            slope[:, cols] = (normal_cdf + pre * density).astype(BF16)

        return run

    def feed_down(j):
        def run(w):
            acc[:, pl.ds(j * 256, 256)] = dot(act[...], matrix(w[...])) + vec(DOWN, j * 256, 256)

        return run

    def norm_three():
        gvecs[...] = jnp.zeros_like(gvecs)

        def body(at):
            normed, inverse = normalise(flow[at, :] + acc[at, :])
            d_attn[at, :] = (normed * vec(GAIN3) + vec(SHIFT3)).astype(BF16)
            grad = normalise_back(GAIN3, cot[at, :].astype(F32), normed, inverse, vec(GAIN3))
            low = grad.astype(BF16)
            flow[at, :] = grad
            d_ffn[at, :] = low
            gvecs[pl.ds(DOWN, 1), :] += jnp.sum(low.astype(F32), axis=0, keepdims=True)

        over_rows(body)
        hand_out(d_attn, r["block_out"], 7)

    def pre_back(i):
        def run(w):
            cols = pl.ds(i * width, width)
            value = None
            for q in range(4):
                part = dot_nt(d_ffn[:, pl.ds(q * 256, 256)], matrix(w[q * zs : (q + 1) * zs]))
                value = part if value is None else value + part
            low = (value * slope[:, cols].astype(F32)).astype(BF16)
            slope[:, cols] = low
            gvecs[pl.ds(UP + i, 1), :] = jnp.sum(low.astype(F32), axis=0, keepdims=True)

        return run

    def flow_back(grads, first, j):
        def run(w):
            flow[...] += dot_nt(grads[:, pl.ds(first + j * COLS, COLS)], matrix(w[...]))

        return run

    def norm_two_back():
        def body(at):
            grad = normalise_back(GAIN2, flow[at, :], n2[at, :], r2[at, :], vec(GAIN2))
            low = grad.astype(BF16)
            flow[at, :] = grad
            d_cross[at, :] = low
            gvecs[pl.ds(CROSS_O, 1), :] += jnp.sum(low.astype(F32), axis=0, keepdims=True)

        over_rows(body)

    def norm_one_back():
        gvecs[pl.ds(CROSS_Q, 1), :] = jnp.sum(cross_q[...].astype(F32), axis=0, keepdims=True)

        def body(at):
            grad = normalise_back(GAIN1, flow[at, :], n1[at, :], r1[at, :], vec(GAIN1))
            low = grad.astype(BF16)
            flow[at, :] = grad
            d_self[at, :] = low
            gvecs[pl.ds(SELF_O, 1), :] += jnp.sum(low.astype(F32), axis=0, keepdims=True)

        over_rows(body)

    def attn_back(grads, j):
        def run(w):
            value = dot_nt(grads[:, pl.ds(j * COLS, COLS)], matrix(w[...]))
            if j == 0:
                acc[...] = value
                if grads is d_cross:
                    out_copies.pop(0).wait()
            else:
                d_attn[...] = (acc[...] + value).astype(BF16)

        return run

    def vector_sums():
        gvecs[pl.ds(SELF_Q, 1), :] = jnp.sum(qkv[:, pl.ds(0, width)].astype(F32), axis=0, keepdims=True)
        pack_vectors()

    def target_done():
        d_ffn[...] = flow[...].astype(BF16)
        hand_out(d_ffn, r["target_grad"], 8)

    out_copies = []

    def hand_out(value, target, i):
        copy = pltpu.make_async_copy(value, target, r["out_sem"].at[i])
        copy.start()
        out_copies.append(copy)

    staged, stage_sem = r["staged"], r["stage_sem"]
    stage_copies = []

    def memory_back(half, tiles):
        half_cols = width // 2

        def run(w):
            weights = [matrix(w[c // 2, c % 2 * zh : (c % 2 + 1) * zh]) for c in range(4)]
            for tile in tiles:
                slot = len(stage_copies) % 2
                if len(stage_copies) >= 2:
                    stage_copies[-2].wait()
                at_rows = pl.ds(tile * 512, 512)
                value = dot_nt(cross_k[at_rows, :half_cols], weights[0])
                value += dot_nt(cross_k[at_rows, half_cols:], weights[1])
                value += dot_nt(cross_v[at_rows, :half_cols], weights[2])
                value += dot_nt(cross_v[at_rows, half_cols:], weights[3])
                staged[slot] = value.astype(BF16)
                copy = pltpu.make_async_copy(
                    staged.at[slot],
                    r["memory_grad"].at[at_rows, pl.ds(half * half_cols, half_cols)],
                    stage_sem.at[slot],
                )
                copy.start()
                stage_copies.append(copy)

        return run


    every = (far_all, pl.ds(0, 2), pl.ds(0, 2), pl.ds(0, 2))
    wbuf, wquarter = r["wbuf"], r["wquarter"]
    wslots = wbuf.shape[0]
    uses = {"column": 0, "quarter": 0}

    def next_slot(kind, slots):
        uses[kind] += 1
        return (uses[kind] - 1) % slots

    def column_load(a, col):
        slot = next_slot("column", wslots)
        src = whole[a].at[(*every, pl.ds(0, rows), pl.ds(col, COLS))]
        return dict(buffer=wbuf.at[slot], takes=[slot], copies=[(src, wbuf.at[slot])])

    def quarter_load(j):
        slot = next_slot("quarter", 2)
        copies = [
            (
                whole[FDOWN].at[(*every, pl.ds(row, rows), pl.ds(j * 256, 256))],
                wquarter.at[(slot, *every, pl.ds(row, rows))],
                index[(FDOWN, row, j * 256 // COLS * COLS)],
            )
            for row in range(0, down_rows, rows)
        ]
        return dict(buffer=wquarter.at[slot], takes=[wslots + slot], copies=copies)

    def group_load(i):
        slot = next_slot("quarter", 2)
        copies = [
            (
                whole[FDOWN].at[(pl.ds(i * zs, zs), *every[1:], pl.ds(0, down_rows), pl.ds(q * 256, 256))],
                wquarter.at[slot, pl.ds(q * zs, zs)],
            )
            for q in range(4)
        ]
        return dict(buffer=wquarter.at[slot], takes=[wslots + slot], copies=copies)

    def half_load(i):
        copies = [
            (
                whole[CQKV].at[
                    (pl.ds(i * zh, zh), *every[1:], pl.ds(0, rows), pl.ds(width + c * COLS, COLS))
                ],
                wbuf.at[2 * i + c // 2, pl.ds(c % 2 * zh, zh)],
            )
            for c in range(4)
        ]
        return dict(buffer=wbuf.at[pl.ds(2 * i, 2)], takes=[2 * i, 2 * i + 1], copies=copies)

    chunks, index = gather_chunks([s.shape for s in shards])
    count = len(chunks)
    per_half = width // COLS
    forward = []
    backward = []

    def piece(pieces, cost, run, load=None, dep=0, name=None):
        pieces.append(dict(cost=cost, run=run, load=load, dep=dep, name=name))

    def down_dep(j):
        return index[(FDOWN, down_rows - rows, j * 256 // COLS * COLS)]

    piece(forward, 4.0, take_vectors, None, 0)
    for j in range(3 * width // COLS):
        piece(forward, 0.5, self_project(j), column_load(SQKV, j * COLS), index[(SQKV, 0, j * COLS)])
    for first in range(0, samples * pairs, 4):
        piece(forward, 1.2, self_attend(first, first + 4), None, 0)
    for j in range(per_half):
        piece(forward, 0.5, branch(self_attn, SELF_O, j), column_load(SOUT, j * COLS), index[(SOUT, 0, j * COLS)])
    piece(forward, 0.9, norm_one)
    piece(forward, 0.5, turn(x_in))
    piece(forward, 0.5, turn(self_attn))
    for target, at, first in ((cross_k, None, width), (cross_v, CROSS_V, 2 * width)):
        for j in range(per_half):
            col = first + j * COLS
            dep = index[(CQKV, 0, col)]
            piece(forward, 1.2, cross_project(target, at, j, 0), column_load(CQKV, col), dep)
            piece(forward, 1.2, cross_project(target, at, j, samples * mem_len // 512), "keep", dep)
    for j in range(per_half):
        piece(forward, 0.5, cross_query(j), column_load(CQKV, j * COLS), index[(CQKV, 0, j * COLS)])
    piece(forward, 0.5, turn(h1_low))
    for s in range(samples):
        for i in range(width // 256):
            piece(forward, 0.3 * (2 * (width // 256 - i) - 1) / 2, turn_memory(s, i))
    for first in range(0, samples * pairs, 2):
        piece(forward, 1.6, cross_attend(first, first + 2))
    for j in range(per_half):
        piece(forward, 0.5, branch(cross_attn, CROSS_O, j), column_load(COUT, j * COLS), index[(COUT, 0, j * COLS)])
    piece(forward, 0.9, norm_two)
    piece(forward, 0.5, turn(cross_attn))
    for j in range(hidden // COLS):
        piece(forward, 1.2, feed_up(j), column_load(FUP, j * COLS), index[(FUP, 0, j * COLS)])
    piece(forward, 0.5, turn(h2_low))
    for j in range(width // 256):
        piece(forward, 0.8, feed_down(j), quarter_load(j), down_dep(j))
    piece(forward, 2.0, norm_three)

    for i in range(4):
        piece(backward, 0.7, pre_back(i), group_load(i), name="pre%d" % i)
    for j in range(hidden // COLS):
        piece(backward, 0.3, flow_back(slope, 0, j), column_load(FUP, j * COLS))
    piece(backward, 0.9, norm_two_back, name="norm2")
    for j in range(per_half):
        piece(backward, 0.3, attn_back(d_cross, j), column_load(COUT, j * COLS))
    for first in range(0, samples * pairs):
        piece(backward, 1.2, cross_attend_back(first, first + 1), name="cross")
    for j in range(per_half):
        piece(backward, 0.3, flow_back(cross_q, 0, j), column_load(CQKV, j * COLS))
    piece(backward, 0.9, norm_one_back, name="norm1")
    for j in range(per_half):
        piece(backward, 0.3, attn_back(d_self, j), column_load(SOUT, j * COLS))
    for first in range(0, samples * pairs, 2):
        piece(backward, 1.0, self_attend_back(first, first + 2), name="self")
    piece(backward, 1.0, vector_sums, name="vectors")
    for j in range(3 * width // COLS):
        piece(backward, 0.3, flow_back(qkv, 0, j), column_load(SQKV, j * COLS))
    piece(backward, 0.5, target_done)
    tile_count = samples * mem_len // 512
    for half in range(2):
        for first in range(tile_count):
            piece(backward, 1.6, memory_back(half, range(first, first + 1)), half_load(half) if first == 0 else "keep")

    def prepare(pieces, holders):
        last = None
        for p in pieces:
            p["done"], p["started"] = False, 0
            p["copies"], p["deps"], p["after"], p["buffer"] = [], [], [], None
            if p["load"] == "keep":
                p["buffer"] = last["buffer"]
                for slot in last["load"]["takes"]:
                    holders[slot] = p
            elif p["load"] is not None:
                p["buffer"] = p["load"]["buffer"]
                for slot in p["load"]["takes"]:
                    if slot in holders:
                        p["after"].append(holders[slot])
                    holders[slot] = p
                for n, (src, dst, *dep) in enumerate(p["load"]["copies"]):
                    sem = r["load_sem"].at[p["load"]["takes"][0], n]
                    p["copies"].append(pltpu.make_async_copy(src, dst, sem))
                    p["deps"].append(dep[0] if dep else p["dep"])
                last = p

    def start(p, ready):
        while p["started"] < len(p["copies"]) and p["deps"][p["started"]] <= ready:
            p["copies"][p["started"]].start()
            p["started"] += 1

    def look_ahead(pieces, ready):
        for later in pieces[:AHEAD]:
            if all(p["done"] for p in later["after"]):
                start(later, ready)
            if later["dep"] > ready:
                break

    def run_piece(pieces, ready):
        p = pieces.pop(0)
        start(p, ready)
        look_ahead(pieces, ready)
        for copy in p["copies"]:
            copy.wait()
        if p["buffer"] is not None:
            p["run"](p["buffer"])
        else:
            p["run"]()
        p["done"] = True
        return p

    def work(pieces, ready, limit):
        spent = 0.0
        look_ahead(pieces, ready)
        while pieces and pieces[0]["dep"] <= ready and spent < limit:
            spent += run_piece(pieces, ready)["cost"]

    holders = {}
    prepare(forward, holders)
    prepare(backward, holders)


    in_copies = [
        pltpu.make_async_copy(r["mem_hbm"], mem, r["in_sem"].at[0]),
        pltpu.make_async_copy(r["cot_hbm"], cot, r["in_sem"].at[1]),
        pltpu.make_async_copy(r["x_hbm"], x_in, r["in_sem"].at[2]),
    ]

    def block(ref, k, *lead):
        _, row, row_count, col, cols = chunks[k]
        return ref.at[(*lead, pl.ds(row, row_count), pl.ds(col, cols))]

    def gathered(k, *lead):
        return block(whole[chunks[k][0]], k, *lead)

    local = []
    for a in range(7):
        copy = pltpu.make_async_copy(shards[a], whole[a].at[far, y, core, x], r["local_sem"].at[a])
        copy.start()
        local.append(copy)
    greet(me)
    for copy in in_copies:
        copy.start()

    sent = {}

    def go(k, copy):
        copy.start()
        sent.setdefault(k, []).append(copy)
        return copy

    far_copies, near_copies, other_copies, pass_copies, twin_copies = {}, {}, {}, {}, {}
    last_lane = far_count - 1
    gsend, grecv = r["gsend"], r["grecv"]

    def send(k, lane, ref, device):
        return go(k, remote(ref, ref, gsend.at[k, lane], grecv.at[k, lane], device))

    def start_far(k):
        far_copies[k] = [
            go(
                k,
                remote(
                    block(shards[chunks[k][0]], k),
                    gathered(k, far, y, core, x),
                    gsend.at[k, d],
                    grecv.at[k, d],
                    device,
                )
            )
            for d, (_, device) in enumerate(me["far_devices"])
        ]
        if cross_way[k]:
            near_copies[k] = go(
                k,
                remote(
                    block(shards[chunks[k][0]], k),
                    gathered(k, far, y, core, x),
                    gsend.at[k, last_lane],
                    grecv.at[k, last_lane],
                    me["near_device"],
                )
            )

    def start_near(k):
        column = gathered(k, far_all, y, core, x)
        other_copies[k] = send(k, last_lane + 1, column, me["other_device"])
        if cross_way[k]:
            near_copies[k].wait_recv()
            landed = gathered(k, far, near[0], core, near[1])
            near_copies[k] = [
                send(k, last_lane + 4 + d, landed, device) for d, (_, device) in enumerate(me["far_devices"])
            ]
        else:
            near_copies[k] = [send(k, last_lane, column, me["near_device"])]

    def start_pass(k):
        pass_copies[k] = send(k, last_lane + 2, gathered(k, far_all, near[0], core, near[1]), me["other_device"])

    def start_twin(k):
        half = gathered(k, far_all, pl.ds(0, 2), core, pl.ds(0, 2))
        twin_copies[k] = send(k, last_lane + 3, half, me["twin_device"])

    cross_way = [crossed(far_count, GATHER_CROSSED, chunk[0], k) for k, chunk in enumerate(chunks)]
    skew = GATHER_SKEW
    for t in range(count + 3 * skew + 1):
        k = t - 3 * skew
        if 0 <= k < count:
            other_copies[k].wait_recv()
            pass_copies[k].wait_recv()
            start_twin(k)
        k = t - 2 * skew
        if 0 <= k < count:
            for copy in near_copies[k]:
                copy.wait_recv()
            start_pass(k)
        k = t - skew
        if 0 <= k < count:
            if k == 0:
                for copy in local:
                    copy.wait()
            for copy in far_copies[k]:
                copy.wait_recv()
            start_near(k)
        if t < count:
            start_far(t)
        k = t - 3 * skew - 1
        if k >= 0:
            if k == 0:
                for copy in in_copies:
                    copy.wait()
            twin_copies[k].wait_recv()
            if k >= 2:
                for copy in sent.pop(k - 2):
                    copy.wait_send()
            work(forward, k, FORWARD_WORK)
    work(forward, count, 1e9)


    own, total, from_other, from_near, from_far = (
        r[n] for n in ("own", "total", "from_other", "from_near", "from_far")
    )
    small_buffers = (r["small_pack"], r["total_s"], r["from_other_s"], r["from_near_s"], r["from_far_s"])
    out_chunks = scatter_chunks(width)
    out_count = len(out_chunks)
    last_chunk = {chunk[0]: k for k, chunk in enumerate(out_chunks)}
    skew = SCATTER_SKEW
    own_slots, total_slots = own.shape[0], total.shape[0]
    other_slots, land_slots = from_other.shape[0], from_near.shape[0]
    from_near_far = r["from_near_far"]
    ssend, srecv = r["ssend"], r["srecv"]

    def buffers(k):
        if out_chunks[k][0] == SMALL:
            return small_buffers
        return (
            own.at[k % own_slots],
            total.at[k % total_slots],
            from_other.at[k % other_slots],
            from_near.at[k % land_slots],
            from_far.at[k % land_slots],
        )

    def compute(k):
        a, col = out_chunks[k]
        if a == SMALL:
            return
        target = buffers(k)[0]
        if a == FDOWN:
            right = d_ffn[:, pl.ds(col, 128)]
            for i in range(hidden // width):
                value = dot(act_t[i * width : (i + 1) * width], right).astype(BF16)
                for piece_at in range(0, width, rows):
                    b = (i * width + piece_at) // down_rows
                    q = piece_at % down_rows // rows
                    target[b // 8, (b // 4) % 2, (b // 2) % 2, b % 2, :, q * 128 : (q + 1) * 128] = value[
                        piece_at : piece_at + rows
                    ]
            return
        left, right = {
            FUP: (h2_low, slope),
            COUT: (cross_attn, d_cross),
            SOUT: (self_attn, d_self),
            SQKV: (x_in, qkv),
            CQKV: (
                (h1_low, cross_q),
                (mem, cross_k),
                (mem, cross_v),
            )[col // width if a == CQKV else 0],
        }[a]
        first = col % width if a == CQKV else col
        cols_at = pl.ds(first, COLS)
        if left is mem:
            part_rows = 512
            for i in range(0, width, part_rows):
                value = None
                for s in range(samples):
                    part = dot(
                        mem[s * mem_len + i : s * mem_len + i + part_rows],
                        right[pl.ds(s * mem_len, mem_len), cols_at],
                    )
                    value = part if value is None else value + part
                store_blocks(target, i, value.astype(BF16))
        else:
            turned = [left[:, i : i + 256] for i in range(0, width, 256)]
            value = dot(jnp.concatenate(turned, axis=0), right[:, cols_at])
            store_blocks(target, 0, value.astype(BF16))

    def store_blocks(target, first, value):
        for at in range(0, value.shape[0], rows):
            b = (first + at) // rows
            target[b // 8, (b // 4) % 2, (b // 2) % 2, b % 2] = value[at : at + rows]

    twins, others, nears, fars, near_fars = {}, {}, {}, {}, {}
    cross_out = [crossed(far_count, SCATTER_CROSSED, chunk[0], k) for k, chunk in enumerate(out_chunks)]

    def start_twin_sum(k):
        target, landing = buffers(k)[:2]
        twins[k] = remote(
            target.at[far_all, pl.ds(0, 2), 1 - core, pl.ds(0, 2)],
            landing,
            ssend.at[k, 0],
            srecv.at[k, 0],
            me["twin_device"],
        )
        twins[k].start()

    def add_own(k):
        mine, running = buffers(k)[:2]

        def body(i, carry):
            f, yy, xx = i // 4, (i // 2) % 2, i % 2
            running[f, yy, xx] = running[f, yy, xx] + mine[f, yy, core, xx]
            return carry

        lax.fori_loop(0, far_count * 4, body, 0)

    def start_others(k):
        running, landing = buffers(k)[1:3]
        others[k] = []
        for i, place in enumerate((diagonal, other)):
            copy = remote(
                running.at[far_all, place[0], place[1]],
                landing.at[i],
                ssend.at[k, 1 + i],
                srecv.at[k, 1 + i],
                me["other_device"],
            )
            copy.start()
            others[k].append(copy)

    def add_other(k, i):
        running, landing = buffers(k)[1:3]
        place = (near, (y, x))[i]

        def body(f, carry):
            running[f, place[0], place[1]] = running[f, place[0], place[1]] + landing[i, f]
            return carry

        lax.fori_loop(0, far_count, body, 0)

    def start_near_sum(k):
        _, running, _, landing, _ = buffers(k)
        source, target = running.at[far_all, near[0], near[1]], landing
        if cross_out[k]:
            source, target = running.at[far, near[0], near[1]], landing.at[0]
        nears[k] = remote(source, target, ssend.at[k, 3], srecv.at[k, 3], me["near_device"])
        nears[k].start()

    def start_near_fars(k):
        running, landing = buffers(k)[1], from_near_far.at[k % land_slots]
        near_fars[k] = []
        for d, (target, device) in enumerate(me["far_devices"]):
            lane = far_count + 3 + d
            copy = remote(
                running.at[target, near[0], near[1]], landing.at[d], ssend.at[k, lane], srecv.at[k, lane], device
            )
            copy.start()
            near_fars[k].append(copy)

    def add_near_fars(k):
        running, landing = buffers(k)[1], from_near_far.at[k % land_slots]
        result = running[far, near[0], near[1]].astype(F32)
        for d in range(far_count - 1):
            result += landing[d].astype(F32)
        running[far, near[0], near[1]] = result.astype(BF16)

    def add_near(k):
        _, running, _, landing, _ = buffers(k)

        def body(f, carry):
            running[f, y, x] = running[f, y, x] + landing[f]
            return carry

        lax.fori_loop(0, far_count, body, 0)

    def start_fars(k):
        _, running, _, _, landing = buffers(k)
        fars[k] = []
        for d, (target, device) in enumerate(me["far_devices"]):
            copy = remote(running.at[target, y, x], landing.at[d], ssend.at[k, 4 + d], srecv.at[k, 4 + d], device)
            copy.start()
            fars[k].append(copy)

    def finish(k):
        _, running, _, _, landing = buffers(k)
        a, col = out_chunks[k]
        result = running[far, y, x].astype(F32)
        for d in range(far_count - 1):
            result += landing[d].astype(F32)
        if cross_out[k]:
            result += buffers(k)[3][0].astype(F32)
        if a == SMALL:
            lane = (far * 8 + y * 4 + core * 2 + x) * rows % 128
            up_lane = (far * 8 + y * 4 + core * 2 + x) * down_rows % 128
            vectors = pltpu.roll(result, (128 - lane) % 128, 1)
            ups = pltpu.roll(result, (128 - up_lane) % 128, 1)
            row = lax.broadcasted_iota(jnp.int32, result.shape, 0)
            sums[a][...] = jnp.where(row == VECTORS, ups, vectors)
        elif a == FDOWN:
            for q in range(4):
                sums[a][q * rows : (q + 1) * rows, pl.ds(col, 128)] = result[:, q * 128 : (q + 1) * 128]
        else:
            sums[a][:, pl.ds(col, COLS)] = result
        if k == last_chunk[a]:
            hand_out(sums[a], r["o%d" % a], a)
        for copy in (*others[k], nears[k], *fars[k], *near_fars.get(k, ())):
            copy.wait_send()

    needs = {FUP: "pre3", COUT: "norm2", CQKV: "cross", SOUT: "norm1", SQKV: "self", SMALL: "vectors"}

    def make_chunk(k):
        need = needs.get(out_chunks[k][0])
        while any(p["name"] == need for p in backward if need):
            run_piece(backward, count)
        compute(k)

    make_chunk(0)
    for t in range(out_count + 4 * skew):
        k = t - 4 * skew
        if 0 <= k < out_count:
            for copy in fars[k]:
                copy.wait_recv()
            if cross_out[k]:
                nears[k].wait_recv()
            finish(k)
        k = t - 3 * skew
        if 0 <= k < out_count:
            if cross_out[k]:
                for copy in near_fars[k]:
                    copy.wait_recv()
                add_near_fars(k)
                start_near_sum(k)
            else:
                nears[k].wait_recv()
                add_near(k)
                start_fars(k)
        k = t - 2 * skew
        if 0 <= k < out_count:
            others[k][0].wait_recv()
            add_other(k, 0)
            if cross_out[k]:
                start_near_fars(k)
            else:
                start_near_sum(k)
            others[k][1].wait_recv()
            add_other(k, 1)
            if cross_out[k]:
                start_fars(k)
        k = t - skew
        if 0 <= k < out_count:
            twins[k].wait()
            add_own(k)
            start_others(k)
        if t < out_count:
            start_twin_sum(t)
        if t + 1 < out_count:
            make_chunk(t + 1)
        work(backward, count, BACKWARD_WORK)
    work(backward, count, 1e9)
    for copy in (*stage_copies[-2:], *out_copies):
        copy.wait()
    for copies in sent.values():
        for copy in copies:
            copy.wait_send()


def hand_over_kernel(parts, n, *refs):
    ins, outs, buffers = refs[:n], refs[n : 2 * n], refs[2 * n : 3 * n]
    in_sem, out_sem = refs[3 * n :]

    def copies(ref_from, ref_to, sem):
        return [
            pltpu.make_async_copy(ref_from[a].at[pl.ds(row, count)], ref_to[a].at[pl.ds(row, count)], sem.at[i])
            for i, (a, row, count) in enumerate(parts)
        ]

    arriving, leaving = copies(ins, buffers, in_sem), copies(buffers, outs, out_sem)
    for copy in arriving:
        copy.start()
    for arrived, left in zip(arriving, leaving):
        arrived.wait()
        left.start()
    for copy in leaving:
        copy.wait()


def hand_over(arrays):
    n = len(arrays)
    parts = []
    for a, v in enumerate(arrays):
        count = 512 if v.shape[0] > 512 else v.shape[0]
        parts += [(a, row, count) for row in range(0, v.shape[0], count)]
    anywhere = pl.BlockSpec(memory_space=pl.ANY)
    return pl.pallas_call(
        functools.partial(hand_over_kernel, parts, n),
        out_shape=[jax.ShapeDtypeStruct(v.shape, v.dtype) for v in arrays],
        in_specs=[anywhere] * n,
        out_specs=[anywhere] * n,
        scratch_shapes=[pltpu.VMEM(v.shape, v.dtype) for v in arrays]
        + [pltpu.SemaphoreType.DMA((len(parts),))] * 2,
        compiler_params=pltpu.CompilerParams(vmem_limit_bytes=63 * 2**20),
        name="hand_over",
    )(*arrays)


def layer(mesh, target_input, memory, cotangent, mem_lengths, tgt_lengths, shards, small):
    samples, tgt_len, width = target_input.shape
    mem_len = memory.shape[1]
    far_count = mesh.shape["wide"] // 4
    rows = shards[SQKV].shape[0]
    tokens, keys, hidden = samples * tgt_len, samples * mem_len, 4 * width
    lanes = far_count + 3 + (3 if far_count == 4 else 0)
    count = len(gather_chunks([s.shape for s in shards])[0])
    out_count = len(scatter_chunks(width))
    lead = (far_count, 2, 2, 2)
    total_slots, own_slots = 5 * SCATTER_SKEW + 1, SCATTER_SKEW + 1
    other_slots, land_slots = 2 * SCATTER_SKEW + 1, (4 if far_count == 4 else 3) * SCATTER_SKEW

    def vmem(shape, dtype=BF16):
        return pltpu.VMEM(shape, dtype)

    small_sum = (SMALL_ROWS, 128)
    scratch = [vmem(v.shape, F32) for v in shards] + [
        vmem(small_sum, F32),
        vmem((tokens, width)),
        vmem((keys, width)),
        vmem((tokens, width)),
        vmem((tokens, 3 * width)),
        vmem((tokens, width)),
        vmem((tokens, width), F32),
        vmem((tokens, 1), F32),
        vmem((tokens, width), F32),
        vmem((tokens, width)),
        vmem((tokens, width)),
        vmem((keys, width)),
        vmem((keys, width)),
        vmem((tokens, width)),
        vmem((tokens, width), F32),
        vmem((tokens, 1), F32),
        vmem((tokens, width), F32),
        vmem((tokens, width)),
        vmem((tokens, hidden)),
        vmem((hidden, tokens)),
        vmem((tokens, hidden)),
        vmem((tokens, width), F32),
        vmem((tokens, width)),
        vmem((tokens, width)),
        vmem((tokens, width)),
        vmem((tokens, width)),
        vmem((samples * HEADS // 2, 2 * tgt_len), F32),
        vmem((samples * HEADS // 2, 2 * tgt_len), F32),
        vmem((24, width), F32),
        vmem((24, width), F32),
        vmem((2, 512, width // 2)),
        vmem((4,) + lead + (rows, COLS)),
        vmem((2,) + lead + (4 * rows, 256)),
        vmem(lead + (SMALL_ROWS, 128)),
        vmem((SMALL_ROWS, mesh.size, 128), F32),
        vmem(lead + small_sum, F32),
        vmem((own_slots,) + lead + (rows, COLS)),
        vmem((total_slots, far_count, 2, 2, rows, COLS)),
        vmem((other_slots, 2, far_count, rows, COLS)),
        vmem((land_slots, far_count, rows, COLS)),
        vmem((land_slots, far_count - 1, rows, COLS)),
        vmem((land_slots if far_count == 4 else 1, 3, rows, COLS)),
        vmem((far_count, 2, 2) + small_sum, F32),
        vmem((2, far_count) + small_sum, F32),
        vmem((far_count,) + small_sum, F32),
        vmem((far_count - 1,) + small_sum, F32),
        pltpu.SemaphoreType.DMA((6, 4)),
        pltpu.SemaphoreType.DMA((3,)),
        pltpu.SemaphoreType.DMA((7,)),
        pltpu.SemaphoreType.DMA((count, lanes)),
        pltpu.SemaphoreType.DMA((count, lanes)),
        pltpu.SemaphoreType.DMA((out_count, lanes)),
        pltpu.SemaphoreType.DMA((out_count, lanes)),
        pltpu.SemaphoreType.DMA((2,)),
        pltpu.SemaphoreType.DMA((9,)),
    ]
    in_vmem, anywhere = pl.BlockSpec(memory_space=pltpu.VMEM), pl.BlockSpec(memory_space=pl.ANY)
    in_smem = pl.BlockSpec(memory_space=pltpu.SMEM)
    out_shape = [
        jax.ShapeDtypeStruct((tokens, width), BF16),
        jax.ShapeDtypeStruct((tokens, width), BF16),
        jax.ShapeDtypeStruct((keys, width), BF16),
    ]
    out_shape += [jax.ShapeDtypeStruct(s.shape, F32) for s in shards]
    out_shape += [jax.ShapeDtypeStruct(small_sum, F32)]
    out_shape += [jax.ShapeDtypeStruct(lead + s.shape, BF16) for s in shards]
    outs = pl.pallas_call(
        functools.partial(layer_kernel, (far_count, rows, width, samples, tgt_len, mem_len)),
        out_shape=out_shape,
        in_specs=[anywhere, anywhere, anywhere, in_smem, in_smem] + [in_vmem] * 7,
        out_specs=[anywhere] * 16,
        scratch_shapes=scratch,
        compiler_params=pltpu.CompilerParams(
            collective_id=0, has_side_effects=True, vmem_limit_bytes=63 * 2**20
        ),
        cost_estimate=pl.CostEstimate(flops=52 * 10**9, bytes_accessed=10**8, transcendentals=10**7),
        name="decoder_layer",
    )(
        target_input.reshape(tokens, width),
        memory.reshape(keys, width),
        cotangent.reshape(tokens, width),
        mem_lengths,
        tgt_lengths,
        *shards,
        small,
    )
    return (*hand_over(outs[:9]), outs[9])


def step(
    mesh,
    target_input,
    memory,
    cotangent,
    mem_lengths,
    tgt_lengths,
    self_qkv,
    self_out,
    self_bias,
    norm1_gain,
    norm1_shift,
    cross_qkv,
    cross_out,
    cross_bias,
    norm2_gain,
    norm2_shift,
    ffn_up,
    up_bias,
    ffn_down,
    down_bias,
    norm3_gain,
    norm3_shift,
):
    per, up_per = norm1_gain.shape[0], up_bias.shape[0]
    small = jnp.zeros((SMALL_ROWS, 128), BF16)
    row = 0
    for v in (
        self_bias, norm1_gain, norm1_shift, cross_bias, norm2_gain, norm2_shift,
        down_bias, norm3_gain, norm3_shift, up_bias,
    ):
        v = v.reshape(-1, v.shape[-1])
        small += jnp.pad(v, ((row, SMALL_ROWS - row - v.shape[0]), (0, 128 - v.shape[1])))
        row += v.shape[0]
    block_out, target_grad, memory_grad, *grads, sums = layer(
        mesh, target_input, memory, cotangent, mem_lengths, tgt_lengths,
        [self_qkv, self_out, cross_qkv, cross_out, ffn_up, ffn_down], small,
    )
    return (
        block_out.reshape(target_input.shape),
        target_grad.reshape(target_input.shape),
        memory_grad.reshape(memory.shape),
        grads[SQKV],
        grads[SOUT],
        sums[SELF_Q : SELF_Q + 3, :per],
        sums[GAIN1, :per],
        sums[SHIFT1, :per],
        grads[CQKV],
        grads[COUT],
        sums[CROSS_Q : CROSS_Q + 3, :per],
        sums[GAIN2, :per],
        sums[SHIFT2, :per],
        grads[FUP],
        sums[VECTORS, :up_per],
        grads[FDOWN],
        sums[DOWN, :per],
        sums[GAIN3, :per],
        sums[SHIFT3, :per],
    )


def solution(mesh):
    both = ("wide", "narrow")
    stream, matrix_spec, vector_spec, bias_spec = P(both, None, None), P(both, None), P(both), P(None, both)
    weights = (
        matrix_spec, matrix_spec, bias_spec, vector_spec, vector_spec,
        matrix_spec, matrix_spec, bias_spec, vector_spec, vector_spec,
        matrix_spec, vector_spec, matrix_spec, vector_spec, vector_spec, vector_spec,
    )
    return jax.shard_map(
        functools.partial(step, mesh),
        mesh=mesh,
        in_specs=(stream, stream, stream, vector_spec, vector_spec) + weights,
        out_specs=(stream, stream, stream) + weights,
        check_vma=False,
    )
```

```python
import functools
import math

import jax
import jax.numpy as jnp
from jax import lax
from jax.experimental import pallas as pl
from jax.experimental.pallas import tpu as pltpu
from jax.sharding import PartitionSpec as P

MESH = pl.DeviceIdType.MESH
HEADS = 16
HEAD_DIM = 64
NORM_EPSILON = 1e-05
MASK_VALUE = -1e30
COLS = 512
GATHER_SKEW = 4
SCATTER_SKEW = 2
FORWARD_WORK = 1.5
BACKWARD_WORK = 1.6
HEAVY_WORK = 1.0
GATHER_CROSSED = (0, 1, 0, 1, 1)
SCATTER_CROSSED = (0, 0, 1)
AHEAD = 8
SMALL_ROWS = 16

F32 = jnp.float32
BF16 = jnp.bfloat16

SELF_Q, SELF_V, SELF_O, GAIN1, SHIFT1, CROSS_Q, CROSS_V, CROSS_O, GAIN2, SHIFT2, DOWN, GAIN3, SHIFT3, UP = range(14)
VECTORS = 13


def dot(a, b):
    return lax.dot_general(a, b, (((1,), (0,)), ((), ())), preferred_element_type=F32)


def dot_nt(a, b):
    return lax.dot_general(a, b, (((1,), (1,)), ((), ())), preferred_element_type=F32)


def dot_tn(a, b):
    return lax.dot_general(a, b, (((0,), (0,)), ((), ())), preferred_element_type=F32)


def places(far_count):
    wide = lax.axis_index("wide")
    x = lax.axis_index("narrow")
    far = wide // 4
    y = (wide // 2) % 2
    core = wide % 2
    near_y = y + core * (1 - 2 * y)
    near_x = x + (1 - core) * (1 - 2 * x)
    other_y = y + (1 - core) * (1 - 2 * y)
    other_x = x + core * (1 - 2 * x)

    def device(f, yy, cc, xx):
        return (f * 4 + yy * 2 + cc, xx)

    return dict(
        far=far,
        y=y,
        core=core,
        x=x,
        near=(near_y, near_x),
        other=(other_y, other_x),
        diagonal=(1 - y, 1 - x),
        near_device=device(far, near_y, core, near_x),
        other_device=device(far, other_y, core, other_x),
        twin_device=device(far, y, 1 - core, x),
        far_devices=[
            (lax.rem(far + d, far_count), device(lax.rem(far + d, far_count), y, core, x))
            for d in range(1, far_count)
        ],
    )


def greet(where):
    barrier = pltpu.get_barrier_semaphore()
    partners = [where["near_device"], where["other_device"], where["twin_device"]]
    partners += [device for _, device in where["far_devices"]]
    for device in partners:
        pl.semaphore_signal(barrier, inc=1, device_id=device, device_id_type=MESH)
    pl.semaphore_wait(barrier, len(partners))


def remote(src, dst, send_sem, recv_sem, device):
    return pltpu.make_async_remote_copy(
        src_ref=src,
        dst_ref=dst,
        send_sem=send_sem,
        recv_sem=recv_sem,
        device_id=device,
        device_id_type=MESH,
    )


def matrix(value):
    rows, cols = value.shape[-2:]
    if rows % 16:
        return value.astype(F32).reshape(-1, cols).astype(BF16)
    return value.reshape(-1, cols)


ARRAYS = ("self_qkv", "self_out", "cross_qkv", "cross_out", "ffn_up", "ffn_down")
SQKV, SOUT, CQKV, COUT, FUP, FDOWN, SMALL = range(7)


def crossed(far_count, pattern, array, k):
    return far_count == 4 and array != SMALL and pattern[k % len(pattern)] == 1


def gather_chunks(shapes):
    rows = shapes[SQKV][0]
    width = shapes[SOUT][1]
    chunks = [(SMALL, 0, SMALL_ROWS, 0, 128)]
    for a, first, last in (
        (SQKV, 0, 3 * width),
        (SOUT, 0, width),
        (CQKV, width, 3 * width),
        (CQKV, 0, width),
        (COUT, 0, width),
        (FUP, 0, 4 * width),
    ):
        chunks += [(a, 0, rows, col, COLS) for col in range(first, last, COLS)]
    for col in range(0, width, COLS):
        chunks += [(FDOWN, row, rows, col, COLS) for row in range(0, 4 * rows, rows)]
    index = {(a, row, col): k for k, (a, row, _, col, _) in enumerate(chunks)}
    return chunks, index


def scatter_chunks(width):
    chunks = [(FDOWN, 128 * j) for j in range(width // 128)]
    for a, first, last in (
        (FUP, 0, 4 * width),
        (COUT, 0, width),
        (CQKV, 0, 3 * width),
        (SOUT, 0, width),
    ):
        chunks += [(a, col) for col in range(first, last, COLS)]
    chunks += [(SMALL, 0)]
    chunks += [(SQKV, col) for col in range(0, 3 * width, COLS)]
    return chunks


def layer_kernel(cfg, *refs):
    far_count, rows, width, samples, tgt_len, mem_len = cfg
    devices = 8 * far_count
    hidden = 4 * width
    down_rows = 4 * rows
    tokens = samples * tgt_len
    pairs = HEADS // 2
    scale = 1.0 / math.sqrt(HEAD_DIM)
    zs = max(1, far_count // 4)
    zh = max(1, far_count // 2)

    names = (
        "x_hbm", "mem_hbm", "cot_hbm", "mem_lengths", "tgt_lengths", "i0", "i1", "i2", "i3", "i4", "i5", "i6",
        "block_out", "target_grad", "memory_grad", "o0", "o1", "o2", "o3", "o4", "o5", "o6", "w0", "w1", "w2", "w3",
        "w4", "w5", "g0", "g1", "g2", "g3", "g4", "g5", "small_out", "x", "mem", "cot", "qkv", "self_attn", "n1",
        "r1", "h1", "h1_low", "cross_q", "cross_k", "cross_v", "cross_attn", "n2", "r2", "flow", "h2_low", "act",
        "act_t", "slope", "acc", "d_ffn", "d_cross", "d_attn", "d_self", "self_lse", "cross_lse", "vecs", "gvecs",
        "staged", "wbuf", "wquarter", "small_in", "small_rows", "small_pack", "own", "total", "from_other",
        "from_near", "from_far", "from_near_far", "total_s", "from_other_s", "from_near_s", "from_far_s",
        "load_sem", "in_sem", "local_sem", "gsend", "grecv", "ssend", "srecv", "stage_sem", "out_sem",
    )
    r = dict(zip(names, refs, strict=True))
    x_in, mem, cot = r["x"], r["mem"], r["cot"]
    qkv, self_attn, n1, r1, h1, h1_low = (r[n] for n in ("qkv", "self_attn", "n1", "r1", "h1", "h1_low"))
    cross_q, cross_k, cross_v, cross_attn = (r[n] for n in ("cross_q", "cross_k", "cross_v", "cross_attn"))
    n2, r2, flow, h2_low = (r[n] for n in ("n2", "r2", "flow", "h2_low"))
    act, act_t, slope, acc = (r[n] for n in ("act", "act_t", "slope", "acc"))
    d_ffn, d_cross, d_attn, d_self = (r[n] for n in ("d_ffn", "d_cross", "d_attn", "d_self"))
    vecs, gvecs = r["vecs"], r["gvecs"]
    shards = [r["i%d" % i] for i in range(7)]
    whole = [r["w%d" % i] for i in range(6)] + [r["small_in"]]
    sums = [r["g%d" % i] for i in range(6)] + [r["small_out"]]

    me = places(far_count)
    far, y, core, x = me["far"], me["y"], me["core"], me["x"]
    far_all = pl.ds(0, far_count)
    near, other, diagonal = me["near"], me["other"], me["diagonal"]

    def vec(i, col=0, cols=width):
        return vecs[pl.ds(i, 1), pl.ds(col, cols)]


    def owner_of(per, first):
        device = lax.broadcasted_iota(jnp.int32, (devices, width), 0)
        column = lax.broadcasted_iota(jnp.int32, (devices, width), 1) + first
        return lax.shift_right_logical(column, per.bit_length() - 1) == device

    def spread_of(per):
        lane = lax.broadcasted_iota(jnp.int32, (128, width), 0)
        column = lax.broadcasted_iota(jnp.int32, (128, width), 1)
        return (lane == jnp.bitwise_and(column, per - 1)).astype(F32).astype(BF16)

    def take_vectors():
        small_in, table = r["small_in"], r["small_rows"]

        def body(b, carry):
            tile = small_in[b // 8, (b // 4) % 2, (b // 2) % 2, b % 2].astype(F32)
            for i in range(VECTORS + 1):
                table[i, pl.ds(b, 1), :] = tile[i : i + 1]
            return carry

        lax.fori_loop(0, devices, body, 0)
        spread, owner = spread_of(rows), owner_of(rows, 0)
        for i in range(VECTORS):
            values = dot(table[i].astype(BF16), spread)
            vecs[pl.ds(i, 1), :] = jnp.sum(jnp.where(owner, values, 0.0), axis=0, keepdims=True)
        values = dot(table[VECTORS].astype(BF16), spread_of(down_rows))
        for j in range(4):
            owner = owner_of(down_rows, j * width)
            vecs[pl.ds(UP + j, 1), :] = jnp.sum(jnp.where(owner, values, 0.0), axis=0, keepdims=True)

    def pack_vectors():
        pack = r["small_pack"]

        pack[...] = jnp.zeros_like(pack)
        for b in range(devices):
            lead = (b // 8, (b // 4) % 2, (b // 2) % 2, b % 2)
            lane, up_lane = b * rows // 128 * 128, b * down_rows % width // 128 * 128
            up_row = UP + b * down_rows // width
            pack[(*lead, slice(0, VECTORS))] = gvecs[0:VECTORS, lane : lane + 128]
            pack[(*lead, slice(VECTORS, VECTORS + 1))] = gvecs[up_row : up_row + 1, up_lane : up_lane + 128]

    def turn(ref, first=0, cols=width):
        def run():
            def body(i, carry):
                cols_at = pl.ds(pl.multiple_of(first + i * 256, 256), 256)
                ref[:, cols_at] = ref[:, cols_at].T
                return carry

            lax.fori_loop(0, cols // 256, body, 0)

        return run

    def turn_memory(s, i):
        def run():
            blocks = width // 256

            def at(i, j):
                return (
                    pl.ds(pl.multiple_of(s * mem_len + i * 256, 256), 256),
                    pl.ds(pl.multiple_of(j * 256, 256), 256),
                )

            mem[at(i, i)] = mem[at(i, i)].T
            for j in range(i + 1, blocks):
                upper, lower = mem[at(i, j)].T, mem[at(j, i)].T
                mem[at(i, j)] = lower
                mem[at(j, i)] = upper

        return run

    def self_project(j):
        def run(w):
            value = dot(x_in[...], matrix(w[...]))
            cols = pl.ds(j * COLS, COLS)
            part, first = j * COLS // width, j * COLS % width
            if part == 0:
                value = (value + vec(SELF_Q, first, COLS)) * scale
            if part == 2:
                value = value + vec(SELF_V, first, COLS)
            qkv[:, cols] = value.astype(BF16)

        return run

    def head_masks():
        lane = lax.broadcasted_iota(jnp.int32, (1, 128), 1)
        low = (lane < HEAD_DIM).astype(F32).astype(BF16)
        return low, (lane >= HEAD_DIM).astype(F32).astype(BF16)

    def both_heads(two):
        low, high = head_masks()
        return jnp.concatenate([two * low, two * high], axis=0)

    def one_row_each(stacked):
        lane = lax.broadcasted_iota(jnp.int32, (tgt_len, 128), 1)
        return jnp.where(lane < HEAD_DIM, stacked[:tgt_len], stacked[tgt_len:])

    def scores_of(keys, queries, length, causal):
        scores = dot_nt(keys, queries)
        key = lax.broadcasted_iota(jnp.int32, scores.shape, 0)
        usable = key < length
        if causal:
            query = jnp.bitwise_and(lax.broadcasted_iota(jnp.int32, scores.shape, 1), tgt_len - 1)
            usable = usable & (key <= query)
        return jnp.where(usable, scores, MASK_VALUE)

    def attend(u, queries, q_at, keys, k_at, values, v_at, key_count, lengths, causal, out, lse):
        s, pair = u // pairs, u % pairs
        lane = pair * 128
        q_rows = pl.ds(pl.multiple_of(s * tgt_len, tgt_len), tgt_len)
        k_rows = pl.ds(pl.multiple_of(s * key_count, key_count), key_count)

        def cols(first):
            return pl.ds(pl.multiple_of(first + lane, 128), 128)

        stacked = both_heads(queries[q_rows, cols(q_at)])
        scores = scores_of(keys[k_rows, cols(k_at)], stacked, lengths[s], causal)
        peak = jnp.max(scores, axis=0, keepdims=True)
        exponentials = jnp.exp(scores - peak)
        total = jnp.sum(exponentials, axis=0, keepdims=True)
        probs = (exponentials * (1.0 / total)).astype(BF16)
        mixed = dot_tn(values[k_rows, cols(v_at)], probs)
        out[q_rows, cols(0)] = one_row_each(mixed.T).astype(BF16)
        lse[pl.ds(u, 1), :] = peak + jnp.log(total)

    def attend_back(u, queries, q_at, keys, k_at, values, v_at, key_count, lengths, causal, lse, value_sum):
        s, pair = u // pairs, u % pairs
        lane = pair * 128
        q_rows = pl.ds(pl.multiple_of(s * tgt_len, tgt_len), tgt_len)
        k_rows = pl.ds(pl.multiple_of(s * key_count, key_count), key_count)

        def cols(first):
            return pl.ds(pl.multiple_of(first + lane, 128), 128)

        stacked = both_heads(queries[q_rows, cols(q_at)])
        upstream = both_heads(d_attn[q_rows, cols(0)])
        key_rows = keys[k_rows, cols(k_at)]
        scores = scores_of(key_rows, stacked, lengths[s], causal)
        probs = jnp.exp(scores - lse[pl.ds(u, 1), :])
        prob_grad = dot_nt(values[k_rows, cols(v_at)], upstream)
        delta = jnp.sum(probs * prob_grad, axis=0, keepdims=True)
        score_grad = (probs * (prob_grad - delta)).astype(BF16)
        query_grad = dot_tn(key_rows, score_grad)
        value_grad = dot(probs.astype(BF16), upstream).astype(BF16)
        values[k_rows, cols(v_at)] = value_grad
        keys[k_rows, cols(k_at)] = dot(score_grad, stacked).astype(BF16)
        queries[q_rows, cols(q_at)] = (one_row_each(query_grad.T) * scale).astype(BF16)
        gvecs[pl.ds(value_sum, 1), cols(0)] += jnp.sum(value_grad.astype(F32), axis=0, keepdims=True)

    def self_attend(first, last):
        def body(u, carry):
            attend(u, qkv, 0, qkv, width, qkv, 2 * width, tgt_len, r["tgt_lengths"], True,
                   self_attn, r["self_lse"])
            return carry

        return lambda: lax.fori_loop(first, last, body, 0)

    def cross_attend(first, last):
        def body(u, carry):
            attend(u, cross_q, 0, cross_k, 0, cross_v, 0, mem_len, r["mem_lengths"], False,
                   cross_attn, r["cross_lse"])
            return carry

        return lambda: lax.fori_loop(first, last, body, 0)

    def self_attend_back(first, last):
        def body(u, carry):
            attend_back(u, qkv, 0, qkv, width, qkv, 2 * width, tgt_len, r["tgt_lengths"], True,
                        r["self_lse"], SELF_V)
            return carry

        return lambda: lax.fori_loop(first, last, body, 0)

    def cross_attend_back(first, last):
        def body(u, carry):
            attend_back(u, cross_q, 0, cross_k, 0, cross_v, 0, mem_len, r["mem_lengths"], False,
                        r["cross_lse"], CROSS_V)
            return carry

        return lambda: lax.fori_loop(first, last, body, 0)

    ROW_TILE = 64

    def over_rows(body):
        def step(i, carry):
            body(pl.ds(pl.multiple_of(i * ROW_TILE, ROW_TILE), ROW_TILE))
            return carry

        lax.fori_loop(0, tokens // ROW_TILE, step, 0)

    def normalise(summed):
        average = jnp.mean(summed, axis=-1, keepdims=True)
        centred = summed - average
        inverse = lax.rsqrt(jnp.mean(centred * centred, axis=-1, keepdims=True) + NORM_EPSILON)
        return centred * inverse, inverse

    def normalise_back(at, incoming, normed, inverse, gain):
        gvecs[pl.ds(at, 1), :] += jnp.sum(incoming * normed, axis=0, keepdims=True)
        gvecs[pl.ds(at + 1, 1), :] += jnp.sum(incoming, axis=0, keepdims=True)
        scaled = incoming * gain
        centred = (
            scaled
            - jnp.mean(scaled, axis=-1, keepdims=True)
            - normed * jnp.mean(scaled * normed, axis=-1, keepdims=True)
        )
        return centred * inverse

    def branch(attn, at, j):
        def run(w):
            cols = pl.ds(j * COLS, COLS)
            acc[:, cols] = dot(attn[...], matrix(w[...])) + vec(at, j * COLS, COLS)

        return run

    def norm_one():
        def body(at):
            normed, inverse = normalise(x_in[at, :].astype(F32) + acc[at, :])
            hidden_one = normed * vec(GAIN1) + vec(SHIFT1)
            n1[at, :] = normed
            r1[at, :] = inverse
            h1[at, :] = hidden_one
            h1_low[at, :] = hidden_one.astype(BF16)

        over_rows(body)

    def cross_query(j):
        def run(w):
            cols = pl.ds(j * COLS, COLS)
            value = (dot(h1_low[...], matrix(w[...])) + vec(CROSS_Q, j * COLS, COLS)) * scale
            cross_q[:, cols] = value.astype(BF16)

        return run

    def cross_project(target, at, j, first):
        def run(w):
            weight = matrix(w[...])

            def body(i, carry):
                at_rows = pl.ds(pl.multiple_of(i * 256, 256), 256)
                value = dot(mem[at_rows, :], weight)
                if at is not None:
                    value = value + vec(at, j * COLS, COLS)
                target[at_rows, pl.ds(j * COLS, COLS)] = value.astype(BF16)
                return carry

            lax.fori_loop(first, first + samples * mem_len // 512, body, 0)

        return run

    def norm_two():
        def body(at):
            normed, inverse = normalise(h1[at, :] + acc[at, :])
            hidden_two = normed * vec(GAIN2) + vec(SHIFT2)
            n2[at, :] = normed
            r2[at, :] = inverse
            flow[at, :] = hidden_two
            h2_low[at, :] = hidden_two.astype(BF16)

        over_rows(body)

    def feed_up(j):
        def run(w):
            row, first = UP + j * COLS // width, j * COLS % width
            cols = pl.ds(j * COLS, COLS)
            pre = dot(h2_low[...], matrix(w[...])) + vec(row, first, COLS)
            normal_cdf = 0.5 * (1.0 + lax.erf(pre * (1.0 / math.sqrt(2.0))))
            density = jnp.exp(-0.5 * pre * pre) * (1.0 / math.sqrt(2.0 * math.pi))
            low = (pre * normal_cdf).astype(BF16)
            act[:, cols] = low
            act_t[pl.ds(j * COLS, COLS), :] = low.T
            slope[:, cols] = (normal_cdf + pre * density).astype(BF16)

        return run

    def feed_down(j):
        def run(w):
            acc[:, pl.ds(j * 256, 256)] = dot(act[...], matrix(w[...])) + vec(DOWN, j * 256, 256)

        return run

    def norm_three():
        gvecs[...] = jnp.zeros_like(gvecs)

        def body(at):
            normed, inverse = normalise(flow[at, :] + acc[at, :])
            d_attn[at, :] = (normed * vec(GAIN3) + vec(SHIFT3)).astype(BF16)
            grad = normalise_back(GAIN3, cot[at, :].astype(F32), normed, inverse, vec(GAIN3))
            low = grad.astype(BF16)
            flow[at, :] = grad
            d_ffn[at, :] = low
            gvecs[pl.ds(DOWN, 1), :] += jnp.sum(low.astype(F32), axis=0, keepdims=True)

        over_rows(body)
        hand_out(d_attn, r["block_out"], 7)

    def pre_back(i):
        def run(w):
            cols = pl.ds(i * width, width)
            value = None
            for q in range(4):
                part = dot_nt(d_ffn[:, pl.ds(q * 256, 256)], matrix(w[q * zs : (q + 1) * zs]))
                value = part if value is None else value + part
            low = (value * slope[:, cols].astype(F32)).astype(BF16)
            slope[:, cols] = low
            gvecs[pl.ds(UP + i, 1), :] = jnp.sum(low.astype(F32), axis=0, keepdims=True)

        return run

    def flow_back(grads, first, j):
        def run(w):
            flow[...] += dot_nt(grads[:, pl.ds(first + j * COLS, COLS)], matrix(w[...]))

        return run

    def norm_two_back():
        def body(at):
            grad = normalise_back(GAIN2, flow[at, :], n2[at, :], r2[at, :], vec(GAIN2))
            low = grad.astype(BF16)
            flow[at, :] = grad
            d_cross[at, :] = low
            gvecs[pl.ds(CROSS_O, 1), :] += jnp.sum(low.astype(F32), axis=0, keepdims=True)

        over_rows(body)

    def norm_one_back():
        gvecs[pl.ds(CROSS_Q, 1), :] = jnp.sum(cross_q[...].astype(F32), axis=0, keepdims=True)

        def body(at):
            grad = normalise_back(GAIN1, flow[at, :], n1[at, :], r1[at, :], vec(GAIN1))
            low = grad.astype(BF16)
            flow[at, :] = grad
            d_self[at, :] = low
            gvecs[pl.ds(SELF_O, 1), :] += jnp.sum(low.astype(F32), axis=0, keepdims=True)

        over_rows(body)

    def attn_back(grads, j):
        def run(w):
            value = dot_nt(grads[:, pl.ds(j * COLS, COLS)], matrix(w[...]))
            if j == 0:
                acc[...] = value
                if grads is d_cross:
                    out_copies.pop(0).wait()
            else:
                d_attn[...] = (acc[...] + value).astype(BF16)

        return run

    def vector_sums():
        gvecs[pl.ds(SELF_Q, 1), :] = jnp.sum(qkv[:, pl.ds(0, width)].astype(F32), axis=0, keepdims=True)
        pack_vectors()

    def target_done():
        d_ffn[...] = flow[...].astype(BF16)
        hand_out(d_ffn, r["target_grad"], 8)

    out_copies = []

    def hand_out(value, target, i):
        copy = pltpu.make_async_copy(value, target, r["out_sem"].at[i])
        copy.start()
        out_copies.append(copy)

    staged, stage_sem = r["staged"], r["stage_sem"]
    stage_copies = []

    def memory_back(half, tiles):
        half_cols = width // 2

        def run(w):
            weights = [matrix(w[c // 2, c % 2 * zh : (c % 2 + 1) * zh]) for c in range(4)]
            for tile in tiles:
                slot = len(stage_copies) % 2
                if len(stage_copies) >= 2:
                    stage_copies[-2].wait()
                at_rows = pl.ds(tile * 512, 512)
                value = dot_nt(cross_k[at_rows, :half_cols], weights[0])
                value += dot_nt(cross_k[at_rows, half_cols:], weights[1])
                value += dot_nt(cross_v[at_rows, :half_cols], weights[2])
                value += dot_nt(cross_v[at_rows, half_cols:], weights[3])
                staged[slot] = value.astype(BF16)
                copy = pltpu.make_async_copy(
                    staged.at[slot],
                    r["memory_grad"].at[at_rows, pl.ds(half * half_cols, half_cols)],
                    stage_sem.at[slot],
                )
                copy.start()
                stage_copies.append(copy)

        return run


    every = (far_all, pl.ds(0, 2), pl.ds(0, 2), pl.ds(0, 2))
    wbuf, wquarter = r["wbuf"], r["wquarter"]
    wslots = wbuf.shape[0]
    uses = {"column": 0, "quarter": 0}

    def next_slot(kind, slots):
        uses[kind] += 1
        return (uses[kind] - 1) % slots

    def column_load(a, col):
        slot = next_slot("column", wslots)
        src = whole[a].at[(*every, pl.ds(0, rows), pl.ds(col, COLS))]
        return dict(buffer=wbuf.at[slot], takes=[slot], copies=[(src, wbuf.at[slot])])

    def quarter_load(j):
        slot = next_slot("quarter", 2)
        copies = [
            (
                whole[FDOWN].at[(*every, pl.ds(row, rows), pl.ds(j * 256, 256))],
                wquarter.at[(slot, *every, pl.ds(row, rows))],
                index[(FDOWN, row, j * 256 // COLS * COLS)],
            )
            for row in range(0, down_rows, rows)
        ]
        return dict(buffer=wquarter.at[slot], takes=[wslots + slot], copies=copies)

    def group_load(i):
        slot = next_slot("quarter", 2)
        copies = [
            (
                whole[FDOWN].at[(pl.ds(i * zs, zs), *every[1:], pl.ds(0, down_rows), pl.ds(q * 256, 256))],
                wquarter.at[slot, pl.ds(q * zs, zs)],
            )
            for q in range(4)
        ]
        return dict(buffer=wquarter.at[slot], takes=[wslots + slot], copies=copies)

    def half_load(i):
        copies = [
            (
                whole[CQKV].at[
                    (pl.ds(i * zh, zh), *every[1:], pl.ds(0, rows), pl.ds(width + c * COLS, COLS))
                ],
                wbuf.at[2 * i + c // 2, pl.ds(c % 2 * zh, zh)],
            )
            for c in range(4)
        ]
        return dict(buffer=wbuf.at[pl.ds(2 * i, 2)], takes=[2 * i, 2 * i + 1], copies=copies)

    chunks, index = gather_chunks([s.shape for s in shards])
    count = len(chunks)
    per_half = width // COLS
    forward = []
    backward = []

    def piece(pieces, cost, run, load=None, dep=0, name=None):
        pieces.append(dict(cost=cost, run=run, load=load, dep=dep, name=name))

    def down_dep(j):
        return index[(FDOWN, down_rows - rows, j * 256 // COLS * COLS)]

    piece(forward, 4.0, take_vectors, None, 0)
    for j in range(3 * width // COLS):
        piece(forward, 0.5, self_project(j), column_load(SQKV, j * COLS), index[(SQKV, 0, j * COLS)])
    for first in range(0, samples * pairs, 4):
        piece(forward, 1.2, self_attend(first, first + 4), None, 0)
    for j in range(per_half):
        piece(forward, 0.5, branch(self_attn, SELF_O, j), column_load(SOUT, j * COLS), index[(SOUT, 0, j * COLS)])
    piece(forward, 0.9, norm_one)
    piece(forward, 0.5, turn(x_in))
    piece(forward, 0.5, turn(self_attn))
    for target, at, first in ((cross_k, None, width), (cross_v, CROSS_V, 2 * width)):
        for j in range(per_half):
            col = first + j * COLS
            dep = index[(CQKV, 0, col)]
            piece(forward, 1.2, cross_project(target, at, j, 0), column_load(CQKV, col), dep)
            piece(forward, 1.2, cross_project(target, at, j, samples * mem_len // 512), "keep", dep)
    for j in range(per_half):
        piece(forward, 0.5, cross_query(j), column_load(CQKV, j * COLS), index[(CQKV, 0, j * COLS)])
    piece(forward, 0.5, turn(h1_low))
    for s in range(samples):
        for i in range(width // 256):
            piece(forward, 0.3 * (2 * (width // 256 - i) - 1) / 2, turn_memory(s, i))
    for first in range(0, samples * pairs, 2):
        piece(forward, 1.6, cross_attend(first, first + 2))
    for j in range(per_half):
        piece(forward, 0.5, branch(cross_attn, CROSS_O, j), column_load(COUT, j * COLS), index[(COUT, 0, j * COLS)])
    piece(forward, 0.9, norm_two)
    piece(forward, 0.5, turn(cross_attn))
    for j in range(hidden // COLS):
        piece(forward, 1.2, feed_up(j), column_load(FUP, j * COLS), index[(FUP, 0, j * COLS)])
    piece(forward, 0.5, turn(h2_low))
    for j in range(width // 256):
        piece(forward, 0.8, feed_down(j), quarter_load(j), down_dep(j))
    piece(forward, 2.0, norm_three)

    for i in range(4):
        piece(backward, 1.0, pre_back(i), group_load(i), name="pre%d" % i)
    for j in range(hidden // COLS):
        piece(backward, 0.5, flow_back(slope, 0, j), column_load(FUP, j * COLS))
    piece(backward, 0.9, norm_two_back, name="norm2")
    for j in range(per_half):
        piece(backward, 0.5, attn_back(d_cross, j), column_load(COUT, j * COLS))
    for first in range(0, samples * pairs):
        piece(backward, 1.2, cross_attend_back(first, first + 1), name="cross")
    for j in range(per_half):
        piece(backward, 0.5, flow_back(cross_q, 0, j), column_load(CQKV, j * COLS))
    piece(backward, 0.9, norm_one_back, name="norm1")
    for j in range(per_half):
        piece(backward, 0.5, attn_back(d_self, j), column_load(SOUT, j * COLS))
    for first in range(0, samples * pairs, 2):
        piece(backward, 1.0, self_attend_back(first, first + 2), name="self")
    piece(backward, 1.0, vector_sums, name="vectors")
    for j in range(3 * width // COLS):
        piece(backward, 0.5, flow_back(qkv, 0, j), column_load(SQKV, j * COLS))
    piece(backward, 0.5, target_done)
    tile_count = samples * mem_len // 512
    for half in range(2):
        for first in range(tile_count):
            piece(backward, 1.6, memory_back(half, range(first, first + 1)), half_load(half) if first == 0 else "keep")

    def prepare(pieces, holders):
        last = None
        for p in pieces:
            p["done"], p["started"] = False, 0
            p["copies"], p["deps"], p["after"], p["buffer"] = [], [], [], None
            if p["load"] == "keep":
                p["buffer"] = last["buffer"]
                for slot in last["load"]["takes"]:
                    holders[slot] = p
            elif p["load"] is not None:
                p["buffer"] = p["load"]["buffer"]
                for slot in p["load"]["takes"]:
                    if slot in holders:
                        p["after"].append(holders[slot])
                    holders[slot] = p
                for n, (src, dst, *dep) in enumerate(p["load"]["copies"]):
                    sem = r["load_sem"].at[p["load"]["takes"][0], n]
                    p["copies"].append(pltpu.make_async_copy(src, dst, sem))
                    p["deps"].append(dep[0] if dep else p["dep"])
                last = p

    def start(p, ready):
        while p["started"] < len(p["copies"]) and p["deps"][p["started"]] <= ready:
            p["copies"][p["started"]].start()
            p["started"] += 1

    def look_ahead(pieces, ready):
        for later in pieces[:AHEAD]:
            if all(p["done"] for p in later["after"]):
                start(later, ready)
            if later["dep"] > ready:
                break

    def run_piece(pieces, ready):
        p = pieces.pop(0)
        start(p, ready)
        look_ahead(pieces, ready)
        for copy in p["copies"]:
            copy.wait()
        if p["buffer"] is not None:
            p["run"](p["buffer"])
        else:
            p["run"]()
        p["done"] = True
        return p

    def work(pieces, ready, limit):
        spent = 0.0
        look_ahead(pieces, ready)
        while pieces and pieces[0]["dep"] <= ready and spent < limit:
            spent += run_piece(pieces, ready)["cost"]

    holders = {}
    prepare(forward, holders)
    prepare(backward, holders)


    in_copies = [
        pltpu.make_async_copy(r["mem_hbm"], mem, r["in_sem"].at[0]),
        pltpu.make_async_copy(r["cot_hbm"], cot, r["in_sem"].at[1]),
        pltpu.make_async_copy(r["x_hbm"], x_in, r["in_sem"].at[2]),
    ]

    def block(ref, k, *lead):
        _, row, row_count, col, cols = chunks[k]
        return ref.at[(*lead, pl.ds(row, row_count), pl.ds(col, cols))]

    def gathered(k, *lead):
        return block(whole[chunks[k][0]], k, *lead)

    local = []
    for a in range(7):
        copy = pltpu.make_async_copy(shards[a], whole[a].at[far, y, core, x], r["local_sem"].at[a])
        copy.start()
        local.append(copy)
    greet(me)
    for copy in in_copies:
        copy.start()

    sent, late_sends, near_fars_in = {}, {}, {}
    relayed = far_count == 4
    to_next, to_previous = me["far_devices"][0][1], me["far_devices"][-1][1]

    def go(k, copy):
        copy.start()
        sent.setdefault(k, []).append(copy)
        return copy

    far_copies, near_copies, other_copies, pass_copies, twin_copies = {}, {}, {}, {}, {}
    last_lane = far_count - 1
    gsend, grecv = r["gsend"], r["grecv"]

    def send(k, lane, ref, device):
        return go(k, remote(ref, ref, gsend.at[k, lane], grecv.at[k, lane], device))

    def far_group(k, source, place, lane):
        target = gathered(k, far, place[0], core, place[1])
        copies = []
        for d, (_, device) in enumerate(me["far_devices"]):
            copy = remote(source, target, gsend.at[k, lane + d], grecv.at[k, lane + d], device)
            copies.append(copy)
            if relayed and d != 1:
                away = far != (3 if d == 0 else 0)
                pl.when(away)(copy.start)
                late_sends.setdefault(k, []).append((away, copy))
            else:
                go(k, copy)
        return copies

    def pass_on(k, copies, place, lane, send_lane):
        copies[1].wait_recv()
        for at, origin, d, device in ((1, 3, 0, to_previous), (2, 0, 2, to_next)):
            landed = gathered(k, origin, place[0], core, place[1])
            copy = remote(landed, landed, gsend.at[k, send_lane], grecv.at[k, lane + d], device)
            pl.when(far == at)(copy.start)
            late_sends.setdefault(k, []).append((far == at, copy))

    def far_landed(copies):
        for d, copy in enumerate(copies):
            if not (relayed and d == 1):
                copy.wait_recv()

    def start_far(k):
        own_block = block(shards[chunks[k][0]], k)
        far_copies[k] = far_group(k, own_block, (y, x), 0)
        if cross_way[k]:
            near_copies[k] = go(
                k,
                remote(
                    own_block,
                    gathered(k, far, y, core, x),
                    gsend.at[k, last_lane],
                    grecv.at[k, last_lane],
                    me["near_device"],
                ),
            )

    def start_near(k):
        column = gathered(k, far_all, y, core, x)
        other_copies[k] = send(k, last_lane + 1, column, me["other_device"])
        if cross_way[k]:
            near_copies[k].wait_recv()
            landed = gathered(k, far, near[0], core, near[1])
            near_fars_in[k] = far_group(k, landed, near, last_lane + 4)
        else:
            near_copies[k] = send(k, last_lane, column, me["near_device"])

    def start_pass(k):
        pass_copies[k] = send(k, last_lane + 2, gathered(k, far_all, near[0], core, near[1]), me["other_device"])

    def start_twin(k):
        half = gathered(k, far_all, pl.ds(0, 2), core, pl.ds(0, 2))
        twin_copies[k] = send(k, last_lane + 3, half, me["twin_device"])

    cross_way = [crossed(far_count, GATHER_CROSSED, chunk[0], k) for k, chunk in enumerate(chunks)]
    skew = GATHER_SKEW
    for t in range(count + 3 * skew + 1):
        k = t - 3 * skew
        if 0 <= k < count:
            other_copies[k].wait_recv()
            pass_copies[k].wait_recv()
            start_twin(k)
        k = t - 2 * skew
        if 0 <= k < count:
            if cross_way[k]:
                far_landed(near_fars_in[k])
            else:
                near_copies[k].wait_recv()
            start_pass(k)
        k = t - skew - skew // 2
        if 0 <= k < count and cross_way[k] and relayed:
            pass_on(k, near_fars_in[k], near, last_lane + 4, 2 * last_lane + 5)
        k = t - skew
        if 0 <= k < count:
            if k == 0:
                for copy in local:
                    copy.wait()
            far_landed(far_copies[k])
            start_near(k)
        k = t - skew // 2
        if 0 <= k < count and relayed:
            pass_on(k, far_copies[k], (y, x), 0, 2 * last_lane + 4)
        if t < count:
            start_far(t)
        k = t - 3 * skew - 1
        if k >= 0:
            if k == 0:
                for copy in in_copies:
                    copy.wait()
            twin_copies[k].wait_recv()
            if k >= 2:
                for copy in sent.pop(k - 2):
                    copy.wait_send()
                for here, copy in late_sends.pop(k - 2, ()):
                    pl.when(here)(copy.wait_send)
            work(forward, k, FORWARD_WORK)
    work(forward, count, 1e9)


    own, total, from_other, from_near, from_far = (
        r[n] for n in ("own", "total", "from_other", "from_near", "from_far")
    )
    small_buffers = (r["small_pack"], r["total_s"], r["from_other_s"], r["from_near_s"], r["from_far_s"])
    out_chunks = scatter_chunks(width)
    out_count = len(out_chunks)
    last_chunk = {chunk[0]: k for k, chunk in enumerate(out_chunks)}
    skew = SCATTER_SKEW
    own_slots, total_slots = own.shape[0], total.shape[0]
    other_slots, land_slots = from_other.shape[0], from_near.shape[0]
    from_near_far = r["from_near_far"]
    ssend, srecv = r["ssend"], r["srecv"]

    def buffers(k):
        if out_chunks[k][0] == SMALL:
            return small_buffers
        return (
            own.at[k % own_slots],
            total.at[k % total_slots],
            from_other.at[k % other_slots],
            from_near.at[k % land_slots],
            from_far.at[k % land_slots],
        )

    def compute(k):
        a, col = out_chunks[k]
        if a == SMALL:
            return
        target = buffers(k)[0]
        if a == FDOWN:
            right = d_ffn[:, pl.ds(col, 128)]
            for i in range(hidden // width):
                value = dot(act_t[i * width : (i + 1) * width], right).astype(BF16)
                for piece_at in range(0, width, rows):
                    b = (i * width + piece_at) // down_rows
                    q = piece_at % down_rows // rows
                    target[b // 8, (b // 4) % 2, (b // 2) % 2, b % 2, :, q * 128 : (q + 1) * 128] = value[
                        piece_at : piece_at + rows
                    ]
            return
        left, right = {
            FUP: (h2_low, slope),
            COUT: (cross_attn, d_cross),
            SOUT: (self_attn, d_self),
            SQKV: (x_in, qkv),
            CQKV: (
                (h1_low, cross_q),
                (mem, cross_k),
                (mem, cross_v),
            )[col // width if a == CQKV else 0],
        }[a]
        first = col % width if a == CQKV else col
        cols_at = pl.ds(first, COLS)
        if left is mem:
            part_rows = 512
            for i in range(0, width, part_rows):
                value = None
                for s in range(samples):
                    part = dot(
                        mem[s * mem_len + i : s * mem_len + i + part_rows],
                        right[pl.ds(s * mem_len, mem_len), cols_at],
                    )
                    value = part if value is None else value + part
                store_blocks(target, i, value.astype(BF16))
        else:
            turned = [left[:, i : i + 256] for i in range(0, width, 256)]
            value = dot(jnp.concatenate(turned, axis=0), right[:, cols_at])
            store_blocks(target, 0, value.astype(BF16))

    def store_blocks(target, first, value):
        for at in range(0, value.shape[0], rows):
            b = (first + at) // rows
            target[b // 8, (b // 4) % 2, (b // 2) % 2, b % 2] = value[at : at + rows]

    twins, others, nears, fars, near_fars = {}, {}, {}, {}, {}
    cross_out = [crossed(far_count, SCATTER_CROSSED, chunk[0], k) for k, chunk in enumerate(out_chunks)]

    def start_twin_sum(k):
        target, landing = buffers(k)[:2]
        twins[k] = remote(
            target.at[far_all, pl.ds(0, 2), 1 - core, pl.ds(0, 2)],
            landing,
            ssend.at[k, 0],
            srecv.at[k, 0],
            me["twin_device"],
        )
        twins[k].start()

    def add_own(k):
        mine, running = buffers(k)[:2]

        def body(i, carry):
            f, yy, xx = i // 4, (i // 2) % 2, i % 2
            running[f, yy, xx] = running[f, yy, xx] + mine[f, yy, core, xx]
            return carry

        lax.fori_loop(0, far_count * 4, body, 0)

    def start_others(k):
        running, landing = buffers(k)[1:3]
        others[k] = []
        for i, place in enumerate((diagonal, other)):
            copy = remote(
                running.at[far_all, place[0], place[1]],
                landing.at[i],
                ssend.at[k, 1 + i],
                srecv.at[k, 1 + i],
                me["other_device"],
            )
            copy.start()
            others[k].append(copy)

    def add_other(k, i):
        running, landing = buffers(k)[1:3]
        place = (near, (y, x))[i]

        def body(f, carry):
            running[f, place[0], place[1]] = running[f, place[0], place[1]] + landing[i, f]
            return carry

        lax.fori_loop(0, far_count, body, 0)

    def start_near_sum(k):
        _, running, _, landing, _ = buffers(k)
        source, target = running.at[far_all, near[0], near[1]], landing
        if cross_out[k]:
            source, target = running.at[far, near[0], near[1]], landing.at[0]
        nears[k] = remote(source, target, ssend.at[k, 3], srecv.at[k, 3], me["near_device"])
        nears[k].start()

    def start_near_fars(k):
        running, landing = buffers(k)[1], from_near_far.at[k % land_slots]
        near_fars[k] = []
        for d, (target, device) in enumerate(me["far_devices"]):
            lane = far_count + 3 + d
            copy = remote(
                running.at[target, near[0], near[1]], landing.at[d], ssend.at[k, lane], srecv.at[k, lane], device
            )
            copy.start()
            near_fars[k].append(copy)

    def add_near_fars(k):
        running, landing = buffers(k)[1], from_near_far.at[k % land_slots]
        result = running[far, near[0], near[1]].astype(F32)
        for d in range(far_count - 1):
            result += landing[d].astype(F32)
        running[far, near[0], near[1]] = result.astype(BF16)

    def add_near(k):
        _, running, _, landing, _ = buffers(k)

        def body(f, carry):
            running[f, y, x] = running[f, y, x] + landing[f]
            return carry

        lax.fori_loop(0, far_count, body, 0)

    def start_fars(k):
        _, running, _, _, landing = buffers(k)
        fars[k] = []
        for d, (target, device) in enumerate(me["far_devices"]):
            copy = remote(running.at[target, y, x], landing.at[d], ssend.at[k, 4 + d], srecv.at[k, 4 + d], device)
            copy.start()
            fars[k].append(copy)

    def finish(k):
        _, running, _, _, landing = buffers(k)
        a, col = out_chunks[k]
        result = running[far, y, x].astype(F32)
        for d in range(far_count - 1):
            result += landing[d].astype(F32)
        if cross_out[k]:
            result += buffers(k)[3][0].astype(F32)
        if a == SMALL:
            lane = (far * 8 + y * 4 + core * 2 + x) * rows % 128
            up_lane = (far * 8 + y * 4 + core * 2 + x) * down_rows % 128
            vectors = pltpu.roll(result, (128 - lane) % 128, 1)
            ups = pltpu.roll(result, (128 - up_lane) % 128, 1)
            row = lax.broadcasted_iota(jnp.int32, result.shape, 0)
            sums[a][...] = jnp.where(row == VECTORS, ups, vectors)
        elif a == FDOWN:
            for q in range(4):
                sums[a][q * rows : (q + 1) * rows, pl.ds(col, 128)] = result[:, q * 128 : (q + 1) * 128]
        else:
            sums[a][:, pl.ds(col, COLS)] = result
        if k == last_chunk[a]:
            hand_out(sums[a], r["o%d" % a], a)
        for copy in (*others[k], nears[k], *fars[k], *near_fars.get(k, ())):
            copy.wait_send()

    needs = {FUP: "pre3", COUT: "norm2", CQKV: "cross", SOUT: "norm1", SQKV: "self", SMALL: "vectors"}

    def make_chunk(k):
        need = needs.get(out_chunks[k][0])
        while any(p["name"] == need for p in backward if need):
            run_piece(backward, count)
        compute(k)

    make_chunk(0)
    for t in range(out_count + 4 * skew):
        k = t - 4 * skew
        if 0 <= k < out_count:
            for copy in fars[k]:
                copy.wait_recv()
            if cross_out[k]:
                nears[k].wait_recv()
            finish(k)
        k = t - 3 * skew
        if 0 <= k < out_count:
            if cross_out[k]:
                for copy in near_fars[k]:
                    copy.wait_recv()
                add_near_fars(k)
                start_near_sum(k)
            else:
                nears[k].wait_recv()
                add_near(k)
                start_fars(k)
        k = t - 2 * skew
        if 0 <= k < out_count:
            others[k][0].wait_recv()
            add_other(k, 0)
            if cross_out[k]:
                start_near_fars(k)
            else:
                start_near_sum(k)
            others[k][1].wait_recv()
            add_other(k, 1)
            if cross_out[k]:
                start_fars(k)
        k = t - skew
        if 0 <= k < out_count:
            twins[k].wait()
            add_own(k)
            start_others(k)
        if t < out_count:
            start_twin_sum(t)
        if t + 1 < out_count:
            make_chunk(t + 1)
        heavy = t + 1 < out_count and out_chunks[t + 1][0] == CQKV and out_chunks[t + 1][1] >= width
        work(backward, count, BACKWARD_WORK - (HEAVY_WORK if heavy else 0.0))
    work(backward, count, 1e9)
    for copy in (*stage_copies[-2:], *out_copies):
        copy.wait()
    for copies in sent.values():
        for copy in copies:
            copy.wait_send()
    for copies in late_sends.values():
        for here, copy in copies:
            pl.when(here)(copy.wait_send)


def hand_over_kernel(parts, n, *refs):
    ins, outs, buffers = refs[:n], refs[n : 2 * n], refs[2 * n : 3 * n]
    in_sem, out_sem = refs[3 * n :]

    def copies(ref_from, ref_to, sem):
        return [
            pltpu.make_async_copy(ref_from[a].at[pl.ds(row, count)], ref_to[a].at[pl.ds(row, count)], sem.at[i])
            for i, (a, row, count) in enumerate(parts)
        ]

    arriving, leaving = copies(ins, buffers, in_sem), copies(buffers, outs, out_sem)
    for copy in arriving:
        copy.start()
    for arrived, left in zip(arriving, leaving):
        arrived.wait()
        left.start()
    for copy in leaving:
        copy.wait()


def hand_over(arrays):
    n = len(arrays)
    parts = []
    for a, v in enumerate(arrays):
        count = 512 if v.shape[0] > 512 else v.shape[0]
        parts += [(a, row, count) for row in range(0, v.shape[0], count)]
    anywhere = pl.BlockSpec(memory_space=pl.ANY)
    return pl.pallas_call(
        functools.partial(hand_over_kernel, parts, n),
        out_shape=[jax.ShapeDtypeStruct(v.shape, v.dtype) for v in arrays],
        in_specs=[anywhere] * n,
        out_specs=[anywhere] * n,
        scratch_shapes=[pltpu.VMEM(v.shape, v.dtype) for v in arrays]
        + [pltpu.SemaphoreType.DMA((len(parts),))] * 2,
        compiler_params=pltpu.CompilerParams(vmem_limit_bytes=63 * 2**20),
        name="hand_over",
    )(*arrays)


def layer(mesh, target_input, memory, cotangent, mem_lengths, tgt_lengths, shards, small):
    samples, tgt_len, width = target_input.shape
    mem_len = memory.shape[1]
    far_count = mesh.shape["wide"] // 4
    rows = shards[SQKV].shape[0]
    tokens, keys, hidden = samples * tgt_len, samples * mem_len, 4 * width
    lanes = far_count + 3 + (5 if far_count == 4 else 0)
    count = len(gather_chunks([s.shape for s in shards])[0])
    out_count = len(scatter_chunks(width))
    lead = (far_count, 2, 2, 2)
    total_slots, own_slots = 5 * SCATTER_SKEW + 1, SCATTER_SKEW + 1
    other_slots, land_slots = 2 * SCATTER_SKEW + 1, (4 if far_count == 4 else 3) * SCATTER_SKEW

    def vmem(shape, dtype=BF16):
        return pltpu.VMEM(shape, dtype)

    small_sum = (SMALL_ROWS, 128)
    scratch = [vmem(v.shape, F32) for v in shards] + [
        vmem(small_sum, F32),
        vmem((tokens, width)),
        vmem((keys, width)),
        vmem((tokens, width)),
        vmem((tokens, 3 * width)),
        vmem((tokens, width)),
        vmem((tokens, width), F32),
        vmem((tokens, 1), F32),
        vmem((tokens, width), F32),
        vmem((tokens, width)),
        vmem((tokens, width)),
        vmem((keys, width)),
        vmem((keys, width)),
        vmem((tokens, width)),
        vmem((tokens, width), F32),
        vmem((tokens, 1), F32),
        vmem((tokens, width), F32),
        vmem((tokens, width)),
        vmem((tokens, hidden)),
        vmem((hidden, tokens)),
        vmem((tokens, hidden)),
        vmem((tokens, width), F32),
        vmem((tokens, width)),
        vmem((tokens, width)),
        vmem((tokens, width)),
        vmem((tokens, width)),
        vmem((samples * HEADS // 2, 2 * tgt_len), F32),
        vmem((samples * HEADS // 2, 2 * tgt_len), F32),
        vmem((24, width), F32),
        vmem((24, width), F32),
        vmem((2, 512, width // 2)),
        vmem((4,) + lead + (rows, COLS)),
        vmem((2,) + lead + (4 * rows, 256)),
        vmem(lead + (SMALL_ROWS, 128)),
        vmem((SMALL_ROWS, mesh.size, 128), F32),
        vmem(lead + small_sum, F32),
        vmem((own_slots,) + lead + (rows, COLS)),
        vmem((total_slots, far_count, 2, 2, rows, COLS)),
        vmem((other_slots, 2, far_count, rows, COLS)),
        vmem((land_slots, far_count, rows, COLS)),
        vmem((land_slots, far_count - 1, rows, COLS)),
        vmem((land_slots if far_count == 4 else 1, 3, rows, COLS)),
        vmem((far_count, 2, 2) + small_sum, F32),
        vmem((2, far_count) + small_sum, F32),
        vmem((far_count,) + small_sum, F32),
        vmem((far_count - 1,) + small_sum, F32),
        pltpu.SemaphoreType.DMA((6, 4)),
        pltpu.SemaphoreType.DMA((3,)),
        pltpu.SemaphoreType.DMA((7,)),
        pltpu.SemaphoreType.DMA((count, lanes)),
        pltpu.SemaphoreType.DMA((count, lanes)),
        pltpu.SemaphoreType.DMA((out_count, lanes)),
        pltpu.SemaphoreType.DMA((out_count, lanes)),
        pltpu.SemaphoreType.DMA((2,)),
        pltpu.SemaphoreType.DMA((9,)),
    ]
    in_vmem, anywhere = pl.BlockSpec(memory_space=pltpu.VMEM), pl.BlockSpec(memory_space=pl.ANY)
    in_smem = pl.BlockSpec(memory_space=pltpu.SMEM)
    out_shape = [
        jax.ShapeDtypeStruct((tokens, width), BF16),
        jax.ShapeDtypeStruct((tokens, width), BF16),
        jax.ShapeDtypeStruct((keys, width), BF16),
    ]
    out_shape += [jax.ShapeDtypeStruct(s.shape, F32) for s in shards]
    out_shape += [jax.ShapeDtypeStruct(small_sum, F32)]
    out_shape += [jax.ShapeDtypeStruct(lead + s.shape, BF16) for s in shards]
    outs = pl.pallas_call(
        functools.partial(layer_kernel, (far_count, rows, width, samples, tgt_len, mem_len)),
        out_shape=out_shape,
        in_specs=[anywhere, anywhere, anywhere, in_smem, in_smem] + [in_vmem] * 7,
        out_specs=[anywhere] * 16,
        scratch_shapes=scratch,
        compiler_params=pltpu.CompilerParams(
            collective_id=0, has_side_effects=True, vmem_limit_bytes=63 * 2**20
        ),
        cost_estimate=pl.CostEstimate(flops=52 * 10**9, bytes_accessed=10**8, transcendentals=10**7),
        name="decoder_layer",
    )(
        target_input.reshape(tokens, width),
        memory.reshape(keys, width),
        cotangent.reshape(tokens, width),
        mem_lengths,
        tgt_lengths,
        *shards,
        small,
    )
    return (*hand_over(outs[:9]), outs[9])


def step(
    mesh,
    target_input,
    memory,
    cotangent,
    mem_lengths,
    tgt_lengths,
    self_qkv,
    self_out,
    self_bias,
    norm1_gain,
    norm1_shift,
    cross_qkv,
    cross_out,
    cross_bias,
    norm2_gain,
    norm2_shift,
    ffn_up,
    up_bias,
    ffn_down,
    down_bias,
    norm3_gain,
    norm3_shift,
):
    per, up_per = norm1_gain.shape[0], up_bias.shape[0]
    small = jnp.zeros((SMALL_ROWS, 128), BF16)
    row = 0
    for v in (
        self_bias, norm1_gain, norm1_shift, cross_bias, norm2_gain, norm2_shift,
        down_bias, norm3_gain, norm3_shift, up_bias,
    ):
        v = v.reshape(-1, v.shape[-1])
        small += jnp.pad(v, ((row, SMALL_ROWS - row - v.shape[0]), (0, 128 - v.shape[1])))
        row += v.shape[0]
    block_out, target_grad, memory_grad, *grads, sums = layer(
        mesh, target_input, memory, cotangent, mem_lengths, tgt_lengths,
        [self_qkv, self_out, cross_qkv, cross_out, ffn_up, ffn_down], small,
    )
    return (
        block_out.reshape(target_input.shape),
        target_grad.reshape(target_input.shape),
        memory_grad.reshape(memory.shape),
        grads[SQKV],
        grads[SOUT],
        sums[SELF_Q : SELF_Q + 3, :per],
        sums[GAIN1, :per],
        sums[SHIFT1, :per],
        grads[CQKV],
        grads[COUT],
        sums[CROSS_Q : CROSS_Q + 3, :per],
        sums[GAIN2, :per],
        sums[SHIFT2, :per],
        grads[FUP],
        sums[VECTORS, :up_per],
        grads[FDOWN],
        sums[DOWN, :per],
        sums[GAIN3, :per],
        sums[SHIFT3, :per],
    )


def solution(mesh):
    both = ("wide", "narrow")
    stream, matrix_spec, vector_spec, bias_spec = P(both, None, None), P(both, None), P(both), P(None, both)
    weights = (
        matrix_spec, matrix_spec, bias_spec, vector_spec, vector_spec,
        matrix_spec, matrix_spec, bias_spec, vector_spec, vector_spec,
        matrix_spec, vector_spec, matrix_spec, vector_spec, vector_spec, vector_spec,
    )
    return jax.shard_map(
        functools.partial(step, mesh),
        mesh=mesh,
        in_specs=(stream, stream, stream, vector_spec, vector_spec) + weights,
        out_specs=(stream, stream, stream) + weights,
        check_vma=False,
    )
```

```python
import functools
import math

import jax
import jax.numpy as jnp
from jax import lax
from jax.experimental import pallas as pl
from jax.experimental.pallas import tpu as pltpu
from jax.sharding import PartitionSpec as P

MESH = pl.DeviceIdType.MESH
HEADS = 16
HEAD_DIM = 64
NORM_EPSILON = 1e-05
MASK_VALUE = -1e30
COLS = 512
GATHER_SKEW = 4
SCATTER_SKEW = 2
FORWARD_WORK = 1.5
BACKWARD_WORK = 1.4
HEAVY_WORK = 1.0
GATHER_CROSSED = (1, 0, 1, 0, 1)
SCATTER_CROSSED = (0, 1, 0)
AHEAD = 8
SMALL_ROWS = 16

F32 = jnp.float32
BF16 = jnp.bfloat16

SELF_Q, SELF_V, SELF_O, GAIN1, SHIFT1, CROSS_Q, CROSS_V, CROSS_O, GAIN2, SHIFT2, DOWN, GAIN3, SHIFT3, UP = range(14)
VECTORS = 13


def dot(a, b):
    return lax.dot_general(a, b, (((1,), (0,)), ((), ())), preferred_element_type=F32)


def dot_nt(a, b):
    return lax.dot_general(a, b, (((1,), (1,)), ((), ())), preferred_element_type=F32)


def dot_tn(a, b):
    return lax.dot_general(a, b, (((0,), (0,)), ((), ())), preferred_element_type=F32)


def places(far_count):
    wide = lax.axis_index("wide")
    x = lax.axis_index("narrow")
    far = wide // 4
    y = (wide // 2) % 2
    core = wide % 2
    near_y = y + core * (1 - 2 * y)
    near_x = x + (1 - core) * (1 - 2 * x)
    other_y = y + (1 - core) * (1 - 2 * y)
    other_x = x + core * (1 - 2 * x)

    def device(f, yy, cc, xx):
        return (f * 4 + yy * 2 + cc, xx)

    return dict(
        far=far,
        y=y,
        core=core,
        x=x,
        near=(near_y, near_x),
        other=(other_y, other_x),
        diagonal=(1 - y, 1 - x),
        near_device=device(far, near_y, core, near_x),
        other_device=device(far, other_y, core, other_x),
        twin_device=device(far, y, 1 - core, x),
        far_devices=[
            (lax.rem(far + d, far_count), device(lax.rem(far + d, far_count), y, core, x))
            for d in range(1, far_count)
        ],
    )


def greet(where):
    barrier = pltpu.get_barrier_semaphore()
    partners = [where["near_device"], where["other_device"], where["twin_device"]]
    partners += [device for _, device in where["far_devices"]]
    for device in partners:
        pl.semaphore_signal(barrier, inc=1, device_id=device, device_id_type=MESH)
    pl.semaphore_wait(barrier, len(partners))


def remote(src, dst, send_sem, recv_sem, device):
    return pltpu.make_async_remote_copy(
        src_ref=src,
        dst_ref=dst,
        send_sem=send_sem,
        recv_sem=recv_sem,
        device_id=device,
        device_id_type=MESH,
    )


def matrix(value):
    rows, cols = value.shape[-2:]
    if rows % 16:
        return value.astype(F32).reshape(-1, cols).astype(BF16)
    return value.reshape(-1, cols)


ARRAYS = ("self_qkv", "self_out", "cross_qkv", "cross_out", "ffn_up", "ffn_down")
SQKV, SOUT, CQKV, COUT, FUP, FDOWN, SMALL = range(7)


def crossed(far_count, pattern, array, k):
    return far_count == 4 and array != SMALL and pattern[k % len(pattern)] == 1


def gather_chunks(shapes):
    rows = shapes[SQKV][0]
    width = shapes[SOUT][1]
    chunks = [(SMALL, 0, SMALL_ROWS, 0, 128)]
    for a, first, last in (
        (SQKV, 0, 3 * width),
        (SOUT, 0, width),
        (CQKV, width, 3 * width),
        (CQKV, 0, width),
        (COUT, 0, width),
        (FUP, 0, 4 * width),
    ):
        chunks += [(a, 0, rows, col, COLS) for col in range(first, last, COLS)]
    for col in range(0, width, COLS):
        chunks += [(FDOWN, row, rows, col, COLS) for row in range(0, 4 * rows, rows)]
    index = {(a, row, col): k for k, (a, row, _, col, _) in enumerate(chunks)}
    return chunks, index


def scatter_chunks(width):
    chunks = [(FDOWN, 128 * j) for j in range(width // 128)]
    for a, first, last in (
        (FUP, 0, 4 * width),
        (COUT, 0, width),
        (CQKV, 0, 3 * width),
        (SOUT, 0, width),
    ):
        chunks += [(a, col) for col in range(first, last, COLS)]
    chunks += [(SMALL, 0)]
    chunks += [(SQKV, col) for col in range(0, 3 * width, COLS)]
    return chunks


def layer_kernel(cfg, *refs):
    far_count, rows, width, samples, tgt_len, mem_len = cfg
    devices = 8 * far_count
    hidden = 4 * width
    down_rows = 4 * rows
    tokens = samples * tgt_len
    pairs = HEADS // 2
    scale = 1.0 / math.sqrt(HEAD_DIM)
    zs = max(1, far_count // 4)
    zh = max(1, far_count // 2)

    names = (
        "x_hbm", "mem_hbm", "cot_hbm", "mem_lengths", "tgt_lengths", "i0", "i1", "i2", "i3", "i4", "i5", "i6",
        "block_out", "target_grad", "memory_grad", "o0", "o1", "o2", "o3", "o4", "o5", "o6", "w0", "w1", "w2", "w3",
        "w4", "w5", "g0", "g1", "g2", "g3", "g4", "g5", "small_out", "x", "mem", "cot", "qkv", "self_attn", "n1",
        "r1", "h1", "h1_low", "cross_q", "cross_k", "cross_v", "cross_attn", "n2", "r2", "flow", "h2_low", "act",
        "act_t", "slope", "acc", "d_ffn", "d_cross", "d_attn", "d_self", "self_lse", "cross_lse", "vecs", "gvecs",
        "staged", "wbuf", "wquarter", "small_in", "small_rows", "small_pack", "own", "total", "from_other",
        "from_near", "from_far", "from_near_far", "total_s", "from_other_s", "from_near_s", "from_far_s",
        "load_sem", "in_sem", "local_sem", "gsend", "grecv", "ssend", "srecv", "stage_sem", "out_sem",
    )
    r = dict(zip(names, refs, strict=True))
    x_in, mem, cot = r["x"], r["mem"], r["cot"]
    qkv, self_attn, n1, r1, h1, h1_low = (r[n] for n in ("qkv", "self_attn", "n1", "r1", "h1", "h1_low"))
    cross_q, cross_k, cross_v, cross_attn = (r[n] for n in ("cross_q", "cross_k", "cross_v", "cross_attn"))
    n2, r2, flow, h2_low = (r[n] for n in ("n2", "r2", "flow", "h2_low"))
    act, act_t, slope, acc = (r[n] for n in ("act", "act_t", "slope", "acc"))
    d_ffn, d_cross, d_attn, d_self = (r[n] for n in ("d_ffn", "d_cross", "d_attn", "d_self"))
    vecs, gvecs = r["vecs"], r["gvecs"]
    shards = [r["i%d" % i] for i in range(7)]
    whole = [r["w%d" % i] for i in range(6)] + [r["small_in"]]
    sums = [r["g%d" % i] for i in range(6)] + [r["small_out"]]

    me = places(far_count)
    far, y, core, x = me["far"], me["y"], me["core"], me["x"]
    far_all = pl.ds(0, far_count)
    near, other, diagonal = me["near"], me["other"], me["diagonal"]

    def vec(i, col=0, cols=width):
        return vecs[pl.ds(i, 1), pl.ds(col, cols)]


    def owner_of(per, first):
        device = lax.broadcasted_iota(jnp.int32, (devices, width), 0)
        column = lax.broadcasted_iota(jnp.int32, (devices, width), 1) + first
        return lax.shift_right_logical(column, per.bit_length() - 1) == device

    def spread_of(per):
        lane = lax.broadcasted_iota(jnp.int32, (128, width), 0)
        column = lax.broadcasted_iota(jnp.int32, (128, width), 1)
        return (lane == jnp.bitwise_and(column, per - 1)).astype(F32).astype(BF16)

    def take_vectors():
        small_in, table = r["small_in"], r["small_rows"]

        def body(b, carry):
            tile = small_in[b // 8, (b // 4) % 2, (b // 2) % 2, b % 2].astype(F32)
            for i in range(VECTORS + 1):
                table[i, pl.ds(b, 1), :] = tile[i : i + 1]
            return carry

        lax.fori_loop(0, devices, body, 0)
        spread, owner = spread_of(rows), owner_of(rows, 0)
        for i in range(VECTORS):
            values = dot(table[i].astype(BF16), spread)
            vecs[pl.ds(i, 1), :] = jnp.sum(jnp.where(owner, values, 0.0), axis=0, keepdims=True)
        values = dot(table[VECTORS].astype(BF16), spread_of(down_rows))
        for j in range(4):
            owner = owner_of(down_rows, j * width)
            vecs[pl.ds(UP + j, 1), :] = jnp.sum(jnp.where(owner, values, 0.0), axis=0, keepdims=True)

    def pack_vectors():
        pack = r["small_pack"]

        pack[...] = jnp.zeros_like(pack)
        for b in range(devices):
            lead = (b // 8, (b // 4) % 2, (b // 2) % 2, b % 2)
            lane, up_lane = b * rows // 128 * 128, b * down_rows % width // 128 * 128
            up_row = UP + b * down_rows // width
            pack[(*lead, slice(0, VECTORS))] = gvecs[0:VECTORS, lane : lane + 128]
            pack[(*lead, slice(VECTORS, VECTORS + 1))] = gvecs[up_row : up_row + 1, up_lane : up_lane + 128]

    def turn(ref, first=0, cols=width):
        def run():
            def body(i, carry):
                cols_at = pl.ds(pl.multiple_of(first + i * 256, 256), 256)
                ref[:, cols_at] = ref[:, cols_at].T
                return carry

            lax.fori_loop(0, cols // 256, body, 0)

        return run

    def turn_memory(s, i):
        def run():
            blocks = width // 256

            def at(i, j):
                return (
                    pl.ds(pl.multiple_of(s * mem_len + i * 256, 256), 256),
                    pl.ds(pl.multiple_of(j * 256, 256), 256),
                )

            mem[at(i, i)] = mem[at(i, i)].T
            for j in range(i + 1, blocks):
                upper, lower = mem[at(i, j)].T, mem[at(j, i)].T
                mem[at(i, j)] = lower
                mem[at(j, i)] = upper

        return run

    def self_project(j):
        def run(w):
            value = dot(x_in[...], matrix(w[...]))
            cols = pl.ds(j * COLS, COLS)
            part, first = j * COLS // width, j * COLS % width
            if part == 0:
                value = (value + vec(SELF_Q, first, COLS)) * scale
            if part == 2:
                value = value + vec(SELF_V, first, COLS)
            qkv[:, cols] = value.astype(BF16)

        return run

    def head_masks():
        lane = lax.broadcasted_iota(jnp.int32, (1, 128), 1)
        low = (lane < HEAD_DIM).astype(F32).astype(BF16)
        return low, (lane >= HEAD_DIM).astype(F32).astype(BF16)

    def both_heads(two):
        low, high = head_masks()
        return jnp.concatenate([two * low, two * high], axis=0)

    def one_row_each(stacked):
        lane = lax.broadcasted_iota(jnp.int32, (tgt_len, 128), 1)
        return jnp.where(lane < HEAD_DIM, stacked[:tgt_len], stacked[tgt_len:])

    def scores_of(keys, queries, length, causal):
        scores = dot_nt(keys, queries)
        key = lax.broadcasted_iota(jnp.int32, scores.shape, 0)
        usable = key < length
        if causal:
            query = jnp.bitwise_and(lax.broadcasted_iota(jnp.int32, scores.shape, 1), tgt_len - 1)
            usable = usable & (key <= query)
        return jnp.where(usable, scores, MASK_VALUE)

    def attend(u, queries, q_at, keys, k_at, values, v_at, key_count, lengths, causal, out, lse):
        s, pair = u // pairs, u % pairs
        lane = pair * 128
        q_rows = pl.ds(pl.multiple_of(s * tgt_len, tgt_len), tgt_len)
        k_rows = pl.ds(pl.multiple_of(s * key_count, key_count), key_count)

        def cols(first):
            return pl.ds(pl.multiple_of(first + lane, 128), 128)

        stacked = both_heads(queries[q_rows, cols(q_at)])
        scores = scores_of(keys[k_rows, cols(k_at)], stacked, lengths[s], causal)
        peak = jnp.max(scores, axis=0, keepdims=True)
        exponentials = jnp.exp(scores - peak)
        total = jnp.sum(exponentials, axis=0, keepdims=True)
        probs = (exponentials * (1.0 / total)).astype(BF16)
        mixed = dot_tn(values[k_rows, cols(v_at)], probs)
        out[q_rows, cols(0)] = one_row_each(mixed.T).astype(BF16)
        lse[pl.ds(u, 1), :] = peak + jnp.log(total)

    def attend_back(u, queries, q_at, keys, k_at, values, v_at, key_count, lengths, causal, lse, value_sum):
        s, pair = u // pairs, u % pairs
        lane = pair * 128
        q_rows = pl.ds(pl.multiple_of(s * tgt_len, tgt_len), tgt_len)
        k_rows = pl.ds(pl.multiple_of(s * key_count, key_count), key_count)

        def cols(first):
            return pl.ds(pl.multiple_of(first + lane, 128), 128)

        stacked = both_heads(queries[q_rows, cols(q_at)])
        upstream = both_heads(d_attn[q_rows, cols(0)])
        key_rows = keys[k_rows, cols(k_at)]
        scores = scores_of(key_rows, stacked, lengths[s], causal)
        probs = jnp.exp(scores - lse[pl.ds(u, 1), :])
        prob_grad = dot_nt(values[k_rows, cols(v_at)], upstream)
        delta = jnp.sum(probs * prob_grad, axis=0, keepdims=True)
        score_grad = (probs * (prob_grad - delta)).astype(BF16)
        query_grad = dot_tn(key_rows, score_grad)
        value_grad = dot(probs.astype(BF16), upstream).astype(BF16)
        values[k_rows, cols(v_at)] = value_grad
        keys[k_rows, cols(k_at)] = dot(score_grad, stacked).astype(BF16)
        queries[q_rows, cols(q_at)] = (one_row_each(query_grad.T) * scale).astype(BF16)
        gvecs[pl.ds(value_sum, 1), cols(0)] += jnp.sum(value_grad.astype(F32), axis=0, keepdims=True)

    def self_attend(first, last):
        def body(u, carry):
            attend(u, qkv, 0, qkv, width, qkv, 2 * width, tgt_len, r["tgt_lengths"], True,
                   self_attn, r["self_lse"])
            return carry

        return lambda: lax.fori_loop(first, last, body, 0)

    def cross_attend(first, last):
        def body(u, carry):
            attend(u, cross_q, 0, cross_k, 0, cross_v, 0, mem_len, r["mem_lengths"], False,
                   cross_attn, r["cross_lse"])
            return carry

        return lambda: lax.fori_loop(first, last, body, 0)

    def self_attend_back(first, last):
        def body(u, carry):
            attend_back(u, qkv, 0, qkv, width, qkv, 2 * width, tgt_len, r["tgt_lengths"], True,
                        r["self_lse"], SELF_V)
            return carry

        return lambda: lax.fori_loop(first, last, body, 0)

    def cross_attend_back(first, last):
        def body(u, carry):
            attend_back(u, cross_q, 0, cross_k, 0, cross_v, 0, mem_len, r["mem_lengths"], False,
                        r["cross_lse"], CROSS_V)
            return carry

        return lambda: lax.fori_loop(first, last, body, 0)

    ROW_TILE = 64

    def over_rows(body):
        def step(i, carry):
            body(pl.ds(pl.multiple_of(i * ROW_TILE, ROW_TILE), ROW_TILE))
            return carry

        lax.fori_loop(0, tokens // ROW_TILE, step, 0)

    def normalise(summed):
        average = jnp.mean(summed, axis=-1, keepdims=True)
        centred = summed - average
        inverse = lax.rsqrt(jnp.mean(centred * centred, axis=-1, keepdims=True) + NORM_EPSILON)
        return centred * inverse, inverse

    def normalise_back(at, incoming, normed, inverse, gain):
        gvecs[pl.ds(at, 1), :] += jnp.sum(incoming * normed, axis=0, keepdims=True)
        gvecs[pl.ds(at + 1, 1), :] += jnp.sum(incoming, axis=0, keepdims=True)
        scaled = incoming * gain
        centred = (
            scaled
            - jnp.mean(scaled, axis=-1, keepdims=True)
            - normed * jnp.mean(scaled * normed, axis=-1, keepdims=True)
        )
        return centred * inverse

    def branch(attn, at, j):
        def run(w):
            cols = pl.ds(j * COLS, COLS)
            acc[:, cols] = dot(attn[...], matrix(w[...])) + vec(at, j * COLS, COLS)

        return run

    def norm_one():
        def body(at):
            normed, inverse = normalise(x_in[at, :].astype(F32) + acc[at, :])
            hidden_one = normed * vec(GAIN1) + vec(SHIFT1)
            n1[at, :] = normed
            r1[at, :] = inverse
            h1[at, :] = hidden_one
            h1_low[at, :] = hidden_one.astype(BF16)

        over_rows(body)

    def cross_query(j):
        def run(w):
            cols = pl.ds(j * COLS, COLS)
            value = (dot(h1_low[...], matrix(w[...])) + vec(CROSS_Q, j * COLS, COLS)) * scale
            cross_q[:, cols] = value.astype(BF16)

        return run

    def cross_project(target, at, j, first):
        def run(w):
            weight = matrix(w[...])

            def body(i, carry):
                at_rows = pl.ds(pl.multiple_of(i * 256, 256), 256)
                value = dot(mem[at_rows, :], weight)
                if at is not None:
                    value = value + vec(at, j * COLS, COLS)
                target[at_rows, pl.ds(j * COLS, COLS)] = value.astype(BF16)
                return carry

            lax.fori_loop(first, first + samples * mem_len // 512, body, 0)

        return run

    def norm_two():
        def body(at):
            normed, inverse = normalise(h1[at, :] + acc[at, :])
            hidden_two = normed * vec(GAIN2) + vec(SHIFT2)
            n2[at, :] = normed
            r2[at, :] = inverse
            flow[at, :] = hidden_two
            h2_low[at, :] = hidden_two.astype(BF16)

        over_rows(body)

    def feed_up(j):
        def run(w):
            row, first = UP + j * COLS // width, j * COLS % width
            cols = pl.ds(j * COLS, COLS)
            pre = dot(h2_low[...], matrix(w[...])) + vec(row, first, COLS)
            normal_cdf = 0.5 * (1.0 + lax.erf(pre * (1.0 / math.sqrt(2.0))))
            density = jnp.exp(-0.5 * pre * pre) * (1.0 / math.sqrt(2.0 * math.pi))
            low = (pre * normal_cdf).astype(BF16)
            act[:, cols] = low
            act_t[pl.ds(j * COLS, COLS), :] = low.T
            slope[:, cols] = (normal_cdf + pre * density).astype(BF16)

        return run

    def feed_down(j):
        def run(w):
            acc[:, pl.ds(j * 256, 256)] = dot(act[...], matrix(w[...])) + vec(DOWN, j * 256, 256)

        return run

    def norm_three():
        gvecs[...] = jnp.zeros_like(gvecs)

        def body(at):
            normed, inverse = normalise(flow[at, :] + acc[at, :])
            d_attn[at, :] = (normed * vec(GAIN3) + vec(SHIFT3)).astype(BF16)
            grad = normalise_back(GAIN3, cot[at, :].astype(F32), normed, inverse, vec(GAIN3))
            low = grad.astype(BF16)
            flow[at, :] = grad
            d_ffn[at, :] = low
            gvecs[pl.ds(DOWN, 1), :] += jnp.sum(low.astype(F32), axis=0, keepdims=True)

        over_rows(body)
        hand_out(d_attn, r["block_out"], 7)

    def pre_back(i):
        def run(w):
            cols = pl.ds(i * width, width)
            value = None
            for q in range(4):
                part = dot_nt(d_ffn[:, pl.ds(q * 256, 256)], matrix(w[q * zs : (q + 1) * zs]))
                value = part if value is None else value + part
            low = (value * slope[:, cols].astype(F32)).astype(BF16)
            slope[:, cols] = low
            gvecs[pl.ds(UP + i, 1), :] = jnp.sum(low.astype(F32), axis=0, keepdims=True)

        return run

    def flow_back(grads, first, j):
        def run(w):
            flow[...] += dot_nt(grads[:, pl.ds(first + j * COLS, COLS)], matrix(w[...]))

        return run

    def norm_two_back():
        def body(at):
            grad = normalise_back(GAIN2, flow[at, :], n2[at, :], r2[at, :], vec(GAIN2))
            low = grad.astype(BF16)
            flow[at, :] = grad
            d_cross[at, :] = low
            gvecs[pl.ds(CROSS_O, 1), :] += jnp.sum(low.astype(F32), axis=0, keepdims=True)

        over_rows(body)

    def norm_one_back():
        gvecs[pl.ds(CROSS_Q, 1), :] = jnp.sum(cross_q[...].astype(F32), axis=0, keepdims=True)

        def body(at):
            grad = normalise_back(GAIN1, flow[at, :], n1[at, :], r1[at, :], vec(GAIN1))
            low = grad.astype(BF16)
            flow[at, :] = grad
            d_self[at, :] = low
            gvecs[pl.ds(SELF_O, 1), :] += jnp.sum(low.astype(F32), axis=0, keepdims=True)

        over_rows(body)

    def attn_back(grads, j):
        def run(w):
            value = dot_nt(grads[:, pl.ds(j * COLS, COLS)], matrix(w[...]))
            if j == 0:
                acc[...] = value
                if grads is d_cross:
                    out_copies.pop(0).wait()
            else:
                d_attn[...] = (acc[...] + value).astype(BF16)

        return run

    def vector_sums():
        gvecs[pl.ds(SELF_Q, 1), :] = jnp.sum(qkv[:, pl.ds(0, width)].astype(F32), axis=0, keepdims=True)
        pack_vectors()

    def target_done():
        d_ffn[...] = flow[...].astype(BF16)
        hand_out(d_ffn, r["target_grad"], 8)

    out_copies = []

    def hand_out(value, target, i):
        copy = pltpu.make_async_copy(value, target, r["out_sem"].at[i])
        copy.start()
        out_copies.append(copy)

    staged, stage_sem = r["staged"], r["stage_sem"]
    stage_copies = []

    def memory_back(half, tiles):
        half_cols = width // 2

        def run(w):
            weights = [matrix(w[c // 2, c % 2 * zh : (c % 2 + 1) * zh]) for c in range(4)]
            for tile in tiles:
                slot = len(stage_copies) % 2
                if len(stage_copies) >= 2:
                    stage_copies[-2].wait()
                at_rows = pl.ds(tile * 512, 512)
                value = dot_nt(cross_k[at_rows, :half_cols], weights[0])
                value += dot_nt(cross_k[at_rows, half_cols:], weights[1])
                value += dot_nt(cross_v[at_rows, :half_cols], weights[2])
                value += dot_nt(cross_v[at_rows, half_cols:], weights[3])
                staged[slot] = value.astype(BF16)
                copy = pltpu.make_async_copy(
                    staged.at[slot],
                    r["memory_grad"].at[at_rows, pl.ds(half * half_cols, half_cols)],
                    stage_sem.at[slot],
                )
                copy.start()
                stage_copies.append(copy)

        return run


    every = (far_all, pl.ds(0, 2), pl.ds(0, 2), pl.ds(0, 2))
    wbuf, wquarter = r["wbuf"], r["wquarter"]
    wslots = wbuf.shape[0]
    uses = {"column": 0, "quarter": 0}

    def next_slot(kind, slots):
        uses[kind] += 1
        return (uses[kind] - 1) % slots

    def column_load(a, col):
        slot = next_slot("column", wslots)
        src = whole[a].at[(*every, pl.ds(0, rows), pl.ds(col, COLS))]
        return dict(buffer=wbuf.at[slot], takes=[slot], copies=[(src, wbuf.at[slot])])

    def quarter_load(j):
        slot = next_slot("quarter", 2)
        copies = [
            (
                whole[FDOWN].at[(*every, pl.ds(row, rows), pl.ds(j * 256, 256))],
                wquarter.at[(slot, *every, pl.ds(row, rows))],
                index[(FDOWN, row, j * 256 // COLS * COLS)],
            )
            for row in range(0, down_rows, rows)
        ]
        return dict(buffer=wquarter.at[slot], takes=[wslots + slot], copies=copies)

    def group_load(i):
        slot = next_slot("quarter", 2)
        copies = [
            (
                whole[FDOWN].at[(pl.ds(i * zs, zs), *every[1:], pl.ds(0, down_rows), pl.ds(q * 256, 256))],
                wquarter.at[slot, pl.ds(q * zs, zs)],
            )
            for q in range(4)
        ]
        return dict(buffer=wquarter.at[slot], takes=[wslots + slot], copies=copies)

    def half_load(i):
        copies = [
            (
                whole[CQKV].at[
                    (pl.ds(i * zh, zh), *every[1:], pl.ds(0, rows), pl.ds(width + c * COLS, COLS))
                ],
                wbuf.at[2 * i + c // 2, pl.ds(c % 2 * zh, zh)],
            )
            for c in range(4)
        ]
        return dict(buffer=wbuf.at[pl.ds(2 * i, 2)], takes=[2 * i, 2 * i + 1], copies=copies)

    chunks, index = gather_chunks([s.shape for s in shards])
    count = len(chunks)
    per_half = width // COLS
    forward = []
    backward = []

    def piece(pieces, cost, run, load=None, dep=0, name=None):
        pieces.append(dict(cost=cost, run=run, load=load, dep=dep, name=name))

    def down_dep(j):
        return index[(FDOWN, down_rows - rows, j * 256 // COLS * COLS)]

    piece(forward, 4.0, take_vectors, None, 0)
    for j in range(3 * width // COLS):
        piece(forward, 0.5, self_project(j), column_load(SQKV, j * COLS), index[(SQKV, 0, j * COLS)])
    for first in range(0, samples * pairs, 4):
        piece(forward, 1.2, self_attend(first, first + 4), None, 0)
    for j in range(per_half):
        piece(forward, 0.5, branch(self_attn, SELF_O, j), column_load(SOUT, j * COLS), index[(SOUT, 0, j * COLS)])
    piece(forward, 0.9, norm_one)
    piece(forward, 0.5, turn(x_in))
    piece(forward, 0.5, turn(self_attn))
    for target, at, first in ((cross_k, None, width), (cross_v, CROSS_V, 2 * width)):
        for j in range(per_half):
            col = first + j * COLS
            dep = index[(CQKV, 0, col)]
            piece(forward, 1.2, cross_project(target, at, j, 0), column_load(CQKV, col), dep)
            piece(forward, 1.2, cross_project(target, at, j, samples * mem_len // 512), "keep", dep)
    for j in range(per_half):
        piece(forward, 0.5, cross_query(j), column_load(CQKV, j * COLS), index[(CQKV, 0, j * COLS)])
    piece(forward, 0.5, turn(h1_low))
    for s in range(samples):
        for i in range(width // 256):
            piece(forward, 0.3 * (2 * (width // 256 - i) - 1) / 2, turn_memory(s, i))
    for first in range(0, samples * pairs, 2):
        piece(forward, 1.6, cross_attend(first, first + 2))
    for j in range(per_half):
        piece(forward, 0.5, branch(cross_attn, CROSS_O, j), column_load(COUT, j * COLS), index[(COUT, 0, j * COLS)])
    piece(forward, 0.9, norm_two)
    piece(forward, 0.5, turn(cross_attn))
    for j in range(hidden // COLS):
        piece(forward, 1.2, feed_up(j), column_load(FUP, j * COLS), index[(FUP, 0, j * COLS)])
    piece(forward, 0.5, turn(h2_low))
    for j in range(width // 256):
        piece(forward, 0.8, feed_down(j), quarter_load(j), down_dep(j))
    piece(forward, 2.0, norm_three)

    for i in range(4):
        piece(backward, 1.0, pre_back(i), group_load(i), name="pre%d" % i)
    for j in range(hidden // COLS):
        piece(backward, 0.5, flow_back(slope, 0, j), column_load(FUP, j * COLS))
    piece(backward, 0.9, norm_two_back, name="norm2")
    for j in range(per_half):
        piece(backward, 0.5, attn_back(d_cross, j), column_load(COUT, j * COLS))
    for first in range(0, samples * pairs):
        piece(backward, 1.2, cross_attend_back(first, first + 1), name="cross")
    for j in range(per_half):
        piece(backward, 0.5, flow_back(cross_q, 0, j), column_load(CQKV, j * COLS))
    piece(backward, 0.9, norm_one_back, name="norm1")
    for j in range(per_half):
        piece(backward, 0.5, attn_back(d_self, j), column_load(SOUT, j * COLS))
    for first in range(0, samples * pairs, 2):
        piece(backward, 1.0, self_attend_back(first, first + 2), name="self")
    piece(backward, 1.0, vector_sums, name="vectors")
    for j in range(3 * width // COLS):
        piece(backward, 0.5, flow_back(qkv, 0, j), column_load(SQKV, j * COLS))
    piece(backward, 0.5, target_done)
    tile_count = samples * mem_len // 512
    for half in range(2):
        for first in range(tile_count):
            piece(backward, 1.6, memory_back(half, range(first, first + 1)), half_load(half) if first == 0 else "keep")

    def prepare(pieces, holders):
        last = None
        for p in pieces:
            p["done"], p["started"] = False, 0
            p["copies"], p["deps"], p["after"], p["buffer"] = [], [], [], None
            if p["load"] == "keep":
                p["buffer"] = last["buffer"]
                for slot in last["load"]["takes"]:
                    holders[slot] = p
            elif p["load"] is not None:
                p["buffer"] = p["load"]["buffer"]
                for slot in p["load"]["takes"]:
                    if slot in holders:
                        p["after"].append(holders[slot])
                    holders[slot] = p
                for n, (src, dst, *dep) in enumerate(p["load"]["copies"]):
                    sem = r["load_sem"].at[p["load"]["takes"][0], n]
                    p["copies"].append(pltpu.make_async_copy(src, dst, sem))
                    p["deps"].append(dep[0] if dep else p["dep"])
                last = p

    def start(p, ready):
        while p["started"] < len(p["copies"]) and p["deps"][p["started"]] <= ready:
            p["copies"][p["started"]].start()
            p["started"] += 1

    def look_ahead(pieces, ready):
        for later in pieces[:AHEAD]:
            if all(p["done"] for p in later["after"]):
                start(later, ready)
            if later["dep"] > ready:
                break

    def run_piece(pieces, ready):
        p = pieces.pop(0)
        start(p, ready)
        look_ahead(pieces, ready)
        for copy in p["copies"]:
            copy.wait()
        if p["buffer"] is not None:
            p["run"](p["buffer"])
        else:
            p["run"]()
        p["done"] = True
        return p

    def work(pieces, ready, limit):
        spent = 0.0
        look_ahead(pieces, ready)
        while pieces and pieces[0]["dep"] <= ready and spent < limit:
            spent += run_piece(pieces, ready)["cost"]

    holders = {}
    prepare(forward, holders)
    prepare(backward, holders)


    in_copies = [
        pltpu.make_async_copy(r["mem_hbm"], mem, r["in_sem"].at[0]),
        pltpu.make_async_copy(r["cot_hbm"], cot, r["in_sem"].at[1]),
        pltpu.make_async_copy(r["x_hbm"], x_in, r["in_sem"].at[2]),
    ]

    def block(ref, k, *lead):
        _, row, row_count, col, cols = chunks[k]
        return ref.at[(*lead, pl.ds(row, row_count), pl.ds(col, cols))]

    def gathered(k, *lead):
        return block(whole[chunks[k][0]], k, *lead)

    local = []
    for a in range(7):
        copy = pltpu.make_async_copy(shards[a], whole[a].at[far, y, core, x], r["local_sem"].at[a])
        copy.start()
        local.append(copy)
    greet(me)
    for copy in in_copies:
        copy.start()

    sent, late_sends, near_fars_in = {}, {}, {}
    relayed = far_count == 4
    to_next, to_previous = me["far_devices"][0][1], me["far_devices"][-1][1]

    def go(k, copy):
        copy.start()
        sent.setdefault(k, []).append(copy)
        return copy

    far_copies, near_copies, other_copies, pass_copies, twin_copies = {}, {}, {}, {}, {}
    last_lane = far_count - 1
    gsend, grecv = r["gsend"], r["grecv"]

    def send(k, lane, ref, device):
        return go(k, remote(ref, ref, gsend.at[k, lane], grecv.at[k, lane], device))

    def far_group(k, source, place, lane):
        target = gathered(k, far, place[0], core, place[1])
        copies = []
        for d, (_, device) in enumerate(me["far_devices"]):
            copy = remote(source, target, gsend.at[k, lane + d], grecv.at[k, lane + d], device)
            copies.append(copy)
            if relayed and d != 1:
                away = far != (3 if d == 0 else 0)
                pl.when(away)(copy.start)
                late_sends.setdefault(k, []).append((away, copy))
            else:
                go(k, copy)
        return copies

    def pass_on(k, copies, place, lane, send_lane):
        copies[1].wait_recv()
        for at, origin, d, device in ((1, 3, 0, to_previous), (2, 0, 2, to_next)):
            landed = gathered(k, origin, place[0], core, place[1])
            copy = remote(landed, landed, gsend.at[k, send_lane], grecv.at[k, lane + d], device)
            pl.when(far == at)(copy.start)
            late_sends.setdefault(k, []).append((far == at, copy))

    def far_landed(copies):
        for d, copy in enumerate(copies):
            if not (relayed and d == 1):
                copy.wait_recv()

    def start_far(k):
        own_block = block(shards[chunks[k][0]], k)
        far_copies[k] = far_group(k, own_block, (y, x), 0)
        if cross_way[k]:
            near_copies[k] = go(
                k,
                remote(
                    own_block,
                    gathered(k, far, y, core, x),
                    gsend.at[k, last_lane],
                    grecv.at[k, last_lane],
                    me["near_device"],
                ),
            )

    def start_near(k):
        column = gathered(k, far_all, y, core, x)
        other_copies[k] = send(k, last_lane + 1, column, me["other_device"])
        if cross_way[k]:
            near_copies[k].wait_recv()
            landed = gathered(k, far, near[0], core, near[1])
            near_fars_in[k] = far_group(k, landed, near, last_lane + 4)
        else:
            near_copies[k] = send(k, last_lane, column, me["near_device"])

    def start_pass(k):
        pass_copies[k] = send(k, last_lane + 2, gathered(k, far_all, near[0], core, near[1]), me["other_device"])

    def start_twin(k):
        half = gathered(k, far_all, pl.ds(0, 2), core, pl.ds(0, 2))
        twin_copies[k] = send(k, last_lane + 3, half, me["twin_device"])

    cross_way = [crossed(far_count, GATHER_CROSSED, chunk[0], k) for k, chunk in enumerate(chunks)]
    skew = GATHER_SKEW
    for t in range(count + 3 * skew + 1):
        k = t - 3 * skew
        if 0 <= k < count:
            other_copies[k].wait_recv()
            pass_copies[k].wait_recv()
            start_twin(k)
        k = t - 2 * skew
        if 0 <= k < count:
            if cross_way[k]:
                far_landed(near_fars_in[k])
            else:
                near_copies[k].wait_recv()
            start_pass(k)
        k = t - skew - skew // 2
        if 0 <= k < count and cross_way[k] and relayed:
            pass_on(k, near_fars_in[k], near, last_lane + 4, 2 * last_lane + 5)
        k = t - skew
        if 0 <= k < count:
            if k == 0:
                for copy in local:
                    copy.wait()
            far_landed(far_copies[k])
            start_near(k)
        k = t - skew // 2
        if 0 <= k < count and relayed:
            pass_on(k, far_copies[k], (y, x), 0, 2 * last_lane + 4)
        if t < count:
            start_far(t)
        k = t - 3 * skew - 1
        if k >= 0:
            if k == 0:
                for copy in in_copies:
                    copy.wait()
            twin_copies[k].wait_recv()
            if k >= 2:
                for copy in sent.pop(k - 2):
                    copy.wait_send()
                for here, copy in late_sends.pop(k - 2, ()):
                    pl.when(here)(copy.wait_send)
            work(forward, k, FORWARD_WORK)
    work(forward, count, 1e9)


    own, total, from_other, from_near, from_far = (
        r[n] for n in ("own", "total", "from_other", "from_near", "from_far")
    )
    small_buffers = (r["small_pack"], r["total_s"], r["from_other_s"], r["from_near_s"], r["from_far_s"])
    out_chunks = scatter_chunks(width)
    out_count = len(out_chunks)
    last_chunk = {chunk[0]: k for k, chunk in enumerate(out_chunks)}
    skew = SCATTER_SKEW
    own_slots, total_slots = own.shape[0], total.shape[0]
    other_slots, land_slots = from_other.shape[0], from_near.shape[0]
    from_near_far = r["from_near_far"]
    ssend, srecv = r["ssend"], r["srecv"]

    def buffers(k):
        if out_chunks[k][0] == SMALL:
            return small_buffers
        return (
            own.at[k % own_slots],
            total.at[k % total_slots],
            from_other.at[k % other_slots],
            from_near.at[k % land_slots],
            from_far.at[k % land_slots],
        )

    def compute(k):
        a, col = out_chunks[k]
        if a == SMALL:
            return
        target = buffers(k)[0]
        if a == FDOWN:
            right = d_ffn[:, pl.ds(col, 128)]
            for i in range(hidden // width):
                value = dot(act_t[i * width : (i + 1) * width], right).astype(BF16)
                for piece_at in range(0, width, rows):
                    b = (i * width + piece_at) // down_rows
                    q = piece_at % down_rows // rows
                    target[b // 8, (b // 4) % 2, (b // 2) % 2, b % 2, :, q * 128 : (q + 1) * 128] = value[
                        piece_at : piece_at + rows
                    ]
            return
        left, right = {
            FUP: (h2_low, slope),
            COUT: (cross_attn, d_cross),
            SOUT: (self_attn, d_self),
            SQKV: (x_in, qkv),
            CQKV: (
                (h1_low, cross_q),
                (mem, cross_k),
                (mem, cross_v),
            )[col // width if a == CQKV else 0],
        }[a]
        first = col % width if a == CQKV else col
        cols_at = pl.ds(first, COLS)
        if left is mem:
            part_rows = 512
            for i in range(0, width, part_rows):
                value = None
                for s in range(samples):
                    part = dot(
                        mem[s * mem_len + i : s * mem_len + i + part_rows],
                        right[pl.ds(s * mem_len, mem_len), cols_at],
                    )
                    value = part if value is None else value + part
                store_blocks(target, i, value.astype(BF16))
        else:
            turned = [left[:, i : i + 256] for i in range(0, width, 256)]
            value = dot(jnp.concatenate(turned, axis=0), right[:, cols_at])
            store_blocks(target, 0, value.astype(BF16))

    def store_blocks(target, first, value):
        for at in range(0, value.shape[0], rows):
            b = (first + at) // rows
            target[b // 8, (b // 4) % 2, (b // 2) % 2, b % 2] = value[at : at + rows]

    twins, others, nears, fars, near_fars = {}, {}, {}, {}, {}
    cross_out = [crossed(far_count, SCATTER_CROSSED, chunk[0], k) for k, chunk in enumerate(out_chunks)]

    def start_twin_sum(k):
        target, landing = buffers(k)[:2]
        twins[k] = remote(
            target.at[far_all, pl.ds(0, 2), 1 - core, pl.ds(0, 2)],
            landing,
            ssend.at[k, 0],
            srecv.at[k, 0],
            me["twin_device"],
        )
        twins[k].start()

    def add_own(k):
        mine, running = buffers(k)[:2]

        def body(i, carry):
            f, yy, xx = i // 4, (i // 2) % 2, i % 2
            running[f, yy, xx] = running[f, yy, xx] + mine[f, yy, core, xx]
            return carry

        lax.fori_loop(0, far_count * 4, body, 0)

    def start_others(k):
        running, landing = buffers(k)[1:3]
        others[k] = []
        for i, place in enumerate((diagonal, other)):
            copy = remote(
                running.at[far_all, place[0], place[1]],
                landing.at[i],
                ssend.at[k, 1 + i],
                srecv.at[k, 1 + i],
                me["other_device"],
            )
            copy.start()
            others[k].append(copy)

    def add_other(k, i):
        running, landing = buffers(k)[1:3]
        place = (near, (y, x))[i]

        def body(f, carry):
            running[f, place[0], place[1]] = running[f, place[0], place[1]] + landing[i, f]
            return carry

        lax.fori_loop(0, far_count, body, 0)

    def start_near_sum(k):
        _, running, _, landing, _ = buffers(k)
        source, target = running.at[far_all, near[0], near[1]], landing
        if cross_out[k]:
            source, target = running.at[far, near[0], near[1]], landing.at[0]
        nears[k] = remote(source, target, ssend.at[k, 3], srecv.at[k, 3], me["near_device"])
        nears[k].start()

    def start_near_fars(k):
        running, landing = buffers(k)[1], from_near_far.at[k % land_slots]
        near_fars[k] = []
        for d, (target, device) in enumerate(me["far_devices"]):
            lane = far_count + 3 + d
            copy = remote(
                running.at[target, near[0], near[1]], landing.at[d], ssend.at[k, lane], srecv.at[k, lane], device
            )
            copy.start()
            near_fars[k].append(copy)

    def add_near_fars(k):
        running, landing = buffers(k)[1], from_near_far.at[k % land_slots]
        result = running[far, near[0], near[1]].astype(F32)
        for d in range(far_count - 1):
            result += landing[d].astype(F32)
        running[far, near[0], near[1]] = result.astype(BF16)

    def add_near(k):
        _, running, _, landing, _ = buffers(k)

        def body(f, carry):
            running[f, y, x] = running[f, y, x] + landing[f]
            return carry

        lax.fori_loop(0, far_count, body, 0)

    def start_fars(k):
        _, running, _, _, landing = buffers(k)
        fars[k] = []
        for d, (target, device) in enumerate(me["far_devices"]):
            copy = remote(running.at[target, y, x], landing.at[d], ssend.at[k, 4 + d], srecv.at[k, 4 + d], device)
            copy.start()
            fars[k].append(copy)

    def finish(k):
        _, running, _, _, landing = buffers(k)
        a, col = out_chunks[k]
        result = running[far, y, x].astype(F32)
        for d in range(far_count - 1):
            result += landing[d].astype(F32)
        if cross_out[k]:
            result += buffers(k)[3][0].astype(F32)
        if a == SMALL:
            lane = (far * 8 + y * 4 + core * 2 + x) * rows % 128
            up_lane = (far * 8 + y * 4 + core * 2 + x) * down_rows % 128
            vectors = pltpu.roll(result, (128 - lane) % 128, 1)
            ups = pltpu.roll(result, (128 - up_lane) % 128, 1)
            row = lax.broadcasted_iota(jnp.int32, result.shape, 0)
            sums[a][...] = jnp.where(row == VECTORS, ups, vectors)
        elif a == FDOWN:
            for q in range(4):
                sums[a][q * rows : (q + 1) * rows, pl.ds(col, 128)] = result[:, q * 128 : (q + 1) * 128]
        else:
            sums[a][:, pl.ds(col, COLS)] = result
        if k == last_chunk[a]:
            hand_out(sums[a], r["o%d" % a], a)
        for copy in (*others[k], nears[k], *fars[k], *near_fars.get(k, ())):
            copy.wait_send()

    needs = {FUP: "pre3", COUT: "norm2", CQKV: "cross", SOUT: "norm1", SQKV: "self", SMALL: "vectors"}

    def make_chunk(k):
        need = needs.get(out_chunks[k][0])
        while any(p["name"] == need for p in backward if need):
            run_piece(backward, count)
        compute(k)

    make_chunk(0)
    for t in range(out_count + 4 * skew):
        k = t - 4 * skew
        if 0 <= k < out_count:
            for copy in fars[k]:
                copy.wait_recv()
            if cross_out[k]:
                nears[k].wait_recv()
            finish(k)
        k = t - 3 * skew
        if 0 <= k < out_count:
            if cross_out[k]:
                for copy in near_fars[k]:
                    copy.wait_recv()
                add_near_fars(k)
                start_near_sum(k)
            else:
                nears[k].wait_recv()
                add_near(k)
                start_fars(k)
        k = t - 2 * skew
        if 0 <= k < out_count:
            others[k][0].wait_recv()
            add_other(k, 0)
            if cross_out[k]:
                start_near_fars(k)
            else:
                start_near_sum(k)
            others[k][1].wait_recv()
            add_other(k, 1)
            if cross_out[k]:
                start_fars(k)
        k = t - skew
        if 0 <= k < out_count:
            twins[k].wait()
            add_own(k)
            start_others(k)
        if t < out_count:
            start_twin_sum(t)
        if t + 1 < out_count:
            make_chunk(t + 1)
        heavy = t + 1 < out_count and out_chunks[t + 1][0] == CQKV and out_chunks[t + 1][1] >= width
        work(backward, count, BACKWARD_WORK - (HEAVY_WORK if heavy else 0.0))
    work(backward, count, 1e9)
    for copy in (*stage_copies[-2:], *out_copies):
        copy.wait()
    for copies in sent.values():
        for copy in copies:
            copy.wait_send()
    for copies in late_sends.values():
        for here, copy in copies:
            pl.when(here)(copy.wait_send)


def hand_over_kernel(parts, n, *refs):
    ins, outs, buffers = refs[:n], refs[n : 2 * n], refs[2 * n : 3 * n]
    in_sem, out_sem = refs[3 * n :]

    def copies(ref_from, ref_to, sem):
        return [
            pltpu.make_async_copy(ref_from[a].at[pl.ds(row, count)], ref_to[a].at[pl.ds(row, count)], sem.at[i])
            for i, (a, row, count) in enumerate(parts)
        ]

    arriving, leaving = copies(ins, buffers, in_sem), copies(buffers, outs, out_sem)
    for copy in arriving:
        copy.start()
    for arrived, left in zip(arriving, leaving):
        arrived.wait()
        left.start()
    for copy in leaving:
        copy.wait()


def hand_over(arrays):
    n = len(arrays)
    parts = []
    for a, v in enumerate(arrays):
        count = 512 if v.shape[0] > 512 else v.shape[0]
        parts += [(a, row, count) for row in range(0, v.shape[0], count)]
    anywhere = pl.BlockSpec(memory_space=pl.ANY)
    return pl.pallas_call(
        functools.partial(hand_over_kernel, parts, n),
        out_shape=[jax.ShapeDtypeStruct(v.shape, v.dtype) for v in arrays],
        in_specs=[anywhere] * n,
        out_specs=[anywhere] * n,
        scratch_shapes=[pltpu.VMEM(v.shape, v.dtype) for v in arrays]
        + [pltpu.SemaphoreType.DMA((len(parts),))] * 2,
        compiler_params=pltpu.CompilerParams(vmem_limit_bytes=63 * 2**20),
        name="hand_over",
    )(*arrays)


def layer(mesh, target_input, memory, cotangent, mem_lengths, tgt_lengths, shards, small):
    samples, tgt_len, width = target_input.shape
    mem_len = memory.shape[1]
    far_count = mesh.shape["wide"] // 4
    rows = shards[SQKV].shape[0]
    tokens, keys, hidden = samples * tgt_len, samples * mem_len, 4 * width
    lanes = far_count + 3 + (5 if far_count == 4 else 0)
    count = len(gather_chunks([s.shape for s in shards])[0])
    out_count = len(scatter_chunks(width))
    lead = (far_count, 2, 2, 2)
    total_slots, own_slots = 5 * SCATTER_SKEW + 1, SCATTER_SKEW + 1
    other_slots, land_slots = 2 * SCATTER_SKEW + 1, (4 if far_count == 4 else 3) * SCATTER_SKEW

    def vmem(shape, dtype=BF16):
        return pltpu.VMEM(shape, dtype)

    small_sum = (SMALL_ROWS, 128)
    scratch = [vmem(v.shape, F32) for v in shards] + [
        vmem(small_sum, F32),
        vmem((tokens, width)),
        vmem((keys, width)),
        vmem((tokens, width)),
        vmem((tokens, 3 * width)),
        vmem((tokens, width)),
        vmem((tokens, width), F32),
        vmem((tokens, 1), F32),
        vmem((tokens, width), F32),
        vmem((tokens, width)),
        vmem((tokens, width)),
        vmem((keys, width)),
        vmem((keys, width)),
        vmem((tokens, width)),
        vmem((tokens, width), F32),
        vmem((tokens, 1), F32),
        vmem((tokens, width), F32),
        vmem((tokens, width)),
        vmem((tokens, hidden)),
        vmem((hidden, tokens)),
        vmem((tokens, hidden)),
        vmem((tokens, width), F32),
        vmem((tokens, width)),
        vmem((tokens, width)),
        vmem((tokens, width)),
        vmem((tokens, width)),
        vmem((samples * HEADS // 2, 2 * tgt_len), F32),
        vmem((samples * HEADS // 2, 2 * tgt_len), F32),
        vmem((24, width), F32),
        vmem((24, width), F32),
        vmem((2, 512, width // 2)),
        vmem((4,) + lead + (rows, COLS)),
        vmem((2,) + lead + (4 * rows, 256)),
        vmem(lead + (SMALL_ROWS, 128)),
        vmem((SMALL_ROWS, mesh.size, 128), F32),
        vmem(lead + small_sum, F32),
        vmem((own_slots,) + lead + (rows, COLS)),
        vmem((total_slots, far_count, 2, 2, rows, COLS)),
        vmem((other_slots, 2, far_count, rows, COLS)),
        vmem((land_slots, far_count, rows, COLS)),
        vmem((land_slots, far_count - 1, rows, COLS)),
        vmem((land_slots if far_count == 4 else 1, 3, rows, COLS)),
        vmem((far_count, 2, 2) + small_sum, F32),
        vmem((2, far_count) + small_sum, F32),
        vmem((far_count,) + small_sum, F32),
        vmem((far_count - 1,) + small_sum, F32),
        pltpu.SemaphoreType.DMA((6, 4)),
        pltpu.SemaphoreType.DMA((3,)),
        pltpu.SemaphoreType.DMA((7,)),
        pltpu.SemaphoreType.DMA((count, lanes)),
        pltpu.SemaphoreType.DMA((count, lanes)),
        pltpu.SemaphoreType.DMA((out_count, lanes)),
        pltpu.SemaphoreType.DMA((out_count, lanes)),
        pltpu.SemaphoreType.DMA((2,)),
        pltpu.SemaphoreType.DMA((9,)),
    ]
    in_vmem, anywhere = pl.BlockSpec(memory_space=pltpu.VMEM), pl.BlockSpec(memory_space=pl.ANY)
    in_smem = pl.BlockSpec(memory_space=pltpu.SMEM)
    out_shape = [
        jax.ShapeDtypeStruct((tokens, width), BF16),
        jax.ShapeDtypeStruct((tokens, width), BF16),
        jax.ShapeDtypeStruct((keys, width), BF16),
    ]
    out_shape += [jax.ShapeDtypeStruct(s.shape, F32) for s in shards]
    out_shape += [jax.ShapeDtypeStruct(small_sum, F32)]
    out_shape += [jax.ShapeDtypeStruct(lead + s.shape, BF16) for s in shards]
    outs = pl.pallas_call(
        functools.partial(layer_kernel, (far_count, rows, width, samples, tgt_len, mem_len)),
        out_shape=out_shape,
        in_specs=[anywhere, anywhere, anywhere, in_smem, in_smem] + [in_vmem] * 7,
        out_specs=[anywhere] * 16,
        scratch_shapes=scratch,
        compiler_params=pltpu.CompilerParams(
            collective_id=0, has_side_effects=True, vmem_limit_bytes=63 * 2**20
        ),
        cost_estimate=pl.CostEstimate(flops=52 * 10**9, bytes_accessed=10**8, transcendentals=10**7),
        name="decoder_layer",
    )(
        target_input.reshape(tokens, width),
        memory.reshape(keys, width),
        cotangent.reshape(tokens, width),
        mem_lengths,
        tgt_lengths,
        *shards,
        small,
    )
    return (*hand_over(outs[:9]), outs[9])


def step(
    mesh,
    target_input,
    memory,
    cotangent,
    mem_lengths,
    tgt_lengths,
    self_qkv,
    self_out,
    self_bias,
    norm1_gain,
    norm1_shift,
    cross_qkv,
    cross_out,
    cross_bias,
    norm2_gain,
    norm2_shift,
    ffn_up,
    up_bias,
    ffn_down,
    down_bias,
    norm3_gain,
    norm3_shift,
):
    per, up_per = norm1_gain.shape[0], up_bias.shape[0]
    small = jnp.zeros((SMALL_ROWS, 128), BF16)
    row = 0
    for v in (
        self_bias, norm1_gain, norm1_shift, cross_bias, norm2_gain, norm2_shift,
        down_bias, norm3_gain, norm3_shift, up_bias,
    ):
        v = v.reshape(-1, v.shape[-1])
        small += jnp.pad(v, ((row, SMALL_ROWS - row - v.shape[0]), (0, 128 - v.shape[1])))
        row += v.shape[0]
    block_out, target_grad, memory_grad, *grads, sums = layer(
        mesh, target_input, memory, cotangent, mem_lengths, tgt_lengths,
        [self_qkv, self_out, cross_qkv, cross_out, ffn_up, ffn_down], small,
    )
    return (
        block_out.reshape(target_input.shape),
        target_grad.reshape(target_input.shape),
        memory_grad.reshape(memory.shape),
        grads[SQKV],
        grads[SOUT],
        sums[SELF_Q : SELF_Q + 3, :per],
        sums[GAIN1, :per],
        sums[SHIFT1, :per],
        grads[CQKV],
        grads[COUT],
        sums[CROSS_Q : CROSS_Q + 3, :per],
        sums[GAIN2, :per],
        sums[SHIFT2, :per],
        grads[FUP],
        sums[VECTORS, :up_per],
        grads[FDOWN],
        sums[DOWN, :per],
        sums[GAIN3, :per],
        sums[SHIFT3, :per],
    )


def solution(mesh):
    both = ("wide", "narrow")
    stream, matrix_spec, vector_spec, bias_spec = P(both, None, None), P(both, None), P(both), P(None, both)
    weights = (
        matrix_spec, matrix_spec, bias_spec, vector_spec, vector_spec,
        matrix_spec, matrix_spec, bias_spec, vector_spec, vector_spec,
        matrix_spec, vector_spec, matrix_spec, vector_spec, vector_spec, vector_spec,
    )
    return jax.shard_map(
        functools.partial(step, mesh),
        mesh=mesh,
        in_specs=(stream, stream, stream, vector_spec, vector_spec) + weights,
        out_specs=(stream, stream, stream) + weights,
        check_vma=False,
    )
```
